128 devices in a mesh: pipe: 2 (over z_hi), dp: 16 (over z_lo, y, core), tensor: 4 (over x).
Axes of the slice: x: 4, y: 4, z: 4 (z_hi: 2, z_lo: 2; z = z_hi * 2 + z_lo), core: 2. Of those that a mesh axis runs over, the one named last changes fastest.
Arguments:
- inputs: bfloat16 [2, 4096, 1024], P(None, ('dp', 'tensor')), may hold values from -6 to 6
- cotangent: bfloat16 [2, 4096, 1024], P(None, ('dp', 'tensor')), may hold values from -16 to 16
- doc_lengths: int32 [2, 16, 4], P(None, 'dp'), may hold values from 1 to 256, as said below
- routes: int32 [2, 2, 4096, 8], P('pipe', None, 'dp'), may hold values from 0 to 15, all different within a row; in each aligned block of 256 rows (0 to 255, 256 to 511, ..., all dimensions but the last counted through in order) at most 160 rows name the same one
- norm_attn: bfloat16 [2, 1024], P('pipe', ('dp', 'tensor')), may hold values from 0.5 to 1.5
- w_query: bfloat16 [2, 1024, 1024], P('pipe', 'dp', 'tensor'), may hold values from -0.1875 to 0.1875
- w_key: bfloat16 [2, 1024, 512], P('pipe', 'dp', 'tensor'), may hold values from -0.1875 to 0.1875
- w_value: bfloat16 [2, 1024, 512], P('pipe', 'dp', 'tensor'), may hold values from -0.1875 to 0.1875
- w_out: bfloat16 [2, 1024, 1024], P('pipe', 'tensor', 'dp'), may hold values from -0.75 to 0.75
- w_router: bfloat16 [2, 1024, 16], P('pipe', ('dp', 'tensor')), may hold values from -0.09375 to 0.09375
- norm_ffn: bfloat16 [2, 1024], P('pipe', ('dp', 'tensor')), may hold values from 0.5 to 1.5
- w_gate: bfloat16 [2, 16, 1024, 512], P('pipe', None, 'dp', 'tensor'), may hold values from -0.1875 to 0.1875
- w_up: bfloat16 [2, 16, 1024, 512], P('pipe', None, 'dp', 'tensor'), may hold values from -0.1875 to 0.1875
- w_down: bfloat16 [2, 16, 512, 1024], P('pipe', None, 'tensor', 'dp'), may hold values from -0.75 to 0.75
Outputs:
- section_out: bfloat16 [2, 2, 4096, 1024], P('pipe', None, ('dp', 'tensor'))
- input_grad: float32 [2, 2, 4096, 1024], P('pipe', None, ('dp', 'tensor'))
- grad_norm_attn: float32 [2, 1024], P('pipe', ('dp', 'tensor'))
- grad_query: float32 [2, 1024, 1024], P('pipe', 'dp', 'tensor')
- grad_key: float32 [2, 1024, 512], P('pipe', 'dp', 'tensor')
- grad_value: float32 [2, 1024, 512], P('pipe', 'dp', 'tensor')
- grad_out: float32 [2, 1024, 1024], P('pipe', 'tensor', 'dp')
- grad_router: float32 [2, 1024, 16], P('pipe', ('dp', 'tensor'))
- grad_norm_ffn: float32 [2, 1024], P('pipe', ('dp', 'tensor'))
- grad_gate: float32 [2, 16, 1024, 512], P('pipe', None, 'dp', 'tensor')
- grad_up: float32 [2, 16, 1024, 512], P('pipe', None, 'dp', 'tensor')
- grad_down: float32 [2, 16, 512, 1024], P('pipe', None, 'tensor', 'dp')
The draws below stay inside these ranges and needn't reach their ends.
Inputs may be any that keep to these rules, and one draw needn't show every extreme that they name: `doc_lengths`: each row holds 4 lengths that sum to 256; one of these documents, at a place drawn from the seed, holds tokens of every index of tensor. `routes`: in each block of 256 consecutive rows (one section, one micro-batch, one pack) no expert is named more than 160 times, and in some blocks one expert is named exactly 160 times.
All inputs are finite; a program needn't handle non-finite values.
Results may differ from the reference program's by a relative error of at most 0.035.
Values may be sent and summed in bfloat16 or wider, within the bound.
No kernel may reach another device: no remote copies, remote signals or barrier semaphores. Data moves between devices by JAX's collectives and lax.ppermute only.
A program may use at most 192 MiB of HBM per device.

```python
import math
import jax
import jax.numpy as jnp
import numpy as np
from jax import lax

D = 1024
HQ = 16
KV = 8
HD = 64
E = 16
TOP = 8
FF = 512
TOK_DEV = 64
MB = 2
NDOC = 4
GT = 256
TOKENS = 4096
CAP = 160
N_DP = 16


def draw_doc_lengths(key, part):
    key = jax.random.fold_in(key, 7)
    short_key, place_key = jax.random.split(key)
    pack_count = TOKENS // GT
    short_docs = jax.random.randint(short_key, (MB, pack_count, NDOC), 1, TOK_DEV // NDOC + 1)
    long_place = jax.random.randint(place_key, (MB, pack_count, 1), 0, NDOC)
    doc_index = jnp.arange(NDOC, dtype=jnp.int32)[None, None, :]
    is_long = doc_index == long_place
    short_docs = jnp.where(is_long, 0, short_docs)
    long_doc = GT - jnp.sum(short_docs, axis=-1, keepdims=True)
    return jnp.where(is_long, long_doc, short_docs).astype(jnp.int32)


def spiked(entries, rng, source, target, shards_of, factor):
    def block_of(dim):
        return (jnp.arange(entries.shape[dim]) // (entries.shape[dim] // shards_of)).reshape((-1,) + (1,) * (entries.ndim - 1 - dim))

    near = jax.random.permutation(rng, shards_of)[block_of(target)]
    second = (block_of(target) + shards_of // 2) % shards_of
    return jnp.where((block_of(source) == near) | (block_of(source) == second), factor * entries, entries)


def shard_levels(rng, shape, pieces, low, top_value):
    factor_of, own = 1.0, jax.random.fold_in(rng, 6)
    for dim, blocks in pieces:
        heights = jnp.exp(jax.random.uniform(jax.random.fold_in(own, dim), (blocks,), jnp.float32, low / len(pieces), top_value / len(pieces)))
        factor_of = factor_of * jnp.repeat(heights, shape[dim] // blocks).reshape([-1 if axis == dim else 1 for axis in range(len(shape))])
    return factor_of


def deal_out(rng, own, number, rows, amount, top, most, skew):
    order = jax.random.permutation(rng, amount)
    crowded, ordinary = portions_of(amount, rows * top, most, skew, True), portions_of(amount, rows * top, most, skew, False)
    places = jnp.arange(amount)

    def named(sizes, rotation):
        used = int((sizes > 0).sum())
        fixed = max(1, used // 4)
        moved = fixed + (places - fixed + rotation * (used - fixed)) % max(1, amount - fixed)
        return jnp.zeros((amount,), jnp.int32).at[order[jnp.where(places < fixed, places, moved)]].set(jnp.asarray(sizes, jnp.int32))

    sizes = jnp.where(number % 4 == 0, named(crowded, number // 4), named(ordinary, number - number // 4 - 1))
    mixed = jax.random.permutation(jax.random.fold_in(own, 3), amount)
    giver, taker = mixed[0:amount // 2 * 2:2], mixed[1:amount // 2 * 2:2]
    room = jnp.minimum(sizes[giver] - 1, most - sizes[taker]) // 2
    room = jnp.where((giver == order[0]) | (taker == order[0]) | (sizes[taker] == 0), 0, jnp.maximum(room, 0))
    moved = jax.random.randint(jax.random.fold_in(own, 4), (amount // 2,), 0, 1 << 20) % (room + 1)
    sizes = sizes.at[giver].add(-moved).at[taker].add(moved)
    members = jnp.searchsorted(jnp.cumsum(sizes), jnp.arange(rows * top), side="right").astype(jnp.int32)
    listing = members.reshape(top, rows).T
    listing = listing[jax.random.permutation(jax.random.fold_in(own, 1), rows)]
    rotation = jax.random.randint(jax.random.fold_in(own, 2), (rows, 1), 0, top)
    return jnp.take_along_axis(listing, (jnp.arange(top)[None, :] + rotation) % top, axis=1)


def portions_of(count, total, reach, lean, full):
    portions = [(1 << 20) // math.isqrt(standing ** lean) + 1 for standing in range(1, count + 1)]
    largest = reach if full else min(reach, max(-(-total // count), total * portions[0] // sum(portions)))
    least = 1 if total - largest >= count - 1 else 0
    counts, spare = [largest] + [least] * (count - 1), total - largest - least * (count - 1)
    while spare > 0:
        movable = [i for i in range(1, count) if counts[i] < largest] or [i for i in range(1, count) if counts[i] < reach]
        whole, remaining = sum([portions[i] for i in movable]), spare
        for i in movable:
            more = min(reach - counts[i], max(1, remaining * portions[i] // whole), spare)
            counts[i] = counts[i] + more
            spare = spare - more
    return np.array(counts)


def normal_values(stream_key, extent, width, reach, cuts=(), kind=jnp.bfloat16):
    entries = width * jax.random.normal(stream_key, extent, jnp.float32)
    if cuts:
        entries = entries * shard_levels(stream_key, extent, cuts, -0.22, 0.18)
    return jnp.clip(entries, -reach, reach).astype(kind)


def noise_with(key, dims, width, reach, pieces, heavy, kind=jnp.bfloat16):
    values = width * jax.random.normal(key, dims, jnp.float32)
    if pieces:
        values = values * shard_levels(key, dims, pieces, -0.22, 0.18)
    return jnp.clip(spiked(values, jax.random.fold_in(key, 3), *heavy), -reach, reach).astype(kind)


def setup_inputs(seed: int = 0) -> dict:
    arg_keys = jax.random.split(jax.random.key(seed), 15)
    inputs = normal_values(arg_keys[0], (MB, TOKENS, D), 1.0, 6.0, ((1, 64),))
    cotangent = noise_with(arg_keys[1], (MB, TOKENS, D), 1.0, 16.0, ((1, 64),), (1, 2, 64, 4.0))
    doc_lengths = draw_doc_lengths(jax.random.fold_in(arg_keys[14], 71), 0)
    routes_keys = jax.random.split(jax.random.fold_in(arg_keys[3], 1), 2 * MB * TOKENS // GT)
    routes_turns = jax.random.permutation(jax.random.fold_in(arg_keys[3], 3), 2 * MB * TOKENS // GT)
    routes = jax.vmap(lambda own, number: deal_out(jax.random.fold_in(arg_keys[3], 2), own, number, GT, E, TOP, CAP, 1))(routes_keys, routes_turns).reshape((2, MB, TOKENS, TOP))
    norm_attn = jnp.clip(1.0 + 0.1 * jax.random.normal(arg_keys[4], (2, D), jnp.float32), 0.5, 1.5).astype(jnp.bfloat16)
    w_query = normal_values(arg_keys[5], (2, D, HQ * HD), D ** -0.5, 0.1875, ((0, 2), (1, 16), (2, 4)))
    w_key = normal_values(arg_keys[6], (2, D, KV * HD), D ** -0.5, 0.1875, ((0, 2), (1, 16), (2, 4)))
    w_value = normal_values(arg_keys[7], (2, D, KV * HD), D ** -0.5, 0.1875, ((0, 2), (1, 16), (2, 4)))
    w_out = normal_values(arg_keys[8], (2, HQ * HD, D), (HQ * HD // 16) ** -0.5, 0.75, ((0, 2), (1, 4), (2, 16)))
    w_router = normal_values(arg_keys[9], (2, D, E), (4 * D) ** -0.5, 0.09375, ((0, 2), (1, 64)))
    norm_ffn = jnp.clip(1.0 + 0.1 * jax.random.normal(arg_keys[10], (2, D), jnp.float32), 0.5, 1.5).astype(jnp.bfloat16)
    w_gate = normal_values(arg_keys[11], (2, E, D, FF), D ** -0.5, 0.1875, ((0, 2), (2, 16), (3, 4)))
    w_up = normal_values(arg_keys[12], (2, E, D, FF), D ** -0.5, 0.1875, ((0, 2), (2, 16), (3, 4)))
    w_down = normal_values(arg_keys[13], (2, E, FF, D), (FF // 8) ** -0.5, 0.75, ((0, 2), (2, 4), (3, 16)))
    return dict(inputs=inputs, cotangent=cotangent, doc_lengths=doc_lengths, routes=routes, norm_attn=norm_attn, w_query=w_query, w_key=w_key, w_value=w_value, w_out=w_out, w_router=w_router, norm_ffn=norm_ffn, w_gate=w_gate, w_up=w_up, w_down=w_down)


EPSILON = 1e-06
MASKED = -1000000000.0
HIGHEST = lax.Precision.HIGHEST

@jax.custom_vjp
def low(v):
    return lax.optimization_barrier(v.astype(jnp.bfloat16)).astype(jnp.float32)

@jax.custom_vjp
def low_back(v):
    return v

def low_keep(v):
    return (low(v), None)

def low_pass(kept, grad):
    return (grad,)

def back_keep(v):
    return (v, None)

def back_low(kept, grad):
    return (low(grad),)
low.defvjp(low_keep, low_pass)
low_back.defvjp(back_keep, back_low)

def rope_tables(position, head_width):
    half_width = head_width // 2
    freq_table = jnp.exp(jnp.arange(half_width, dtype=jnp.float32) * (-2.0 * math.log(10000.0) / head_width))
    angle_table = position.astype(jnp.float32)[:, None] * freq_table[None, :]
    return (jnp.cos(angle_table), jnp.sin(angle_table))

def rotate(values, cosine_table, sine_table):
    half_width = values.shape[-1] // 2
    first_half = values[..., :half_width]
    second_half = values[..., half_width:]
    cosine_rows = cosine_table[:, None, :]
    sine_rows = sine_table[:, None, :]
    return jnp.concatenate([first_half * cosine_rows - second_half * sine_rows, second_half * cosine_rows + first_half * sine_rows], axis=-1)

def doc_layout(lengths, row_count):
    doc_ends = jnp.cumsum(lengths).astype(jnp.int32)
    doc_starts = (doc_ends - lengths).astype(jnp.int32)
    row_index = jnp.arange(row_count, dtype=jnp.int32)
    inside = row_index[:, None] >= doc_starts[None, :]
    segment = lax.optimization_barrier(jnp.sum(inside.astype(jnp.int32), axis=1)).astype(jnp.int32)
    position = (row_index - lax.optimization_barrier(jnp.max(jnp.where(inside, doc_starts[None, :], 0), axis=1))).astype(jnp.int32)
    return (segment, position)

def slot_tables(chosen_ids, capacity):
    flat_ids = chosen_ids.reshape(-1).astype(jnp.int32)
    expert_ids = jnp.arange(E, dtype=jnp.int32)
    onehot = (flat_ids[:, None] == expert_ids[None, :]).astype(jnp.int32)
    running = jnp.cumsum(onehot, axis=0).astype(jnp.int32)
    rank_in = (lax.optimization_barrier(jnp.sum(running * onehot, axis=1)).astype(jnp.int32) - 1).astype(jnp.int32)
    slot_of = (flat_ids * capacity + rank_in).astype(jnp.int32)
    token_of = (jnp.arange(flat_ids.shape[0], dtype=jnp.int32) // chosen_ids.shape[1]).astype(jnp.int32)
    source = jnp.full((E * capacity,), chosen_ids.shape[0], jnp.int32).at[slot_of].set(token_of)
    return (slot_of, source)

def rms_norm(values, gain):
    return values * lax.rsqrt(lax.optimization_barrier(jnp.mean(values * values, axis=-1, keepdims=True)) + EPSILON) * gain

def layer_apply(entering, weights, chosen_ids, segment, position):
    gain_attn, weight_query, weight_key, weight_value, weight_out, weight_router, gain_ffn, weight_gate, weight_up, weight_down = weights
    group_rows = entering.shape[0]
    normed_attn = low(rms_norm(entering, gain_attn))
    cosine_table, sine_table = rope_tables(position, HD)
    query_lin = low_back(jnp.dot(normed_attn, weight_query, precision=HIGHEST)).reshape(group_rows, HQ, HD)
    key_lin = low_back(jnp.dot(normed_attn, weight_key, precision=HIGHEST)).reshape(group_rows, KV, HD)
    query_rows = low(rotate(query_lin, cosine_table, sine_table))
    key_rows = low(rotate(key_lin, cosine_table, sine_table))
    value_rows = low(low_back(jnp.dot(normed_attn, weight_value, precision=HIGHEST))).reshape(group_rows, KV, HD)
    query_grouped = query_rows.reshape(group_rows, KV, HQ // KV, HD)
    row_index = jnp.arange(group_rows, dtype=jnp.int32)
    visible = (segment[:, None] == segment[None, :]) & (row_index[None, :] <= row_index[:, None])
    raw_scores = jnp.einsum('tkgd,skd->kgts', query_grouped, key_rows, precision=HIGHEST) * HD ** (-0.5)
    scores = low_back(jnp.where(visible[None, None], raw_scores, MASKED))
    soft_low = low(jax.nn.softmax(scores, axis=-1))
    mixed = jnp.einsum('kgts,skd->tkgd', soft_low, value_rows, precision=HIGHEST).reshape(group_rows, HQ * HD)
    mixed = low_back(low(mixed))
    hidden = entering + low_back(jnp.dot(mixed, weight_out, precision=HIGHEST))
    normed_ffn = low(rms_norm(hidden, gain_ffn))
    logits = low_back(jnp.dot(normed_ffn, weight_router, precision=HIGHEST))
    gate_values = jax.nn.softmax(jnp.take_along_axis(logits, chosen_ids, axis=1), axis=-1)
    slot_of, source = slot_tables(chosen_ids, CAP)
    padded = jnp.concatenate([normed_ffn, jnp.zeros((1, D), jnp.float32)], axis=0)
    expert_in = padded[source].reshape(E, CAP, D)
    gate_pre = low_back(jnp.einsum('ecd,edf->ecf', expert_in, weight_gate, precision=HIGHEST))
    up_pre = low_back(jnp.einsum('ecd,edf->ecf', expert_in, weight_up, precision=HIGHEST))
    activated = low(jax.nn.silu(gate_pre) * up_pre)
    expert_out = low_back(jnp.einsum('ecf,efd->ecd', activated, weight_down, precision=HIGHEST))
    per_token = expert_out.reshape(E * CAP, D)[slot_of].reshape(group_rows, TOP, D)
    routed = low_back(lax.optimization_barrier(jnp.sum(gate_values[:, :, None] * per_token, axis=1)))
    return hidden + routed

def reference(inputs, cotangent, doc_lengths, routes, norm_attn, w_query, w_key, w_value, w_out, w_router, norm_ffn, w_gate, w_up, w_down):
    instances = MB * N_DP
    x_groups = inputs.astype(jnp.float32).reshape(instances, GT, D)
    probe = jnp.zeros_like(x_groups)
    ids_first = routes[0].reshape(instances, GT, TOP)
    ids_second = routes[1].reshape(instances, GT, TOP)
    lengths_all = doc_lengths.reshape(instances, NDOC)
    stacked = (norm_attn, w_query, w_key, w_value, w_out, w_router, norm_ffn, w_gate, w_up, w_down)
    weights_first = tuple((member[0].astype(jnp.float32) for member in stacked))
    weights_second = tuple((member[1].astype(jnp.float32) for member in stacked))

    def chain(x_all, probe_all, first_weights, second_weights):

        def per_pack(pack_item):
            x_one, probe_one, ids_a, ids_b, length_one = pack_item
            segment, position = doc_layout(length_one, GT)
            y_first = layer_apply(x_one, first_weights, ids_a, segment, position)
            entering = low_back(low(y_first)) + probe_one
            return (y_first, layer_apply(entering, second_weights, ids_b, segment, position))
        return lax.map(jax.checkpoint(per_pack), (x_all, probe_all, ids_first, ids_second, lengths_all))
    (y_first, y_second), backward = jax.vjp(chain, x_groups, probe, weights_first, weights_second)
    cot_groups = cotangent.astype(jnp.float32).reshape(instances, GT, D)
    grad_x, grad_probe, grad_first, grad_second = backward((jnp.zeros_like(y_first), cot_groups))
    section_out = jnp.stack([y_first, y_second]).reshape(2, MB, TOKENS, D).astype(jnp.bfloat16)
    input_grad = jnp.stack([grad_x, grad_probe]).reshape(2, MB, TOKENS, D)
    grads = [jnp.stack([left_grad, right_grad]) for left_grad, right_grad in zip(grad_first, grad_second)]
    return (section_out, input_grad, grads[0], grads[1], grads[2], grads[3], grads[4], grads[5], grads[6], grads[7], grads[8], grads[9])
```

```python
import math

import jax
import jax.numpy as jnp
from jax import lax
from jax.experimental import pallas as pl
from jax.experimental.pallas import tpu as pltpu
from jax.sharding import PartitionSpec as P

HD = 64
E = 16
TOP = 8
EPSILON = 1e-06
MASKED = -1000000000.0
BF = jnp.bfloat16
F32 = jnp.float32
VMEM_LIMIT = 56 * 1024 * 1024
PER = 2
LANES = 128


def params():
    return pltpu.CompilerParams(
        vmem_limit_bytes=VMEM_LIMIT, dimension_semantics=("arbitrary",)
    )


def dot(left, right):
    return jnp.dot(left, right, preferred_element_type=F32)


def dot_nt(left, right):
    return lax.dot_general(
        left, right, (((1,), (1,)), ((), ())), preferred_element_type=F32
    )


def dot_tn(left, right):
    return lax.dot_general(
        left, right, (((0,), (0,)), ((), ())), preferred_element_type=F32
    )


def column(rows, index):
    lanes = lax.broadcasted_iota(jnp.int32, rows.shape, 1)
    return jnp.sum(jnp.where(lanes == index, rows, 0.0), axis=1, keepdims=True)


def whole(shape):
    return pl.BlockSpec(shape, lambda i, s: (0,) * len(shape))


def rms_scale(values):
    return lax.rsqrt(jnp.mean(values * values, axis=-1, keepdims=True) + EPSILON)


def norm_back(values, scale_rows, gain, grad_normed):
    weighted = grad_normed * gain
    grad_values = scale_rows * weighted - values * scale_rows**3 * jnp.mean(
        weighted * values, axis=-1, keepdims=True
    )
    grad_gain = jnp.sum(grad_normed * values * scale_rows, axis=0, keepdims=True)
    return grad_values, grad_gain


def swap_halves(values):
    width = values.shape[1]
    lanes = lax.broadcasted_iota(jnp.int32, values.shape, 1)
    ahead = pltpu.roll(values, width - HD // 2, 1)
    behind = pltpu.roll(values, HD // 2, 1)
    return jnp.where(lanes % HD < HD // 2, ahead, behind)


def assemble(me, pieces, peers, target, extra=None):
    rows = pieces[0].shape[0]
    for shift in range(peers):
        owner = lax.rem(me + peers - shift, peers)
        place = pl.ds(pl.multiple_of(owner * rows, rows), rows)
        block = pieces[shift][...]
        if extra is not None:
            block = block + extra[place, :]
        target[place, :] = block


def own_rows(me, rows):
    return pl.ds(pl.multiple_of(me * rows, rows), rows)


def attention_forward_kernel(n_pieces, has_full, *refs):
    (sref, *refs) = refs
    pieces, refs = refs[:n_pieces], refs[n_pieces:]
    full_ref = None
    if has_full:
        full_ref, refs = refs[0], refs[1:]
    (
        gains_ref,
        cos_ref,
        sin_ref,
        bias_ref,
        picked_ref,
        w_ref,
        router_ref,
        a_ref,
        xown_ref,
        qkv_ref,
        o_ref,
        lse_ref,
        hown_ref,
        b_ref,
        gates_ref,
        hidden,
        rows_in,
    ) = refs
    step = pl.program_id(0)
    me = sref[0]
    group, width = b_ref.shape
    shard = xown_ref.shape[0]

    @pl.when(step == 0)
    def _():
        if n_pieces:
            assemble(me, pieces, n_pieces, rows_in, full_ref)
        else:
            rows_in[...] = full_ref[...]
        entering = rows_in[...].astype(F32)
        a_ref[...] = (entering * rms_scale(entering) * gains_ref[0:1, :]).astype(BF)
        xown_ref[...] = rows_in[own_rows(me, shard), :]
        hidden[...] = entering

    weights = w_ref[:, 0].reshape(width, -1)
    qkv = dot(a_ref[...], weights[:, :512])
    qk = qkv[:, :384]
    cos = jnp.concatenate([cos_ref[0]] * 3, axis=1)
    sin = jnp.concatenate([sin_ref[0]] * 3, axis=1)
    turned = qk * cos + swap_halves(qk) * sin
    q = (turned[:, :256] * HD**-0.5).astype(BF)
    k = turned[:, 256:].astype(BF)
    v = qkv[:, 384:].astype(BF)
    qkv_ref[0, :, :256] = q
    qkv_ref[0, :, 256:384] = k
    qkv_ref[0, :, 384:] = v
    bias = bias_ref[0]
    lanes = lax.broadcasted_iota(jnp.int32, (group, LANES), 1)
    lse_all = jnp.zeros((group, LANES), F32)
    outs = []
    for head in range(4):
        kv = head // 2
        scores = dot_nt(q[:, head * HD : (head + 1) * HD], k[:, kv * HD : (kv + 1) * HD])
        scores = scores + bias
        peak = jnp.max(scores, axis=1, keepdims=True)
        soft = jnp.exp(scores - peak)
        total = jnp.sum(soft, axis=1, keepdims=True)
        lse_all = jnp.where(lanes == head, peak + jnp.log(total), lse_all)
        soft = (soft * (1.0 / total)).astype(BF)
        outs.append(dot(soft, v[:, kv * HD : (kv + 1) * HD]))
    mixed = jnp.concatenate(outs, axis=1).astype(BF)
    o_ref[0] = mixed
    lse_ref[0] = lse_all
    hidden[...] += dot_nt(mixed, weights[:, 512:])

    @pl.when(step == pl.num_programs(0) - 1)
    def _():
        rows = hidden[...]
        normed = (rows * rms_scale(rows) * gains_ref[1:2, :]).astype(BF)
        b_ref[...] = normed
        hown_ref[...] = hidden[own_rows(me, shard), :]
        logits = dot(normed, router_ref[...])
        picked = picked_ref[0]
        peak = jnp.max(jnp.where(picked > 0, logits, -1e30), axis=1, keepdims=True)
        powers = jnp.where(picked > 0, jnp.exp(jnp.minimum(logits - peak, 0.0)), 0.0)
        gates_ref[...] = powers / jnp.sum(powers, axis=1, keepdims=True)


def attention_forward(scalars, pieces, full, gains, tables, picked, w_attn, router):
    dp, peers, dr, cols = w_attn.shape
    width = dp * dr
    group = tables[0].shape[1]
    shard = group // peers
    cos, sin, bias = tables
    pick = lambda i, s: (s[1], 0, 0)
    operands = [*pieces] + ([full] if full is not None else [])
    in_specs = [whole(x.shape) for x in operands] + [
        whole(gains.shape),
        pl.BlockSpec((1,) + cos.shape[1:], pick),
        pl.BlockSpec((1,) + sin.shape[1:], pick),
        pl.BlockSpec((1,) + bias.shape[1:], pick),
        pl.BlockSpec((1,) + picked.shape[1:], pick),
        pl.BlockSpec((dp, 1, dr, cols), lambda i, s: (0, i, 0, 0)),
        whole(router.shape),
    ]
    per_step = lambda i, s: (i, 0, 0)
    out_shape = [
        jax.ShapeDtypeStruct((group, width), BF),
        jax.ShapeDtypeStruct((shard, width), BF),
        jax.ShapeDtypeStruct((peers, group, 512), BF),
        jax.ShapeDtypeStruct((peers, group, 256), BF),
        jax.ShapeDtypeStruct((peers, group, LANES), F32),
        jax.ShapeDtypeStruct((shard, width), F32),
        jax.ShapeDtypeStruct((group, width), BF),
        jax.ShapeDtypeStruct((group, E), F32),
    ]
    out_specs = [
        whole((group, width)),
        whole((shard, width)),
        pl.BlockSpec((1, group, 512), per_step),
        pl.BlockSpec((1, group, 256), per_step),
        pl.BlockSpec((1, group, LANES), per_step),
        whole((shard, width)),
        whole((group, width)),
        whole((group, E)),
    ]
    return pl.pallas_call(
        lambda *refs: attention_forward_kernel(len(pieces), full is not None, *refs),
        grid_spec=pltpu.PrefetchScalarGridSpec(
            num_scalar_prefetch=1,
            grid=(peers,),
            in_specs=in_specs,
            out_specs=out_specs,
            scratch_shapes=[pltpu.VMEM((group, width), F32), pltpu.VMEM((group, width), BF)],
        ),
        out_shape=out_shape,
        compiler_params=params(),
        cost_estimate=pl.CostEstimate(
            flops=2 * group * width * cols * peers + 16 * 4 * group * group * HD,
            bytes_accessed=w_attn.size * 2 + 6 * group * width * 2,
            transcendentals=16 * group * group,
        ),
        name="attention_forward",
    )(scalars, *operands, gains, cos, sin, bias, picked, w_attn, router)


def experts_forward_kernel(peers, sref, b_ref, gate_ref, w_ref, *refs):
    pieces, (gu_ref, total) = refs[:peers], refs[peers:]
    step = pl.program_id(0)
    width = b_ref.shape[1]
    ff = w_ref.shape[-1]
    b = b_ref[...]
    gates = gate_ref[...]
    acts, downs = [], []
    for j in range(PER):
        gate_up = jnp.concatenate(
            [w_ref[:, 0, j].reshape(width, ff), w_ref[:, 1, j].reshape(width, ff)], axis=1
        )
        both = dot(b, gate_up)
        gu_ref[j] = both.astype(BF)
        gate_pre, up_pre = both[:, :ff], both[:, ff:]
        act = gate_pre * jax.nn.sigmoid(gate_pre) * up_pre
        acts.append((act * column(gates, step * PER + j)).astype(BF))
        downs.append(w_ref[:, 2, j].reshape(width, ff))
    out = dot_nt(jnp.concatenate(acts, axis=1), jnp.concatenate(downs, axis=1))

    @pl.when(step == 0)
    def _():
        total[...] = out

    @pl.when(step > 0)
    def _():
        total[...] += out

    @pl.when(step == pl.num_programs(0) - 1)
    def _():
        rows = b_ref.shape[0] // peers
        for shift in range(peers):
            place = own_rows(lax.rem(sref[0] + shift, peers), rows)
            pieces[shift][...] = total[place, :].astype(BF)


def experts_forward(scalars, b, gates, w, peers):
    group, width = b.shape
    dp, _, experts, dr, ff = w.shape
    piece = (group // peers, width)
    return pl.pallas_call(
        lambda *refs: experts_forward_kernel(peers, *refs),
        grid_spec=pltpu.PrefetchScalarGridSpec(
            num_scalar_prefetch=1,
            grid=(experts // PER,),
            in_specs=[
                whole((group, width)),
                whole((group, experts)),
                pl.BlockSpec((dp, 3, PER, dr, ff), lambda i, s: (0, 0, i, 0, 0)),
            ],
            out_specs=[whole(piece)] * peers
            + [pl.BlockSpec((PER, group, 2 * ff), lambda i, s: (i, 0, 0))],
            scratch_shapes=[pltpu.VMEM((group, width), F32)],
        ),
        out_shape=[jax.ShapeDtypeStruct(piece, BF)] * peers
        + [jax.ShapeDtypeStruct((experts, group, 2 * ff), BF)],
        compiler_params=params(),
        cost_estimate=pl.CostEstimate(
            flops=2 * group * width * ff * 3 * experts,
            bytes_accessed=w.size * 2 + experts * group * 2 * ff * 2,
            transcendentals=experts * group * ff,
        ),
        name="experts_forward",
    )(scalars, b, gates, w)


def experts_backward_kernel(peers, n_pieces, has_full, *refs):
    (sref, *refs) = refs
    given, refs = refs[:n_pieces], refs[n_pieces:]
    full_ref = None
    if has_full:
        full_ref, refs = refs[0], refs[1:]
    gate_ref, gu_ref, w_ref, *refs = refs
    pieces, refs = refs[:peers], refs[peers:]
    grad_ref, dgu_ref, ga_ref, total, total_gate = refs
    step = pl.program_id(0)
    group, width = grad_ref.shape
    ff = w_ref.shape[-1]

    @pl.when(step == 0)
    def _():
        if n_pieces:
            assemble(sref[0], given, n_pieces, grad_ref, full_ref)
        else:
            grad_ref[...] = full_ref[...]

    grad = grad_ref[...]
    gates = gate_ref[...]
    down = jnp.concatenate([w_ref[:, 2, j].reshape(width, ff) for j in range(PER)], axis=1)
    turned = dot(grad, down)
    lanes = lax.broadcasted_iota(jnp.int32, (group, LANES), 1)
    grad_gate = jnp.zeros((group, LANES), F32)
    out = None
    for j in range(PER):
        expert = step * PER + j
        back = turned[:, j * ff : (j + 1) * ff]
        both = gu_ref[j].astype(F32)
        gate_pre, up_pre = both[:, :ff], both[:, ff:]
        sigma = jax.nn.sigmoid(gate_pre)
        silu = gate_pre * sigma
        act = silu * up_pre
        gate = column(gates, expert)
        grad_gate = jnp.where(
            lanes == expert, jnp.sum(act * back, axis=1, keepdims=True), grad_gate
        )
        grad_act = gate * back
        grad_pre = (grad_act * up_pre * sigma * (1.0 + gate_pre * (1.0 - sigma))).astype(BF)
        grad_up = (grad_act * silu).astype(BF)
        grad_both = jnp.concatenate([grad_pre, grad_up], axis=1)
        dgu_ref[j] = grad_both
        ga_ref[:, j * ff : (j + 1) * ff] = (gate * act).astype(BF)
        gate_up = jnp.concatenate(
            [w_ref[:, 0, j].reshape(width, ff), w_ref[:, 1, j].reshape(width, ff)], axis=1
        )
        part = dot_nt(grad_both, gate_up)
        out = part if out is None else out + part

    @pl.when(step == 0)
    def _():
        total[...] = out
        total_gate[...] = grad_gate

    @pl.when(step > 0)
    def _():
        total[...] += out
        total_gate[...] += grad_gate

    @pl.when(step == pl.num_programs(0) - 1)
    def _():
        rows = group // peers
        for shift in range(peers):
            place = own_rows(lax.rem(sref[0] + shift, peers), rows)
            pieces[shift][:, :width] = total[place, :].astype(BF)
            pieces[shift][:, width:] = total_gate[place, :].astype(BF)


def experts_backward(scalars, given, full, gates, gu, w, peers):
    dp, _, experts, dr, ff = w.shape
    group = gates.shape[0]
    width = dp * dr
    piece = (group // peers, width + LANES)
    operands = [*given] + ([full] if full is not None else [])
    return pl.pallas_call(
        lambda *refs: experts_backward_kernel(peers, len(given), full is not None, *refs),
        grid_spec=pltpu.PrefetchScalarGridSpec(
            num_scalar_prefetch=1,
            grid=(experts // PER,),
            in_specs=[whole(x.shape) for x in operands]
            + [
                whole((group, experts)),
                pl.BlockSpec((PER, group, 2 * ff), lambda i, s: (i, 0, 0)),
                pl.BlockSpec((dp, 3, PER, dr, ff), lambda i, s: (0, 0, i, 0, 0)),
            ],
            out_specs=[whole(piece)] * peers
            + [
                whole((group, width)),
                pl.BlockSpec((PER, group, 2 * ff), lambda i, s: (i, 0, 0)),
                pl.BlockSpec((group, PER * ff), lambda i, s: (0, i)),
            ],
            scratch_shapes=[pltpu.VMEM((group, width), F32), pltpu.VMEM((group, LANES), F32)],
        ),
        out_shape=[jax.ShapeDtypeStruct(piece, BF)] * peers
        + [
            jax.ShapeDtypeStruct((group, width), BF),
            jax.ShapeDtypeStruct((experts, group, 2 * ff), BF),
            jax.ShapeDtypeStruct((group, experts * ff), BF),
        ],
        compiler_params=params(),
        cost_estimate=pl.CostEstimate(
            flops=2 * group * width * ff * 3 * experts,
            bytes_accessed=w.size * 2 + 5 * experts * group * ff * 2,
            transcendentals=experts * group * ff,
        ),
        name="experts_backward",
    )(scalars, *operands, gates, gu, w)


def middle_kernel(peers, sref, *refs):
    pieces, refs = refs[:peers], refs[peers:]
    grad_ref, hown_ref, gates_ref, b_ref, gains_ref, router_ref, dh_ref, do_ref, small_ref = refs
    rows, width = grad_ref.shape
    place = own_rows(sref[0], rows)
    joined = pieces[0][...].astype(F32)
    for shift in range(1, peers):
        joined = joined + pieces[shift][...].astype(F32)
    grad_normed = joined[:, :width]
    grad_gate = joined[:, width : width + E]
    gates = gates_ref[place, :]
    grad_logits = (
        gates * (grad_gate - jnp.sum(gates * grad_gate, axis=1, keepdims=True))
    ).astype(BF)
    normed = b_ref[place, :]
    grad_normed = grad_normed + dot_nt(grad_logits, router_ref[...])
    hidden = hown_ref[...]
    part, grad_gain = norm_back(hidden, rms_scale(hidden), gains_ref[1:2, :], grad_normed)
    grad_hidden = grad_ref[...].astype(F32) + part
    dh_ref[...] = grad_hidden
    do_ref[...] = grad_hidden.astype(BF)
    small_ref[0:E, :] = dot_tn(grad_logits, normed)
    small_ref[E : E + 1, :] = grad_gain
    small_ref[E + 1 :, :] = jnp.zeros((small_ref.shape[0] - E - 1, width), F32)


def middle(scalars, pieces, grad_own, hown, gates, b, gains, router):
    rows, width = grad_own.shape
    operands = [*pieces, grad_own, hown, gates, b, gains, router]
    return pl.pallas_call(
        lambda *refs: middle_kernel(len(pieces), *refs),
        grid_spec=pltpu.PrefetchScalarGridSpec(
            num_scalar_prefetch=1,
            grid=(1,),
            in_specs=[whole(x.shape) for x in operands],
            out_specs=[whole((rows, width)), whole((rows, width)), whole((24, width))],
        ),
        out_shape=[
            jax.ShapeDtypeStruct((rows, width), F32),
            jax.ShapeDtypeStruct((rows, width), BF),
            jax.ShapeDtypeStruct((24, width), F32),
        ],
        compiler_params=params(),
        cost_estimate=pl.CostEstimate(
            flops=rows * width * 64, bytes_accessed=rows * width * 24, transcendentals=rows
        ),
        name="norm_backward",
    )(scalars, *operands)


def attention_backward_kernel(peers, sref, *refs):
    pieces, refs = refs[:peers], refs[peers:]
    (
        dh_ref,
        xown_ref,
        gains_ref,
        cos_ref,
        sin_ref,
        bias_ref,
        qkv_ref,
        lse_ref,
        w_ref,
        dx_ref,
        dxlow_ref,
        gain_ref,
        full_ref,
        dqkv_ref,
        total,
        now,
    ) = refs
    step = pl.program_id(0)
    me = sref[0]
    group, width = full_ref.shape
    shard = dh_ref.shape[0]

    @pl.when(step == 0)
    def _():
        assemble(me, pieces, peers, full_ref)
        total[...] = jnp.zeros_like(total)

    weights = w_ref[:, 0].reshape(width, -1)
    do = dot(full_ref[...], weights[:, 512:]).astype(BF)
    qkv = qkv_ref[0]
    q, k, v = qkv[:, :256], qkv[:, 256:384], qkv[:, 384:]
    q_turned = q.T
    do_turned = do.T
    bias = bias_ref[0]
    lse = lse_ref[0]
    dq, dk, dv = [], [], []
    for kv in range(2):
        k_one = k[:, kv * HD : (kv + 1) * HD]
        v_one = v[:, kv * HD : (kv + 1) * HD]
        dk_one = dv_one = None
        for head in (2 * kv, 2 * kv + 1):
            part = slice(head * HD, (head + 1) * HD)
            scores = dot_nt(q[:, part], k_one) + bias
            soft = jnp.exp(scores - lse[:, head : head + 1])
            grad_soft = dot_nt(do[:, part], v_one)
            grad_scores = soft * (
                grad_soft - jnp.sum(soft * grad_soft, axis=1, keepdims=True)
            )
            grad_scores = grad_scores.astype(BF)
            dq.append(dot(grad_scores, k_one))
            dk_part = dot(q_turned[part, :], grad_scores)
            dv_part = dot(do_turned[part, :], soft.astype(BF))
            dk_one = dk_part if dk_one is None else dk_one + dk_part
            dv_one = dv_part if dv_one is None else dv_one + dv_part
        dk.append(dk_one)
        dv.append(dv_one)
    grad_k = jnp.concatenate(dk, axis=0).T
    grad_v = jnp.concatenate(dv, axis=0).T
    grad_qk = jnp.concatenate([jnp.concatenate(dq, axis=1) * HD**-0.5, grad_k], axis=1)
    cos = jnp.concatenate([cos_ref[0]] * 3, axis=1)
    sin = jnp.concatenate([sin_ref[0]] * 3, axis=1)
    grad_qk = (grad_qk * cos - swap_halves(grad_qk) * sin).astype(BF)
    now[:, :384] = grad_qk
    now[:, 384:] = grad_v.astype(BF)

    @pl.when(step == me)
    def _():
        dqkv_ref[...] = now[...]

    total[...] += dot_nt(now[own_rows(me, shard), :], weights[:, :512])

    @pl.when(step == pl.num_programs(0) - 1)
    def _():
        entering = xown_ref[...].astype(F32)
        part, grad_gain = norm_back(
            entering, rms_scale(entering), gains_ref[0:1, :], total[...]
        )
        grad_entering = dh_ref[...] + part
        dx_ref[...] = grad_entering
        dxlow_ref[...] = grad_entering.astype(BF)
        gain_ref[...] = jnp.broadcast_to(grad_gain, gain_ref.shape)


def attention_backward(scalars, pieces, dh, xown, gains, tables, qkv, lse, w_attn):
    dp, peers, dr, cols = w_attn.shape
    width = dp * dr
    group = qkv.shape[1]
    shard = group // peers
    cos, sin, bias = tables
    pick = lambda i, s: (s[1], 0, 0)
    per_step = lambda i, s: (i, 0, 0)
    return pl.pallas_call(
        lambda *refs: attention_backward_kernel(peers, *refs),
        grid_spec=pltpu.PrefetchScalarGridSpec(
            num_scalar_prefetch=1,
            grid=(peers,),
            in_specs=[whole(x.shape) for x in pieces]
            + [
                whole(dh.shape),
                whole(xown.shape),
                whole(gains.shape),
                pl.BlockSpec((1,) + cos.shape[1:], pick),
                pl.BlockSpec((1,) + sin.shape[1:], pick),
                pl.BlockSpec((1,) + bias.shape[1:], pick),
                pl.BlockSpec((1, group, 512), per_step),
                pl.BlockSpec((1, group, LANES), per_step),
                pl.BlockSpec((dp, 1, dr, cols), lambda i, s: (0, i, 0, 0)),
            ],
            out_specs=[
                whole((shard, width)),
                whole((shard, width)),
                whole((8, width)),
                whole((group, width)),
                whole((group, 512)),
            ],
            scratch_shapes=[pltpu.VMEM((shard, width), F32), pltpu.VMEM((group, 512), BF)],
        ),
        out_shape=[
            jax.ShapeDtypeStruct((shard, width), F32),
            jax.ShapeDtypeStruct((shard, width), BF),
            jax.ShapeDtypeStruct((8, width), F32),
            jax.ShapeDtypeStruct((group, width), BF),
            jax.ShapeDtypeStruct((group, 512), BF),
        ],
        compiler_params=params(),
        cost_estimate=pl.CostEstimate(
            flops=group * width * 1024 * 2 + 16 * 10 * group * group * HD,
            bytes_accessed=w_attn.size * 2 + 6 * group * width * 2,
            transcendentals=16 * group * group,
        ),
        name="attention_backward",
    )(scalars, *pieces, dh, xown, gains, cos, sin, bias, qkv, lse, w_attn)


def expert_weights_kernel(
    b0_ref, b1_ref, g0_ref, g1_ref, g2_ref, dgu0_ref, dgu1_ref, dgu2_ref,
    ga0_ref, ga1_ref, out_ref, bt_ref, gt_ref,
):
    group = b0_ref.shape[0]
    dp, _, _, dr, ff = out_ref.shape

    @pl.when(pl.program_id(0) == 0)
    def _():
        bt_ref[:, :group] = b0_ref[...].T
        bt_ref[:, group:] = b1_ref[...].T
        gt_ref[:, :group] = (g0_ref[...] + g2_ref[...]).T
        gt_ref[:, group:] = g1_ref[...].T

    bt = bt_ref[...]
    for j in range(PER):
        rows = jnp.concatenate([dgu0_ref[j] + dgu2_ref[j], dgu1_ref[j]], axis=0)
        grads = dot(bt, rows).astype(BF)
        out_ref[:, 0, j] = grads[:, :ff].reshape(dp, dr, ff)
        out_ref[:, 1, j] = grads[:, ff:].reshape(dp, dr, ff)
    rows = jnp.concatenate([ga0_ref[...], ga1_ref[...]], axis=0)
    grads = dot(gt_ref[...], rows).astype(BF)
    for j in range(PER):
        out_ref[:, 2, j] = grads[:, j * ff : (j + 1) * ff].reshape(dp, dr, ff)


def expert_weights(rows_b, grads, dgus, gas, dp, first, count):
    group, width = rows_b[0].shape
    _, _, ff2 = dgus[0].shape
    ff = ff2 // 2
    dr = width // dp
    base = first // PER
    square = pl.BlockSpec((group, width), lambda i: (0, 0))
    wide = pl.BlockSpec((PER, group, ff2), lambda i: (base + i, 0, 0))
    flat = pl.BlockSpec((group, PER * ff), lambda i: (0, base + i))
    return pl.pallas_call(
        expert_weights_kernel,
        grid=(count // PER,),
        in_specs=[square] * 5 + [wide] * 3 + [flat] * 2,
        out_specs=pl.BlockSpec((dp, 3, PER, dr, ff), lambda i: (0, 0, i, 0, 0)),
        out_shape=jax.ShapeDtypeStruct((dp, 3, count, dr, ff), BF),
        scratch_shapes=[pltpu.VMEM((width, 2 * group), BF), pltpu.VMEM((width, 2 * group), BF)],
        compiler_params=params(),
        cost_estimate=pl.CostEstimate(
            flops=4 * group * width * ff * 3 * count,
            bytes_accessed=dp * 3 * count * dr * ff * 2 + 9 * count * group * ff * 2,
            transcendentals=0,
        ),
        name="expert_weight_grads",
    )(*rows_b, *grads, *dgus, *gas)


def attention_weights_kernel(
    sref, a0_ref, a1_ref, o0_ref, o1_ref, f0_ref, f1_ref, f2_ref, d0_ref, d1_ref, d2_ref, out_ref
):
    dp, dr, _ = out_ref.shape
    first = dot_tn(a0_ref[...], d0_ref[...] + d2_ref[...]) + dot_tn(a1_ref[...], d1_ref[...])
    out_ref[:, :, :512] = first.astype(BF).reshape(dp, dr, 512)
    second = dot_tn(f0_ref[...] + f2_ref[...], o0_ref[0]) + dot_tn(f1_ref[...], o1_ref[0])
    out_ref[:, :, 512:] = second.astype(BF).reshape(dp, dr, 256)


def attention_weights(scalars, a_rows, o_rows, fulls, dqkvs, dp):
    group, width = a_rows[0].shape
    dr = width // dp
    own = pl.BlockSpec((1, group, 256), lambda i, s: (s[0], 0, 0))
    return pl.pallas_call(
        attention_weights_kernel,
        grid_spec=pltpu.PrefetchScalarGridSpec(
            num_scalar_prefetch=1,
            grid=(1,),
            in_specs=[whole((group, width))] * 2
            + [own] * 2
            + [whole((group, width))] * 3
            + [whole((group, 512))] * 3,
            out_specs=whole((dp, dr, 768)),
        ),
        out_shape=jax.ShapeDtypeStruct((dp, dr, 768), BF),
        compiler_params=params(),
        cost_estimate=pl.CostEstimate(
            flops=4 * group * width * 768,
            bytes_accessed=group * width * 14 + width * 768 * 2,
            transcendentals=0,
        ),
        name="attention_weight_grads",
    )(scalars, *a_rows, *o_rows, *fulls, *dqkvs)


def moved(array, peers, shift):
    return lax.ppermute(array, "tensor", [(i, (i + shift) % peers) for i in range(peers)])


def to_owner(pieces, peers):
    return [pieces[0]] + [moved(pieces[s], peers, s) for s in range(1, peers)]


def to_all(rows, peers):
    return [rows] + [moved(rows, peers, s) for s in range(1, peers)]


def across(rows, peers, up):
    start, end = (0, peers) if up else (peers, 0)
    return [
        lax.ppermute(
            rows,
            ("pipe", "tensor"),
            [(start + i, end + (i + s) % peers) for i in range(peers)],
        )
        for s in range(peers)
    ]


def tables_of(lengths, group):
    ends = jnp.cumsum(lengths)
    starts = ends - lengths
    index = jnp.arange(group, dtype=jnp.int32)
    inside = index[:, None] >= starts[None, :]
    start = jnp.max(jnp.where(inside, starts[None, :], 0), axis=1)
    position = (index - start).astype(F32)
    half = HD // 2
    freq = jnp.exp(jnp.arange(half, dtype=F32) * (-2.0 * math.log(10000.0) / HD))
    angle = position[:, None] * freq[None, :]
    cos, sin = jnp.cos(angle), jnp.sin(angle)
    visible = (index[None, :] <= index[:, None]) & (index[None, :] >= start[:, None])
    bias = jnp.where(visible, 0.0, MASKED).astype(F32)
    return (
        jnp.concatenate([cos, cos, cos, cos], axis=1),
        jnp.concatenate([-sin, sin, -sin, sin], axis=1),
        bias,
    )


def per_device(
    inputs, cotangent, doc_lengths, routes, norm_attn, w_query, w_key, w_value, w_out,
    w_router, norm_ffn, w_gate, w_up, w_down,
):
    section = lax.axis_index("pipe")
    first_section = section == 0
    me = lax.axis_index("tensor")
    peers = lax.axis_size("tensor")
    dp = lax.axis_size("dp")
    micro = inputs.shape[0]
    shard, width = inputs.shape[1:]
    group = shard * peers

    piece = jnp.concatenate([w_query[0], w_key[0], w_value[0], w_out[0].T], axis=1)
    w_attn = lax.all_gather(lax.all_gather(piece, "tensor", axis=0), "dp", axis=0)
    small = jnp.concatenate(
        [w_router[0], norm_attn[0][:, None], norm_ffn[0][:, None]], axis=1
    )
    small = lax.all_gather(small, ("dp", "tensor"), axis=0, tiled=True)
    router = small[:, :E]
    gains = small[:, E:].T.astype(F32)
    rows_in = lax.all_gather(inputs, "tensor", axis=1, tiled=True)
    rows_in = jnp.where(first_section, rows_in, jnp.zeros_like(rows_in))
    pieces_w = jnp.stack([w_gate[0], w_up[0], w_down[0].transpose(0, 2, 1)])
    w_experts = lax.all_gather(pieces_w, "dp", axis=0)
    own_cot = jnp.where(first_section, jnp.zeros_like(cotangent), cotangent)
    full_cot = lax.all_gather(own_cot, "tensor", axis=1, tiled=True)

    tables = jax.vmap(lambda lengths: tables_of(lengths, group))(doc_lengths[:, 0])
    ids = jnp.arange(E, dtype=jnp.int32)
    picked = jnp.any(routes[0][..., None] == ids, axis=2).astype(F32)

    outputs, saves = [], []
    received = None
    for tick in range(micro + 1):
        which = jnp.clip(tick - section, 0, micro - 1)
        scalars = jnp.stack([me, which]).astype(jnp.int32)
        pieces = received if received is not None else []
        full = rows_in[tick] if tick < micro else None
        a, xown, qkv, mixed, lse, hown, b, gates = attention_forward(
            scalars, pieces, full, gains, tables, picked, w_attn, router
        )
        *parts, gu = experts_forward(scalars, b, gates, w_experts, peers)
        parts = to_owner(parts, peers)
        result = hown
        for part in parts:
            result = result + part.astype(F32)
        sent = result.astype(BF)
        outputs.append(sent)
        saves.append((a, xown, qkv, mixed, lse, hown, b, gates, gu))
        if tick < micro:
            received = across(sent, peers, True)

    chosen = jax.tree.map(lambda x, y: jnp.where(first_section, x, y), saves[0], saves[2])
    kept = [saves[1], chosen, saves[1]]
    received = None
    grads_in, small_total, per_tick = [], None, []
    for tick in range(micro + 1):
        a, xown, qkv, mixed, lse, hown, b, gates, gu = kept[tick]
        which = jnp.clip(tick - 1 + section, 0, micro - 1)
        scalars = jnp.stack([me, which]).astype(jnp.int32)
        pieces = received if received is not None else []
        full = full_cot[tick] if tick < micro else None
        *parts, grad, dgu, ga = experts_backward(scalars, pieces, full, gates, gu, w_experts, peers)
        grad_own = None
        if tick < micro:
            grad_own = own_cot[tick]
        if pieces:
            grad_own = pieces[0] if grad_own is None else grad_own + pieces[0]
        parts = to_owner(parts, peers)
        dh, do, small_part = middle(scalars, parts, grad_own, hown, gates, b, gains, router)
        dx, dx_low, gain_part, do_full, dqkv = attention_backward(
            scalars, to_all(do, peers), dh, xown, gains, tables, qkv, lse, w_attn
        )
        grads_in.append(dx)
        if tick < micro:
            received = across(dx_low, peers, False)
        small_part = jnp.concatenate([small_part[: E + 1], gain_part[:1]], axis=0)
        small_total = small_part if small_total is None else small_total + small_part
        per_tick.append((grad, dgu, ga, do_full, dqkv))

    grad_rows, dgus, gas, fulls, dqkvs = ([t[i] for t in per_tick] for i in range(5))
    grad_experts = expert_weights(
        [kept[0][6], kept[1][6]], grad_rows, dgus, gas[:2], dp, 0, E
    )
    expert_sums = lax.psum_scatter(grad_experts, "dp", scatter_dimension=0, tiled=True)[0]
    grad_attn = attention_weights(
        scalars, [kept[0][0], kept[1][0]], [kept[0][3], kept[1][3]], fulls, dqkvs, dp
    )
    attn_sums = lax.psum_scatter(grad_attn, "dp", scatter_dimension=0, tiled=True)[0]
    small_sums = lax.psum_scatter(
        small_total.T, ("dp", "tensor"), scatter_dimension=0, tiled=True
    )
    expert_sums = expert_sums.astype(F32)
    attn_sums = attn_sums.astype(F32)
    cols_q, cols_k = w_query.shape[2], w_key.shape[2]
    section_rows = jnp.stack(
        [jnp.where(first_section, outputs[m], outputs[m + 1]) for m in range(micro)]
    )
    grad_in = jnp.stack(
        [jnp.where(first_section, grads_in[m + 1], grads_in[m]) for m in range(micro)]
    )
    return (
        section_rows[None],
        grad_in[None],
        small_sums[:, E + 1][None],
        attn_sums[:, :cols_q][None],
        attn_sums[:, cols_q : cols_q + cols_k][None],
        attn_sums[:, cols_q + cols_k : cols_q + 2 * cols_k][None],
        attn_sums[:, cols_q + 2 * cols_k :].T[None],
        small_sums[:, :E][None],
        small_sums[:, E][None],
        expert_sums[0][None],
        expert_sums[1][None],
        expert_sums[2].transpose(0, 2, 1)[None],
    )


def solution(mesh):
    in_specs = (
        P(None, ("dp", "tensor"), None),
        P(None, ("dp", "tensor"), None),
        P(None, "dp", None),
        P("pipe", None, "dp", None),
        P("pipe", ("dp", "tensor")),
        P("pipe", "dp", "tensor"),
        P("pipe", "dp", "tensor"),
        P("pipe", "dp", "tensor"),
        P("pipe", "tensor", "dp"),
        P("pipe", ("dp", "tensor"), None),
        P("pipe", ("dp", "tensor")),
        P("pipe", None, "dp", "tensor"),
        P("pipe", None, "dp", "tensor"),
        P("pipe", None, "tensor", "dp"),
    )
    out_specs = (
        P("pipe", None, ("dp", "tensor"), None),
        P("pipe", None, ("dp", "tensor"), None),
        P("pipe", ("dp", "tensor")),
        P("pipe", "dp", "tensor"),
        P("pipe", "dp", "tensor"),
        P("pipe", "dp", "tensor"),
        P("pipe", "tensor", "dp"),
        P("pipe", ("dp", "tensor"), None),
        P("pipe", ("dp", "tensor")),
        P("pipe", None, "dp", "tensor"),
        P("pipe", None, "dp", "tensor"),
        P("pipe", None, "tensor", "dp"),
    )
    return jax.shard_map(
        per_device, mesh=mesh, in_specs=in_specs, out_specs=out_specs, check_vma=False
    )
```

```python
import math

import jax
import jax.numpy as jnp
from jax import lax
from jax.experimental import pallas as pl
from jax.experimental.pallas import tpu as pltpu
from jax.sharding import PartitionSpec as P

HD = 64
E = 16
TOP = 8
EPSILON = 1e-06
MASKED = -1000000000.0
BF = jnp.bfloat16
F32 = jnp.float32
VMEM_LIMIT = 56 * 1024 * 1024
PER = 2
LANES = 128


def params():
    return pltpu.CompilerParams(
        vmem_limit_bytes=VMEM_LIMIT, dimension_semantics=("arbitrary",)
    )


def dot(left, right):
    return jnp.dot(left, right, preferred_element_type=F32)


def dot_nt(left, right):
    return lax.dot_general(
        left, right, (((1,), (1,)), ((), ())), preferred_element_type=F32
    )


def dot_tn(left, right):
    return lax.dot_general(
        left, right, (((0,), (0,)), ((), ())), preferred_element_type=F32
    )


def column(rows, index):
    lanes = lax.broadcasted_iota(jnp.int32, rows.shape, 1)
    return jnp.sum(jnp.where(lanes == index, rows, 0.0), axis=1, keepdims=True)


def whole(shape):
    return pl.BlockSpec(shape, lambda i, s: (0,) * len(shape))


def rms_scale(values):
    return lax.rsqrt(jnp.mean(values * values, axis=-1, keepdims=True) + EPSILON)


def norm_back(values, scale_rows, gain, grad_normed):
    weighted = grad_normed * gain
    grad_values = scale_rows * weighted - values * scale_rows**3 * jnp.mean(
        weighted * values, axis=-1, keepdims=True
    )
    grad_gain = jnp.sum(grad_normed * values * scale_rows, axis=0, keepdims=True)
    return grad_values, grad_gain


def swap_halves(values):
    width = values.shape[1]
    lanes = lax.broadcasted_iota(jnp.int32, values.shape, 1)
    ahead = pltpu.roll(values, width - HD // 2, 1)
    behind = pltpu.roll(values, HD // 2, 1)
    return jnp.where(lanes % HD < HD // 2, ahead, behind)


def assemble(me, pieces, target):
    rows = pieces[0].shape[0]
    for shift in range(4):
        owner = lax.rem(me + 4 - shift, 4)
        target[own_rows(owner, rows), :] = pieces[shift][...]


def own_rows(me, rows):
    return pl.ds(pl.multiple_of(me * rows, rows), rows)


def anywhere(count):
    return [pl.BlockSpec(memory_space=pl.ANY)] * count


def fetches(sources, buffers, sems):
    copies = []
    for shift in range(4):
        if shift == 2:
            half = sources[2].shape[0]
            copies.append(
                [
                    pltpu.make_async_copy(sources[2], buffers.at[2, pl.ds(0, half)], sems.at[2]),
                    pltpu.make_async_copy(
                        sources[3], buffers.at[2, pl.ds(half, half)], sems.at[4]
                    ),
                ]
            )
        else:
            source = sources[shift] if shift < 2 else sources[4]
            copies.append(
                [pltpu.make_async_copy(source, buffers.at[shift], sems.at[shift])]
            )
    return copies


def group_weights(buffers, step):
    dp = buffers.shape[1]
    blocks = [
        buffers[step, :, 64 * j : 64 * (j + 1), :].reshape(dp * 64, LANES) for j in range(6)
    ]
    return jnp.concatenate(blocks[:4], axis=1), jnp.concatenate(blocks[4:], axis=1)


def smalls_kernel(sref, *refs):
    sources, (router_ref, gains_ref, stage, sems) = refs[:5], refs[5:]
    dp = stage.shape[0]
    half = dp // 2
    me = sref[0]
    copies = []
    for place, source in enumerate(sources):
        shift = (0, 1, 2, 2, 3)[place]
        owner = lax.rem(me + 4 - shift, 4)
        rows = pl.ds(0, dp)
        if shift == 2:
            rows = pl.ds(half * (place - 2), half)
        copies.append(
            pltpu.make_async_copy(
                source.at[:, pl.ds(384, 16)], stage.at[rows, owner], sems.at[place]
            )
        )
    for copy in copies:
        copy.start()
    for copy in copies:
        copy.wait()
    rows = stage[...].reshape(dp * 64, LANES)
    router_ref[...] = rows
    turned = rows.astype(F32).T
    gains_ref[...] = turned[E : E + 8, :]


def smalls_of(scalars, w_attn):
    dp = w_attn[0].shape[0]
    width = dp * 64
    return pl.pallas_call(
        smalls_kernel,
        grid_spec=pltpu.PrefetchScalarGridSpec(
            num_scalar_prefetch=1,
            grid=(1,),
            in_specs=anywhere(5),
            out_specs=[whole((width, LANES)), whole((8, width))],
            scratch_shapes=[pltpu.VMEM((dp, 4, 16, LANES), BF), pltpu.SemaphoreType.DMA((5,))],
        ),
        out_shape=[
            jax.ShapeDtypeStruct((width, LANES), BF),
            jax.ShapeDtypeStruct((8, width), F32),
        ],
        compiler_params=params(),
        name="router_and_gains",
    )(scalars, *w_attn)


def attention_forward_kernel(n_after, sref, *refs):
    pieces, refs = refs[:4], refs[4:]
    sources, refs = refs[:5], refs[5 + n_after :]
    (
        gains_ref, cos_ref, sin_ref, bias_ref, picked_ref, router_ref,
        a_ref, xown_ref, qkv_ref, o_ref, lse_ref, hown_ref, b_ref, gates_ref,
        hidden, buffers, sems,
    ) = refs
    step = pl.program_id(0)
    me = sref[0]
    group, width = b_ref.shape
    shard = xown_ref.shape[0]

    @pl.when(sref[1] > 0)
    def _():
        copies = fetches(sources, buffers, sems)

        @pl.when(step == 0)
        def _():
            for part in copies:
                for copy in part:
                    copy.start()
            assemble(me, pieces, b_ref)
            entering = b_ref[...].astype(F32)
            a_ref[...] = (entering * rms_scale(entering) * gains_ref[0:1, :]).astype(BF)
            xown_ref[...] = pieces[0][...]
            hidden[...] = entering

        for shift, part in enumerate(copies):

            @pl.when(step == shift)
            def _(part=part):
                for copy in part:
                    copy.wait()

        w_qkv, w_out = group_weights(buffers, step)
        qkv = dot(a_ref[...], w_qkv)
        qk = qkv[:, :384]
        cos = jnp.concatenate([cos_ref[...]] * 3, axis=1)
        sin = jnp.concatenate([sin_ref[...]] * 3, axis=1)
        turned = qk * cos + swap_halves(qk) * sin
        q = (turned[:, :256] * HD**-0.5).astype(BF)
        k = turned[:, 256:].astype(BF)
        v = qkv[:, 384:].astype(BF)
        qkv_ref[0, :, :256] = q
        qkv_ref[0, :, 256:384] = k
        qkv_ref[0, :, 384:] = v
        bias = bias_ref[...]
        lanes = lax.broadcasted_iota(jnp.int32, (group, LANES), 1)
        lse_all = jnp.zeros((group, LANES), F32)
        outs = []
        for head in range(4):
            kv = head // 2
            scores = dot_nt(q[:, head * HD : (head + 1) * HD], k[:, kv * HD : (kv + 1) * HD])
            scores = scores + bias
            peak = jnp.max(scores, axis=1, keepdims=True)
            soft = jnp.exp(scores - peak)
            total = jnp.sum(soft, axis=1, keepdims=True)
            lse_all = jnp.where(lanes == head, peak + jnp.log(total), lse_all)
            soft = (soft * (1.0 / total)).astype(BF)
            outs.append(dot(soft, v[:, kv * HD : (kv + 1) * HD]))
        mixed = jnp.concatenate(outs, axis=1).astype(BF)

        @pl.when(step == 0)
        def _():
            o_ref[...] = mixed

        lse_ref[0] = lse_all
        hidden[...] += dot_nt(mixed, w_out)

        @pl.when(step == pl.num_programs(0) - 1)
        def _():
            rows = hidden[...]
            normed = (rows * rms_scale(rows) * gains_ref[1:2, :]).astype(BF)
            b_ref[...] = normed
            hown_ref[...] = hidden[own_rows(me, shard), :]
            logits = dot(normed, router_ref[...])[:, :E]
            picked = picked_ref[...]
            peak = jnp.max(jnp.where(picked > 0, logits, -1e30), axis=1, keepdims=True)
            powers = jnp.where(picked > 0, jnp.exp(jnp.minimum(logits - peak, 0.0)), 0.0)
            gates_ref[...] = powers / jnp.sum(powers, axis=1, keepdims=True)


def attention_forward(scalars, pieces, gains, tables, picked, w_attn, router, after):
    shard, width = pieces[0].shape
    group = 4 * shard
    dp = width // 64
    cos, sin, bias = tables
    smalls = [gains, cos, sin, bias, picked, router]
    per_step = lambda i, s: (i * s[1], 0, 0)
    outs = [
        ((group, width), BF, None),
        ((shard, width), BF, None),
        ((4, group, 512), BF, (1, group, 512)),
        ((group, 256), BF, None),
        ((4, group, LANES), F32, (1, group, LANES)),
        ((shard, width), F32, None),
        ((group, width), BF, None),
        ((group, E), F32, None),
    ]
    return pl.pallas_call(
        lambda *refs: attention_forward_kernel(len(after), *refs),
        grid_spec=pltpu.PrefetchScalarGridSpec(
            num_scalar_prefetch=1,
            grid=(4,),
            in_specs=[whole(x.shape) for x in pieces]
            + anywhere(5 + len(after))
            + [whole(x.shape) for x in smalls],
            out_specs=[
                whole(shape) if block is None else pl.BlockSpec(block, per_step)
                for shape, _, block in outs
            ],
            scratch_shapes=[
                pltpu.VMEM((group, width), F32),
                pltpu.VMEM((4, dp, 400, LANES), BF),
                pltpu.SemaphoreType.DMA((5,)),
            ],
        ),
        out_shape=[jax.ShapeDtypeStruct(shape, kind) for shape, kind, _ in outs],
        compiler_params=params(),
        cost_estimate=pl.CostEstimate(
            flops=2 * group * width * 768 * 4 + 16 * 4 * group * group * HD,
            bytes_accessed=width * 768 * 8 + 6 * group * width * 2,
            transcendentals=16 * group * group,
        ),
        name="attention_forward",
    )(scalars, *pieces, *w_attn, *after, *smalls)


def experts_forward_kernel(n_after, sref, *refs):
    (b_ref, gate_ref, w_ref, *refs) = refs[n_after:]
    pieces, (gu_ref, total) = refs[:4], refs[4:]
    step = pl.program_id(0)
    width = b_ref.shape[1]
    ff = w_ref.shape[-1]

    @pl.when(sref[1] > 0)
    def _():
        b = b_ref[...]
        gates = gate_ref[...]
        acts, downs = [], []
        for j in range(PER):
            gate_up = jnp.concatenate(
                [w_ref[:, 0, j].reshape(width, ff), w_ref[:, 1, j].reshape(width, ff)], axis=1
            )
            both = dot(b, gate_up)
            gu_ref[j] = both.astype(BF)
            gate_pre, up_pre = both[:, :ff], both[:, ff:]
            act = gate_pre * jax.nn.sigmoid(gate_pre) * up_pre
            acts.append((act * column(gates, step * PER + j)).astype(BF))
            downs.append(w_ref[:, 2, j].reshape(width, ff))
        out = dot_nt(jnp.concatenate(acts, axis=1), jnp.concatenate(downs, axis=1))

        @pl.when(step == 0)
        def _():
            total[...] = out

        @pl.when(step > 0)
        def _():
            total[...] += out

        @pl.when(step == pl.num_programs(0) - 1)
        def _():
            rows = b_ref.shape[0] // 4
            for shift in range(4):
                place = own_rows(lax.rem(sref[0] + shift, 4), rows)
                pieces[shift][...] = total[place, :].astype(BF)


def experts_forward(scalars, b, gates, w, after):
    group, width = b.shape
    dp, _, experts, dr, ff = w.shape
    piece = (group // 4, width)
    return pl.pallas_call(
        lambda *refs: experts_forward_kernel(len(after), *refs),
        grid_spec=pltpu.PrefetchScalarGridSpec(
            num_scalar_prefetch=1,
            grid=(experts // PER,),
            in_specs=anywhere(len(after))
            + [
                whole((group, width)),
                whole((group, experts)),
                pl.BlockSpec((dp, 3, PER, dr, ff), lambda i, s: (0, 0, i * s[1], 0, 0)),
            ],
            out_specs=[whole(piece)] * 4
            + [pl.BlockSpec((PER, group, 2 * ff), lambda i, s: (i * s[1], 0, 0))],
            scratch_shapes=[pltpu.VMEM((group, width), F32)],
        ),
        out_shape=[jax.ShapeDtypeStruct(piece, BF)] * 4
        + [jax.ShapeDtypeStruct((experts, group, 2 * ff), BF)],
        compiler_params=params(),
        cost_estimate=pl.CostEstimate(
            flops=2 * group * width * ff * 3 * experts,
            bytes_accessed=w.size * 2 + experts * group * 2 * ff * 2,
            transcendentals=experts * group * ff,
        ),
        name="experts_forward",
    )(scalars, *after, b, gates, w)


def experts_backward_kernel(n_after, sref, *refs):
    (*refs,) = refs[n_after:]
    given, refs = refs[:4], refs[4:]
    gate_ref, gu_ref, w_ref, *refs = refs
    pieces, refs = refs[:4], refs[4:]
    grad_ref, dgu_ref, ga_ref, total, total_gate = refs
    step = pl.program_id(0)
    group, width = grad_ref.shape
    ff = w_ref.shape[-1]

    @pl.when(sref[1] > 0)
    def _():
        @pl.when(step == 0)
        def _():
            assemble(sref[0], given, grad_ref)

        grad = grad_ref[...]
        gates = gate_ref[...]
        down = jnp.concatenate(
            [w_ref[:, 2, j].reshape(width, ff) for j in range(PER)], axis=1
        )
        turned = dot(grad, down)
        lanes = lax.broadcasted_iota(jnp.int32, (group, LANES), 1)
        grad_gate = jnp.zeros((group, LANES), F32)
        out = None
        for j in range(PER):
            expert = step * PER + j
            back = turned[:, j * ff : (j + 1) * ff]
            both = gu_ref[j].astype(F32)
            gate_pre, up_pre = both[:, :ff], both[:, ff:]
            sigma = jax.nn.sigmoid(gate_pre)
            silu = gate_pre * sigma
            act = silu * up_pre
            gate = column(gates, expert)
            grad_gate = jnp.where(
                lanes == expert, jnp.sum(act * back, axis=1, keepdims=True), grad_gate
            )
            grad_act = gate * back
            grad_pre = grad_act * up_pre * sigma * (1.0 + gate_pre * (1.0 - sigma))
            grad_up = grad_act * silu
            grad_both = jnp.concatenate([grad_pre.astype(BF), grad_up.astype(BF)], axis=1)
            dgu_ref[j] = grad_both
            ga_ref[:, j * ff : (j + 1) * ff] = (gate * act).astype(BF)
            gate_up = jnp.concatenate(
                [w_ref[:, 0, j].reshape(width, ff), w_ref[:, 1, j].reshape(width, ff)], axis=1
            )
            part = dot_nt(grad_both, gate_up)
            out = part if out is None else out + part

        @pl.when(step == 0)
        def _():
            total[...] = out
            total_gate[...] = grad_gate

        @pl.when(step > 0)
        def _():
            total[...] += out
            total_gate[...] += grad_gate

        @pl.when(step == pl.num_programs(0) - 1)
        def _():
            rows = group // 4
            for shift in range(4):
                place = own_rows(lax.rem(sref[0] + shift, 4), rows)
                pieces[shift][:, :width] = total[place, :].astype(BF)
                pieces[shift][:, width:] = total_gate[place, :].astype(BF)


def experts_backward(scalars, given, gates, gu, w, after):
    dp, _, experts, dr, ff = w.shape
    group = gates.shape[0]
    width = dp * dr
    piece = (group // 4, width + LANES)
    return pl.pallas_call(
        lambda *refs: experts_backward_kernel(len(after), *refs),
        grid_spec=pltpu.PrefetchScalarGridSpec(
            num_scalar_prefetch=1,
            grid=(experts // PER,),
            in_specs=anywhere(len(after))
            + [whole(x.shape) for x in given]
            + [
                whole((group, experts)),
                pl.BlockSpec((PER, group, 2 * ff), lambda i, s: (i * s[1], 0, 0)),
                pl.BlockSpec((dp, 3, PER, dr, ff), lambda i, s: (0, 0, i * s[1], 0, 0)),
            ],
            out_specs=[whole(piece)] * 4
            + [
                whole((group, width)),
                pl.BlockSpec((PER, group, 2 * ff), lambda i, s: (i * s[1], 0, 0)),
                pl.BlockSpec((group, PER * ff), lambda i, s: (0, i * s[1])),
            ],
            scratch_shapes=[pltpu.VMEM((group, width), F32), pltpu.VMEM((group, LANES), F32)],
        ),
        out_shape=[jax.ShapeDtypeStruct(piece, BF)] * 4
        + [
            jax.ShapeDtypeStruct((group, width), BF),
            jax.ShapeDtypeStruct((experts, group, 2 * ff), BF),
            jax.ShapeDtypeStruct((group, experts * ff), BF),
        ],
        compiler_params=params(),
        cost_estimate=pl.CostEstimate(
            flops=2 * group * width * ff * 3 * experts,
            bytes_accessed=w.size * 2 + 5 * experts * group * ff * 2,
            transcendentals=experts * group * ff,
        ),
        name="experts_backward",
    )(scalars, *after, *given, gates, gu, w)


def middle_kernel(n_after, sref, *refs):
    refs = refs[n_after:]
    pieces, refs = refs[:4], refs[4:]
    grad_ref, hown_ref, gates_ref, b_ref, gains_ref, router_ref, dh_ref, do_ref, small_ref = refs
    rows, width = grad_ref.shape

    @pl.when(sref[1] > 0)
    def _():
        place = own_rows(sref[0], rows)
        joined = pieces[0][...].astype(F32)
        for shift in range(1, 4):
            joined = joined + pieces[shift][...].astype(F32)
        grad_normed = joined[:, :width]
        grad_gate = joined[:, width : width + E]
        gates = gates_ref[place, :]
        grad_logits = (
            gates * (grad_gate - jnp.sum(gates * grad_gate, axis=1, keepdims=True))
        ).astype(BF)
        normed = b_ref[place, :]
        grad_normed = grad_normed + dot_nt(grad_logits, router_ref[:, :E])
        hidden = hown_ref[...]
        part, grad_gain = norm_back(hidden, rms_scale(hidden), gains_ref[1:2, :], grad_normed)
        grad_hidden = grad_ref[...].astype(F32) + part
        dh_ref[...] = grad_hidden
        do_ref[...] = grad_hidden.astype(BF)
        small_ref[0:E, :] = dot_tn(grad_logits, normed)
        small_ref[E : E + 1, :] = grad_gain
        small_ref[E + 1 :, :] = jnp.zeros((small_ref.shape[0] - E - 1, width), F32)


def middle(scalars, pieces, grad_own, hown, gates, b, gains, router, after):
    rows, width = grad_own.shape
    operands = [*pieces, grad_own, hown, gates, b, gains, router]
    return pl.pallas_call(
        lambda *refs: middle_kernel(len(after), *refs),
        grid_spec=pltpu.PrefetchScalarGridSpec(
            num_scalar_prefetch=1,
            grid=(1,),
            in_specs=anywhere(len(after)) + [whole(x.shape) for x in operands],
            out_specs=[whole((rows, width)), whole((rows, width)), whole((24, width))],
        ),
        out_shape=[
            jax.ShapeDtypeStruct((rows, width), F32),
            jax.ShapeDtypeStruct((rows, width), BF),
            jax.ShapeDtypeStruct((24, width), F32),
        ],
        compiler_params=params(),
        cost_estimate=pl.CostEstimate(
            flops=rows * width * 64, bytes_accessed=rows * width * 24, transcendentals=rows
        ),
        name="norm_backward",
    )(scalars, *after, *operands)


def attention_backward_kernel(n_after, sref, *refs):
    pieces, refs = refs[:4], refs[4:]
    sources, refs = refs[:5], refs[5 + n_after :]
    (
        dh_ref, xown_ref, small_ref, gains_ref, cos_ref, sin_ref, bias_ref, qkv_ref, lse_ref,
        dx_ref, dxlow_ref, small_out_ref, full_ref, dqkv_ref,
        total, now, buffers, sems,
    ) = refs
    step = pl.program_id(0)
    me = sref[0]
    shard = dh_ref.shape[0]

    @pl.when(sref[1] > 0)
    def _():
        copies = fetches(sources, buffers, sems)

        @pl.when(step == 0)
        def _():
            for part in copies:
                for copy in part:
                    copy.start()
            assemble(me, pieces, full_ref)
            total[...] = jnp.zeros_like(total)

        for shift, part in enumerate(copies):

            @pl.when(step == shift)
            def _(part=part):
                for copy in part:
                    copy.wait()

        w_qkv, w_out = group_weights(buffers, step)
        do = dot(full_ref[...], w_out).astype(BF)
        qkv = qkv_ref[0]
        q, k, v = qkv[:, :256], qkv[:, 256:384], qkv[:, 384:]
        q_turned = q.T
        do_turned = do.T
        bias = bias_ref[...]
        lse = lse_ref[0]
        dq, dk, dv = [], [], []
        for kv in range(2):
            k_one = k[:, kv * HD : (kv + 1) * HD]
            v_one = v[:, kv * HD : (kv + 1) * HD]
            dk_one = dv_one = None
            for head in (2 * kv, 2 * kv + 1):
                part = slice(head * HD, (head + 1) * HD)
                scores = dot_nt(q[:, part], k_one) + bias
                soft = jnp.exp(scores - lse[:, head : head + 1])
                grad_soft = dot_nt(do[:, part], v_one)
                grad_scores = soft * (
                    grad_soft - jnp.sum(soft * grad_soft, axis=1, keepdims=True)
                )
                grad_scores = grad_scores.astype(BF)
                dq.append(dot(grad_scores, k_one))
                dk_part = dot(q_turned[part, :], grad_scores)
                dv_part = dot(do_turned[part, :], soft.astype(BF))
                dk_one = dk_part if dk_one is None else dk_one + dk_part
                dv_one = dv_part if dv_one is None else dv_one + dv_part
            dk.append(dk_one)
            dv.append(dv_one)
        grad_k = jnp.concatenate(dk, axis=0).T
        grad_v = jnp.concatenate(dv, axis=0).T
        grad_qk = jnp.concatenate([jnp.concatenate(dq, axis=1) * HD**-0.5, grad_k], axis=1)
        cos = jnp.concatenate([cos_ref[...]] * 3, axis=1)
        sin = jnp.concatenate([sin_ref[...]] * 3, axis=1)
        grad_qk = (grad_qk * cos - swap_halves(grad_qk) * sin).astype(BF)
        now[:, :384] = grad_qk
        now[:, 384:] = grad_v.astype(BF)

        @pl.when(step == 0)
        def _():
            dqkv_ref[...] = now[...]

        total[...] += dot_nt(now[own_rows(me, shard), :], w_qkv)

        @pl.when(step == pl.num_programs(0) - 1)
        def _():
            entering = xown_ref[...].astype(F32)
            part, grad_gain = norm_back(
                entering, rms_scale(entering), gains_ref[0:1, :], total[...]
            )
            grad_entering = dh_ref[...] + part
            dx_ref[...] = grad_entering
            dxlow_ref[...] = grad_entering.astype(BF)
            rows = lax.broadcasted_iota(jnp.int32, small_ref.shape, 0)
            small_out_ref[...] = jnp.where(rows == E + 1, grad_gain, small_ref[...])


def attention_backward(
    scalars, pieces, dh, xown, small, gains, tables, qkv, lse, w_attn, after
):
    shard, width = dh.shape
    group = 4 * shard
    dp = width // 64
    cos, sin, bias = tables
    smalls = [dh, xown, small, gains, cos, sin, bias]
    per_step = lambda i, s: (i * s[1], 0, 0)
    outs = [
        ((shard, width), F32),
        ((shard, width), BF),
        (small.shape, F32),
        ((group, width), BF),
        ((group, 512), BF),
    ]
    return pl.pallas_call(
        lambda *refs: attention_backward_kernel(len(after), *refs),
        grid_spec=pltpu.PrefetchScalarGridSpec(
            num_scalar_prefetch=1,
            grid=(4,),
            in_specs=[whole(x.shape) for x in pieces]
            + anywhere(5 + len(after))
            + [whole(x.shape) for x in smalls]
            + [
                pl.BlockSpec((1, group, 512), per_step),
                pl.BlockSpec((1, group, LANES), per_step),
            ],
            out_specs=[whole(shape) for shape, _ in outs],
            scratch_shapes=[
                pltpu.VMEM((shard, width), F32),
                pltpu.VMEM((group, 512), BF),
                pltpu.VMEM((4, dp, 400, LANES), BF),
                pltpu.SemaphoreType.DMA((5,)),
            ],
        ),
        out_shape=[jax.ShapeDtypeStruct(shape, kind) for shape, kind in outs],
        compiler_params=params(),
        cost_estimate=pl.CostEstimate(
            flops=group * width * 1024 * 2 + 16 * 10 * group * group * HD,
            bytes_accessed=width * 768 * 8 + 6 * group * width * 2,
            transcendentals=16 * group * group,
        ),
        name="attention_backward",
    )(scalars, *pieces, *w_attn, *after, *smalls, qkv, lse)


def expert_weights_kernel(sref, *refs):
    b, refs = refs[:4], refs[4:]
    g, refs = refs[:4], refs[4:]
    dgu, refs = refs[:4], refs[4:]
    ga, refs = refs[:4], refs[4:]
    out_ref, bt_ref, gt_ref = refs
    group = b[0].shape[0]
    dp, _, _, dr, ff = out_ref.shape
    first = sref[1] > 0

    def chosen(four, micro, *index):
        index = index or (Ellipsis,)
        return jnp.where(first, four[micro][index], four[2 + micro][index])

    @pl.when(pl.program_id(0) == 0)
    def _():
        for micro in range(2):
            place = slice(micro * group, (micro + 1) * group)
            bt_ref[:, place] = chosen(b, micro).T
            gt_ref[:, place] = chosen(g, micro).T

    bt = bt_ref[...]
    for j in range(PER):
        rows = jnp.concatenate([chosen(dgu, 0, j), chosen(dgu, 1, j)], axis=0)
        grads = dot(bt, rows).astype(BF)
        out_ref[:, 0, j] = grads[:, :ff].reshape(dp, dr, ff)
        out_ref[:, 1, j] = grads[:, ff:].reshape(dp, dr, ff)
    rows = jnp.concatenate([chosen(ga, 0), chosen(ga, 1)], axis=0)
    grads = dot(gt_ref[...], rows).astype(BF)
    for j in range(PER):
        out_ref[:, 2, j] = grads[:, j * ff : (j + 1) * ff].reshape(dp, dr, ff)


def expert_weights(scalars, rows_b, grads, dgus, gas, dp):
    group, width = rows_b[0].shape
    experts, _, ff2 = dgus[0].shape
    ff = ff2 // 2
    dr = width // dp
    square = whole((group, width))
    wide, flat = [], []
    for held in (lambda s: s[1], lambda s: 1 - s[1]):
        wide += [
            pl.BlockSpec((PER, group, ff2), lambda i, s, held=held: (i * held(s), 0, 0))
        ] * 2
        flat += [pl.BlockSpec((group, PER * ff), lambda i, s, held=held: (0, i * held(s)))] * 2
    return pl.pallas_call(
        expert_weights_kernel,
        grid_spec=pltpu.PrefetchScalarGridSpec(
            num_scalar_prefetch=1,
            grid=(experts // PER,),
            in_specs=[square] * 8 + wide + flat,
            out_specs=pl.BlockSpec((dp, 3, PER, dr, ff), lambda i, s: (0, 0, i, 0, 0)),
            scratch_shapes=[
                pltpu.VMEM((width, 2 * group), BF),
                pltpu.VMEM((width, 2 * group), BF),
            ],
        ),
        out_shape=jax.ShapeDtypeStruct((dp, 3, experts, dr, ff), BF),
        compiler_params=params(),
        cost_estimate=pl.CostEstimate(
            flops=4 * group * width * ff * 3 * experts,
            bytes_accessed=dp * 3 * experts * dr * ff * 2 + 6 * experts * group * ff * 2,
            transcendentals=0,
        ),
        name="expert_weight_grads",
    )(scalars, *rows_b, *grads, *dgus, *gas)


def attention_weights_kernel(sref, *refs):
    a, o, f, d, small = (refs[4 * j : 4 * j + 4] for j in range(5))
    out_ref = refs[20]
    dp = out_ref.shape[0]
    first = sref[1] > 0

    def chosen(four, micro):
        return jnp.where(first, four[micro][...], four[2 + micro][...])

    sums = dot_tn(chosen(a, 0), chosen(d, 0)) + dot_tn(chosen(a, 1), chosen(d, 1))
    for j in range(4):
        out_ref[:, 64 * j : 64 * (j + 1), :] = (
            sums[:, LANES * j : LANES * (j + 1)].astype(BF).reshape(dp, 64, LANES)
        )
    sums = dot_tn(chosen(f, 0), chosen(o, 0)) + dot_tn(chosen(f, 1), chosen(o, 1))
    for j in range(2):
        out_ref[:, 64 * (4 + j) : 64 * (5 + j), :] = (
            sums[:, LANES * j : LANES * (j + 1)].astype(BF).reshape(dp, 64, LANES)
        )
    rows = chosen(small, 0) + chosen(small, 1)
    rows = jnp.concatenate(
        [rows, jnp.zeros((LANES - rows.shape[0], rows.shape[1]), F32)], axis=0
    )
    out_ref[:, 384:, :] = rows.T.astype(BF).reshape(dp, 64, LANES)


def attention_weights(scalars, a, o, f, d, small, dp):
    group, width = a[0].shape
    operands = [*a, *o, *f, *d, *small]
    return pl.pallas_call(
        attention_weights_kernel,
        grid_spec=pltpu.PrefetchScalarGridSpec(
            num_scalar_prefetch=1,
            grid=(1,),
            in_specs=[whole(x.shape) for x in operands],
            out_specs=whole((dp, 448, LANES)),
        ),
        out_shape=jax.ShapeDtypeStruct((dp, 448, LANES), BF),
        compiler_params=params(),
        cost_estimate=pl.CostEstimate(
            flops=4 * group * width * 768,
            bytes_accessed=group * width * 14 + width * 768 * 2,
            transcendentals=0,
        ),
        name="attention_weight_grads",
    )(scalars, *operands)


def moved(array, shift):
    return lax.ppermute(array, "tensor", [(i, (i + shift) % 4) for i in range(4)])


def to_owner(pieces):
    return [pieces[0]] + [moved(pieces[s], s) for s in range(1, 4)]


def to_all(rows):
    return [rows] + [moved(rows, s) for s in range(1, 4)]


def across(rows, up):
    start, end = (0, 4) if up else (4, 0)
    return [
        lax.ppermute(
            rows, ("pipe", "tensor"), [(start + i, end + (i + s) % 4) for i in range(4)]
        )
        for s in range(4)
    ]


def tables_of(lengths, group):
    ends = jnp.cumsum(lengths)
    starts = ends - lengths
    index = jnp.arange(group, dtype=jnp.int32)
    inside = index[:, None] >= starts[None, :]
    start = jnp.max(jnp.where(inside, starts[None, :], 0), axis=1)
    position = (index - start).astype(F32)
    half = HD // 2
    freq = jnp.exp(jnp.arange(half, dtype=F32) * (-2.0 * math.log(10000.0) / HD))
    angle = position[:, None] * freq[None, :]
    cos, sin = jnp.cos(angle), jnp.sin(angle)
    visible = (index[None, :] <= index[:, None]) & (index[None, :] >= start[:, None])
    bias = jnp.where(visible, 0.0, MASKED).astype(F32)
    return (
        jnp.concatenate([cos, cos, cos, cos], axis=1),
        jnp.concatenate([-sin, sin, -sin, sin], axis=1),
        bias,
    )


def per_device(
    inputs, cotangent, doc_lengths, routes, norm_attn, w_query, w_key, w_value, w_out,
    w_router, norm_ffn, w_gate, w_up, w_down,
):
    section = lax.axis_index("pipe")
    first_section = section == 0
    me = lax.axis_index("tensor")
    dp = lax.axis_size("dp")
    micro = inputs.shape[0]
    shard, width = inputs.shape[1:]
    group = shard * 4
    rows_dp = width // dp
    scalars = [
        jnp.stack([me, (section == s).astype(jnp.int32)]).astype(jnp.int32) for s in range(2)
    ]

    out_turned = w_out[0].T
    small = jnp.concatenate([w_router[0], norm_attn[0][:, None], norm_ffn[0][:, None]], axis=1)
    small = jnp.pad(small, ((0, 0), (0, LANES - E - 2)))
    piece = jnp.concatenate(
        [
            w_query[0][:, :LANES], w_query[0][:, LANES:], w_key[0], w_value[0],
            out_turned[:, :LANES], out_turned[:, LANES:], small,
        ],
        axis=0,
    )
    w_own = lax.all_gather(piece, "dp", axis=0)
    pieces_w = jnp.stack([w_gate[0], w_up[0], w_down[0].transpose(0, 2, 1)])
    pieces_w, w_own = lax.optimization_barrier((pieces_w, w_own))
    w_experts = lax.all_gather(pieces_w, "dp", axis=0)
    w_next, w_last = moved(w_own, 1), moved(w_own, 3)
    half = dp // 2
    w_attn = [w_own, w_next, moved(w_next[:half], 1), moved(w_last[half:], 3), w_last]
    router, gains = smalls_of(scalars[0], w_attn)

    rows_in = to_all(inputs)
    rows_in = [[part[m] for part in rows_in] for m in range(micro)]
    rows_cot = to_all(cotangent)
    rows_cot = [[part[m] for part in rows_cot] for m in range(micro)]
    tables = [tables_of(doc_lengths[m, 0], group) for m in range(micro)]
    ids = jnp.arange(E, dtype=jnp.int32)
    picked = jnp.any(routes[0][..., None] == ids, axis=2).astype(F32)

    outputs, saves = [], []
    entering, after = rows_in, []
    for s in range(2):
        kept, sent = [], []
        for m in range(micro):
            (a, xown, qkv, mixed, lse, hown, b, gates) = attention_forward(
                scalars[s], entering[m], gains, tables[m], picked[m], w_attn, router, after
            )
            if m > 0:
                sent.append(finish(parts, hown_before))
            *parts, gu = experts_forward(
                scalars[s], b, gates, w_experts, [sent[-1]] if m > 0 else []
            )
            parts = to_owner(parts)
            hown_before = hown
            after = [gu]
            kept.append((a, xown, qkv, mixed, lse, hown, b, gates, gu))
            if m > 0 and s == 0:
                received = [across(sent[0], True)]
        sent.append(finish(parts, hown_before))
        if s == 0:
            received.append(across(sent[1], True))
            entering = received
        outputs.append(sent)
        saves.append(kept)

    given, own = rows_cot, [cotangent[m] for m in range(micro)]
    grads_in, results = [None, None], [None, None]
    for s in (1, 0):
        kept = saves[s]
        firsts = []
        for m in range(micro):
            gates, gu = kept[m][7], kept[m][8]
            *parts, grad, dgu, ga = experts_backward(
                scalars[s], given[m], gates, gu, w_experts, after
            )
            after = [grad]
            firsts.append((to_owner(parts), grad, dgu, ga))
        if s == 0:
            grad_experts = expert_weights(
                scalars[0],
                [saves[j][m][6] for j in range(2) for m in range(micro)],
                [x[1] for x in firsts + results[1][0]],
                [x[2] for x in firsts + results[1][0]],
                [x[3] for x in firsts + results[1][0]],
                dp,
            )
            after = [grad_experts]
        middles = []
        for m in range(micro):
            dh, do, small = middle(
                scalars[s], firsts[m][0], own[m], kept[m][5], kept[m][7], kept[m][6],
                gains, router, after,
            )
            middles.append((dh, to_all(do), small))
            after = [do]
        lasts, dxs = [], []
        for m in range(micro):
            dh, rows_do, small = middles[m]
            dx, dx_low, small, full, dqkv = attention_backward(
                scalars[s], rows_do, dh, kept[m][1], small, gains, tables[m],
                kept[m][2], kept[m][4], w_attn, after,
            )
            after = [dx]
            dxs.append(dx)
            lasts.append((small, full, dqkv))
            if s == 1:
                if m == 0:
                    received = []
                received.append(across(dx_low, False))
        grads_in[s] = dxs
        results[s] = (firsts, lasts)
        if s == 1:
            given, own = received, [pieces[0] for pieces in received]

    expert_sums = lax.psum_scatter(grad_experts, "dp", scatter_dimension=0, tiled=True)[0]
    lasts = results[0][1] + results[1][1]
    grad_attn = attention_weights(
        scalars[0],
        [saves[s][m][0] for s in range(2) for m in range(micro)],
        [saves[s][m][3] for s in range(2) for m in range(micro)],
        [x[1] for x in lasts],
        [x[2] for x in lasts],
        [x[0] for x in lasts],
        dp,
    )
    grad_attn = lax.all_to_all(grad_attn, "dp", 0, 0, tiled=True)
    attn_sums = jnp.sum(grad_attn.astype(F32), axis=0)
    small = attn_sums[384:].reshape(4, 16, LANES)
    small_own = None
    for shift in range(4):
        part = lax.dynamic_index_in_dim(small, (me + shift) % 4, 0, keepdims=False)
        part = moved(part, shift) if shift else part
        small_own = part if small_own is None else small_own + part
    expert_sums = expert_sums.astype(F32)
    blocks = [attn_sums[64 * j : 64 * (j + 1)] for j in range(6)]
    section_rows = jnp.stack(
        [jnp.where(first_section, outputs[0][m], outputs[1][m]) for m in range(micro)]
    )
    grad_in = jnp.stack(
        [jnp.where(first_section, grads_in[0][m], grads_in[1][m]) for m in range(micro)]
    )
    return (
        section_rows[None],
        grad_in[None],
        small_own[:, E + 1][None],
        jnp.concatenate(blocks[:2], axis=1)[None],
        blocks[2][None],
        blocks[3][None],
        jnp.concatenate(blocks[4:], axis=1).T[None],
        small_own[:, :E][None],
        small_own[:, E][None],
        expert_sums[0][None],
        expert_sums[1][None],
        expert_sums[2].transpose(0, 2, 1)[None],
    )


def finish(parts, hown):
    result = hown
    for part in parts:
        result = result + part.astype(F32)
    return result.astype(BF)


def solution(mesh):
    in_specs = (
        P(None, ("dp", "tensor"), None),
        P(None, ("dp", "tensor"), None),
        P(None, "dp", None),
        P("pipe", None, "dp", None),
        P("pipe", ("dp", "tensor")),
        P("pipe", "dp", "tensor"),
        P("pipe", "dp", "tensor"),
        P("pipe", "dp", "tensor"),
        P("pipe", "tensor", "dp"),
        P("pipe", ("dp", "tensor"), None),
        P("pipe", ("dp", "tensor")),
        P("pipe", None, "dp", "tensor"),
        P("pipe", None, "dp", "tensor"),
        P("pipe", None, "tensor", "dp"),
    )
    out_specs = (
        P("pipe", None, ("dp", "tensor"), None),
        P("pipe", None, ("dp", "tensor"), None),
        P("pipe", ("dp", "tensor")),
        P("pipe", "dp", "tensor"),
        P("pipe", "dp", "tensor"),
        P("pipe", "dp", "tensor"),
        P("pipe", "tensor", "dp"),
        P("pipe", ("dp", "tensor"), None),
        P("pipe", ("dp", "tensor")),
        P("pipe", None, "dp", "tensor"),
        P("pipe", None, "dp", "tensor"),
        P("pipe", None, "tensor", "dp"),
    )
    return jax.shard_map(
        per_device, mesh=mesh, in_specs=in_specs, out_specs=out_specs, check_vma=False
    )
```

```python
import math

import jax
import jax.numpy as jnp
from jax import lax
from jax.experimental import pallas as pl
from jax.experimental.pallas import tpu as pltpu
from jax.sharding import PartitionSpec as P

HD = 64
E = 16
TOP = 8
EPSILON = 1e-06
MASKED = -1000000000.0
BF = jnp.bfloat16
F32 = jnp.float32
VMEM_LIMIT = 56 * 1024 * 1024
PER = 2
LANES = 128


def params():
    return pltpu.CompilerParams(
        vmem_limit_bytes=VMEM_LIMIT, dimension_semantics=("arbitrary",)
    )


def dot(left, right):
    return jnp.dot(left, right, preferred_element_type=F32)


def dot_nt(left, right):
    return lax.dot_general(
        left, right, (((1,), (1,)), ((), ())), preferred_element_type=F32
    )


def dot_tn(left, right):
    return lax.dot_general(
        left, right, (((0,), (0,)), ((), ())), preferred_element_type=F32
    )


def column(rows, index):
    lanes = lax.broadcasted_iota(jnp.int32, rows.shape, 1)
    return jnp.sum(jnp.where(lanes == index, rows, 0.0), axis=1, keepdims=True)


def whole(shape):
    return pl.BlockSpec(shape, lambda i, s: (0,) * len(shape))


def rms_scale(values):
    return lax.rsqrt(jnp.mean(values * values, axis=-1, keepdims=True) + EPSILON)


def norm_back(values, scale_rows, gain, grad_normed):
    weighted = grad_normed * gain
    grad_values = scale_rows * weighted - values * scale_rows**3 * jnp.mean(
        weighted * values, axis=-1, keepdims=True
    )
    grad_gain = jnp.sum(grad_normed * values * scale_rows, axis=0, keepdims=True)
    return grad_values, grad_gain


def swap_halves(values):
    width = values.shape[1]
    lanes = lax.broadcasted_iota(jnp.int32, values.shape, 1)
    ahead = pltpu.roll(values, width - HD // 2, 1)
    behind = pltpu.roll(values, HD // 2, 1)
    return jnp.where(lanes % HD < HD // 2, ahead, behind)


def assemble(me, pieces, target):
    rows = pieces[0].shape[0]
    for shift in range(4):
        owner = lax.rem(me + 4 - shift, 4)
        target[own_rows(owner, rows), :] = pieces[shift][...]


def own_rows(me, rows):
    return pl.ds(pl.multiple_of(me * rows, rows), rows)


def anywhere(count):
    return [pl.BlockSpec(memory_space=pl.ANY)] * count


def fetches(core, sources, buffers, sems):
    dp = buffers.shape[1]
    half, quarter = dp // 2, dp // 4
    here, there = core * half, (1 - core) * half
    copies = [[pltpu.make_async_copy(sources[0], buffers.at[0], sems.at[0])]]
    number = 1
    for shift, starts in (
        (1, (here, there)),
        (2, (here, here + quarter, there, there + quarter)),
        (3, (here, there)),
    ):
        group = []
        for start in starts:
            source = sources[number]
            place = buffers.at[shift, pl.ds(start, source.shape[0])]
            group.append(pltpu.make_async_copy(source, place, sems.at[number]))
            number += 1
        copies.append(group)
    return copies


def group_weights(buffers, step):
    dp = buffers.shape[1]
    blocks = [
        buffers[step, :, 64 * j : 64 * (j + 1), :].reshape(dp * 64, LANES) for j in range(6)
    ]
    return jnp.concatenate(blocks[:4], axis=1), jnp.concatenate(blocks[4:], axis=1)


def smalls_kernel(sref, *refs):
    sources, (router_ref, gains_ref, stage, sems) = refs[:9], refs[9:]
    dp = stage.shape[0]
    half, quarter = dp // 2, dp // 4
    me = sref[0]
    here, there = sref[2] * half, (1 - sref[2]) * half
    places = (
        (0, 0), (1, here), (1, there),
        (2, here), (2, here + quarter), (2, there), (2, there + quarter), (3, here), (3, there),
    )
    copies = []
    for number, (shift, start) in enumerate(places):
        source = sources[number]
        owner = lax.rem(me + 4 - shift, 4)
        copies.append(
            pltpu.make_async_copy(
                source.at[:, pl.ds(384, 16)],
                stage.at[pl.ds(start, source.shape[0]), owner],
                sems.at[number],
            )
        )
    for copy in copies:
        copy.start()
    for copy in copies:
        copy.wait()
    rows = stage[...].reshape(dp * 64, LANES)
    router_ref[...] = rows
    turned = rows.astype(F32).T
    gains_ref[...] = turned[E : E + 8, :]


def smalls_of(scalars, w_attn):
    dp = w_attn[0].shape[0]
    width = dp * 64
    return pl.pallas_call(
        smalls_kernel,
        grid_spec=pltpu.PrefetchScalarGridSpec(
            num_scalar_prefetch=1,
            grid=(1,),
            in_specs=anywhere(9),
            out_specs=[whole((width, LANES)), whole((8, width))],
            scratch_shapes=[pltpu.VMEM((dp, 4, 16, LANES), BF), pltpu.SemaphoreType.DMA((9,))],
        ),
        out_shape=[
            jax.ShapeDtypeStruct((width, LANES), BF),
            jax.ShapeDtypeStruct((8, width), F32),
        ],
        compiler_params=params(),
        name="router_and_gains",
    )(scalars, *w_attn)


def attention_forward_kernel(n_after, sref, *refs):
    pieces, refs = refs[:4], refs[4:]
    sources, refs = refs[:9], refs[9 + n_after :]
    (
        gains_ref, cos_ref, sin_ref, bias_ref, picked_ref, router_ref,
        a_ref, xown_ref, qkv_ref, o_ref, lse_ref, hown_ref, b_ref, gates_ref,
        hidden, buffers, sems,
    ) = refs
    step = pl.program_id(0)
    me = sref[0]
    group, width = b_ref.shape
    shard = xown_ref.shape[0]

    @pl.when(sref[1] > 0)
    def _():
        copies = fetches(sref[2], sources, buffers, sems)

        @pl.when(step == 0)
        def _():
            for part in copies:
                for copy in part:
                    copy.start()
            assemble(me, pieces, b_ref)
            entering = b_ref[...].astype(F32)
            a_ref[...] = (entering * rms_scale(entering) * gains_ref[0:1, :]).astype(BF)
            xown_ref[...] = pieces[0][...]
            hidden[...] = entering

        for shift, part in enumerate(copies):

            @pl.when(step == shift)
            def _(part=part):
                for copy in part:
                    copy.wait()

        w_qkv, w_out = group_weights(buffers, step)
        qkv = dot(a_ref[...], w_qkv)
        qk = qkv[:, :384]
        cos = jnp.concatenate([cos_ref[...]] * 3, axis=1)
        sin = jnp.concatenate([sin_ref[...]] * 3, axis=1)
        turned = qk * cos + swap_halves(qk) * sin
        q = (turned[:, :256] * HD**-0.5).astype(BF)
        k = turned[:, 256:].astype(BF)
        v = qkv[:, 384:].astype(BF)
        qkv_ref[0, :, :256] = q
        qkv_ref[0, :, 256:384] = k
        qkv_ref[0, :, 384:] = v
        bias = bias_ref[...]
        lanes = lax.broadcasted_iota(jnp.int32, (group, LANES), 1)
        lse_all = jnp.zeros((group, LANES), F32)
        outs = []
        for head in range(4):
            kv = head // 2
            scores = dot_nt(q[:, head * HD : (head + 1) * HD], k[:, kv * HD : (kv + 1) * HD])
            scores = scores + bias
            peak = jnp.max(scores, axis=1, keepdims=True)
            soft = jnp.exp(scores - peak)
            total = jnp.sum(soft, axis=1, keepdims=True)
            lse_all = jnp.where(lanes == head, peak + jnp.log(total), lse_all)
            soft = (soft * (1.0 / total)).astype(BF)
            outs.append(dot(soft, v[:, kv * HD : (kv + 1) * HD]))
        mixed = jnp.concatenate(outs, axis=1).astype(BF)

        @pl.when(step == 0)
        def _():
            o_ref[...] = mixed

        lse_ref[0] = lse_all
        hidden[...] += dot_nt(mixed, w_out)

        @pl.when(step == pl.num_programs(0) - 1)
        def _():
            rows = hidden[...]
            normed = (rows * rms_scale(rows) * gains_ref[1:2, :]).astype(BF)
            b_ref[...] = normed
            hown_ref[...] = hidden[own_rows(me, shard), :]
            logits = dot(normed, router_ref[...])[:, :E]
            picked = picked_ref[...]
            peak = jnp.max(jnp.where(picked > 0, logits, -1e30), axis=1, keepdims=True)
            powers = jnp.where(picked > 0, jnp.exp(jnp.minimum(logits - peak, 0.0)), 0.0)
            gates_ref[...] = powers / jnp.sum(powers, axis=1, keepdims=True)


def attention_forward(scalars, pieces, gains, tables, picked, w_attn, router, after):
    shard, width = pieces[0].shape
    group = 4 * shard
    dp = width // 64
    cos, sin, bias = tables
    smalls = [gains, cos, sin, bias, picked, router]
    per_step = lambda i, s: (i * s[1], 0, 0)
    outs = [
        ((group, width), BF, None),
        ((shard, width), BF, None),
        ((4, group, 512), BF, (1, group, 512)),
        ((group, 256), BF, None),
        ((4, group, LANES), F32, (1, group, LANES)),
        ((shard, width), F32, None),
        ((group, width), BF, None),
        ((group, E), F32, None),
    ]
    return pl.pallas_call(
        lambda *refs: attention_forward_kernel(len(after), *refs),
        grid_spec=pltpu.PrefetchScalarGridSpec(
            num_scalar_prefetch=1,
            grid=(4,),
            in_specs=[whole(x.shape) for x in pieces]
            + anywhere(9 + len(after))
            + [whole(x.shape) for x in smalls],
            out_specs=[
                whole(shape) if block is None else pl.BlockSpec(block, per_step)
                for shape, _, block in outs
            ],
            scratch_shapes=[
                pltpu.VMEM((group, width), F32),
                pltpu.VMEM((4, dp, 400, LANES), BF),
                pltpu.SemaphoreType.DMA((9,)),
            ],
        ),
        out_shape=[jax.ShapeDtypeStruct(shape, kind) for shape, kind, _ in outs],
        compiler_params=params(),
        cost_estimate=pl.CostEstimate(
            flops=2 * group * width * 768 * 4 + 16 * 4 * group * group * HD,
            bytes_accessed=width * 768 * 8 + 6 * group * width * 2,
            transcendentals=16 * group * group,
        ),
        name="attention_forward",
    )(scalars, *pieces, *w_attn, *after, *smalls)


def experts_forward_kernel(n_after, sref, *refs):
    (b_ref, gate_ref, w_ref, *refs) = refs[n_after:]
    pieces, (gu_ref, total) = refs[:4], refs[4:]
    step = pl.program_id(0)
    width = b_ref.shape[1]
    ff = w_ref.shape[-1]

    @pl.when(sref[1] > 0)
    def _():
        b = b_ref[...]
        gates = gate_ref[...]
        acts, downs = [], []
        for j in range(PER):
            gate_up = jnp.concatenate(
                [w_ref[:, 0, j].reshape(width, ff), w_ref[:, 1, j].reshape(width, ff)], axis=1
            )
            both = dot(b, gate_up)
            gu_ref[j] = both.astype(BF)
            gate_pre, up_pre = both[:, :ff], both[:, ff:]
            act = gate_pre * jax.nn.sigmoid(gate_pre) * up_pre
            acts.append((act * column(gates, step * PER + j)).astype(BF))
            downs.append(w_ref[:, 2, j].reshape(width, ff))
        out = dot_nt(jnp.concatenate(acts, axis=1), jnp.concatenate(downs, axis=1))

        @pl.when(step == 0)
        def _():
            total[...] = out

        @pl.when(step > 0)
        def _():
            total[...] += out

        @pl.when(step == pl.num_programs(0) - 1)
        def _():
            rows = b_ref.shape[0] // 4
            for shift in range(4):
                place = own_rows(lax.rem(sref[0] + shift, 4), rows)
                pieces[shift][...] = total[place, :].astype(BF)


def experts_forward(scalars, b, gates, w, after):
    group, width = b.shape
    dp, _, experts, dr, ff = w.shape
    piece = (group // 4, width)
    return pl.pallas_call(
        lambda *refs: experts_forward_kernel(len(after), *refs),
        grid_spec=pltpu.PrefetchScalarGridSpec(
            num_scalar_prefetch=1,
            grid=(experts // PER,),
            in_specs=anywhere(len(after))
            + [
                whole((group, width)),
                whole((group, experts)),
                pl.BlockSpec((dp, 3, PER, dr, ff), lambda i, s: (0, 0, i * s[1], 0, 0)),
            ],
            out_specs=[whole(piece)] * 4
            + [pl.BlockSpec((PER, group, 2 * ff), lambda i, s: (i * s[1], 0, 0))],
            scratch_shapes=[pltpu.VMEM((group, width), F32)],
        ),
        out_shape=[jax.ShapeDtypeStruct(piece, BF)] * 4
        + [jax.ShapeDtypeStruct((experts, group, 2 * ff), BF)],
        compiler_params=params(),
        cost_estimate=pl.CostEstimate(
            flops=2 * group * width * ff * 3 * experts,
            bytes_accessed=w.size * 2 + experts * group * 2 * ff * 2,
            transcendentals=experts * group * ff,
        ),
        name="experts_forward",
    )(scalars, *after, b, gates, w)


def experts_backward_kernel(n_after, sref, *refs):
    (*refs,) = refs[n_after:]
    given, refs = refs[:4], refs[4:]
    gate_ref, gu_ref, w_ref, *refs = refs
    pieces, refs = refs[:4], refs[4:]
    grad_ref, dgu_ref, ga_ref, total, total_gate = refs
    step = pl.program_id(0)
    group, width = grad_ref.shape
    ff = w_ref.shape[-1]

    @pl.when(sref[1] > 0)
    def _():
        @pl.when(step == 0)
        def _():
            assemble(sref[0], given, grad_ref)

        grad = grad_ref[...]
        gates = gate_ref[...]
        down = jnp.concatenate(
            [w_ref[:, 2, j].reshape(width, ff) for j in range(PER)], axis=1
        )
        turned = dot(grad, down)
        lanes = lax.broadcasted_iota(jnp.int32, (group, LANES), 1)
        grad_gate = jnp.zeros((group, LANES), F32)
        out = None
        for j in range(PER):
            expert = step * PER + j
            back = turned[:, j * ff : (j + 1) * ff]
            both = gu_ref[j].astype(F32)
            gate_pre, up_pre = both[:, :ff], both[:, ff:]
            sigma = jax.nn.sigmoid(gate_pre)
            silu = gate_pre * sigma
            act = silu * up_pre
            gate = column(gates, expert)
            grad_gate = jnp.where(
                lanes == expert, jnp.sum(act * back, axis=1, keepdims=True), grad_gate
            )
            grad_act = gate * back
            grad_pre = grad_act * up_pre * sigma * (1.0 + gate_pre * (1.0 - sigma))
            grad_up = grad_act * silu
            grad_both = jnp.concatenate([grad_pre.astype(BF), grad_up.astype(BF)], axis=1)
            dgu_ref[j] = grad_both
            ga_ref[:, j * ff : (j + 1) * ff] = (gate * act).astype(BF)
            gate_up = jnp.concatenate(
                [w_ref[:, 0, j].reshape(width, ff), w_ref[:, 1, j].reshape(width, ff)], axis=1
            )
            part = dot_nt(grad_both, gate_up)
            out = part if out is None else out + part

        @pl.when(step == 0)
        def _():
            total[...] = out
            total_gate[...] = grad_gate

        @pl.when(step > 0)
        def _():
            total[...] += out
            total_gate[...] += grad_gate

        @pl.when(step == pl.num_programs(0) - 1)
        def _():
            rows = group // 4
            for shift in range(4):
                place = own_rows(lax.rem(sref[0] + shift, 4), rows)
                pieces[shift][:, :width] = total[place, :].astype(BF)
                pieces[shift][:, width:] = total_gate[place, :].astype(BF)


def experts_backward(scalars, given, gates, gu, w, after):
    dp, _, experts, dr, ff = w.shape
    group = gates.shape[0]
    width = dp * dr
    piece = (group // 4, width + LANES)
    return pl.pallas_call(
        lambda *refs: experts_backward_kernel(len(after), *refs),
        grid_spec=pltpu.PrefetchScalarGridSpec(
            num_scalar_prefetch=1,
            grid=(experts // PER,),
            in_specs=anywhere(len(after))
            + [whole(x.shape) for x in given]
            + [
                whole((group, experts)),
                pl.BlockSpec((PER, group, 2 * ff), lambda i, s: (i * s[1], 0, 0)),
                pl.BlockSpec((dp, 3, PER, dr, ff), lambda i, s: (0, 0, i * s[1], 0, 0)),
            ],
            out_specs=[whole(piece)] * 4
            + [
                whole((group, width)),
                pl.BlockSpec((PER, group, 2 * ff), lambda i, s: (i * s[1], 0, 0)),
                pl.BlockSpec((group, PER * ff), lambda i, s: (0, i * s[1])),
            ],
            scratch_shapes=[pltpu.VMEM((group, width), F32), pltpu.VMEM((group, LANES), F32)],
        ),
        out_shape=[jax.ShapeDtypeStruct(piece, BF)] * 4
        + [
            jax.ShapeDtypeStruct((group, width), BF),
            jax.ShapeDtypeStruct((experts, group, 2 * ff), BF),
            jax.ShapeDtypeStruct((group, experts * ff), BF),
        ],
        compiler_params=params(),
        cost_estimate=pl.CostEstimate(
            flops=2 * group * width * ff * 3 * experts,
            bytes_accessed=w.size * 2 + 5 * experts * group * ff * 2,
            transcendentals=experts * group * ff,
        ),
        name="experts_backward",
    )(scalars, *after, *given, gates, gu, w)


def middle_kernel(n_after, sref, *refs):
    refs = refs[n_after:]
    pieces, refs = refs[:4], refs[4:]
    grad_ref, hown_ref, gates_ref, b_ref, gains_ref, router_ref, dh_ref, do_ref, small_ref = refs
    rows, width = grad_ref.shape

    @pl.when(sref[1] > 0)
    def _():
        place = own_rows(sref[0], rows)
        joined = pieces[0][...].astype(F32)
        for shift in range(1, 4):
            joined = joined + pieces[shift][...].astype(F32)
        grad_normed = joined[:, :width]
        grad_gate = joined[:, width : width + E]
        gates = gates_ref[place, :]
        grad_logits = (
            gates * (grad_gate - jnp.sum(gates * grad_gate, axis=1, keepdims=True))
        ).astype(BF)
        normed = b_ref[place, :]
        grad_normed = grad_normed + dot_nt(grad_logits, router_ref[:, :E])
        hidden = hown_ref[...]
        part, grad_gain = norm_back(hidden, rms_scale(hidden), gains_ref[1:2, :], grad_normed)
        grad_hidden = grad_ref[...].astype(F32) + part
        dh_ref[...] = grad_hidden
        do_ref[...] = grad_hidden.astype(BF)
        small_ref[0:E, :] = dot_tn(grad_logits, normed)
        small_ref[E : E + 1, :] = grad_gain
        small_ref[E + 1 :, :] = jnp.zeros((small_ref.shape[0] - E - 1, width), F32)


def middle(scalars, pieces, grad_own, hown, gates, b, gains, router, after):
    rows, width = grad_own.shape
    operands = [*pieces, grad_own, hown, gates, b, gains, router]
    return pl.pallas_call(
        lambda *refs: middle_kernel(len(after), *refs),
        grid_spec=pltpu.PrefetchScalarGridSpec(
            num_scalar_prefetch=1,
            grid=(1,),
            in_specs=anywhere(len(after)) + [whole(x.shape) for x in operands],
            out_specs=[whole((rows, width)), whole((rows, width)), whole((24, width))],
        ),
        out_shape=[
            jax.ShapeDtypeStruct((rows, width), F32),
            jax.ShapeDtypeStruct((rows, width), BF),
            jax.ShapeDtypeStruct((24, width), F32),
        ],
        compiler_params=params(),
        cost_estimate=pl.CostEstimate(
            flops=rows * width * 64, bytes_accessed=rows * width * 24, transcendentals=rows
        ),
        name="norm_backward",
    )(scalars, *after, *operands)


def attention_backward_kernel(n_after, sref, *refs):
    pieces, refs = refs[:4], refs[4:]
    sources, refs = refs[:9], refs[9 + n_after :]
    (
        dh_ref, xown_ref, small_ref, gains_ref, cos_ref, sin_ref, bias_ref, qkv_ref, lse_ref,
        dx_ref, dxlow_ref, small_out_ref, full_ref, dqkv_ref,
        total, now, buffers, sems,
    ) = refs
    step = pl.program_id(0)
    me = sref[0]
    shard = dh_ref.shape[0]

    @pl.when(sref[1] > 0)
    def _():
        copies = fetches(sref[2], sources, buffers, sems)

        @pl.when(step == 0)
        def _():
            for part in copies:
                for copy in part:
                    copy.start()
            assemble(me, pieces, full_ref)
            total[...] = jnp.zeros_like(total)

        for shift, part in enumerate(copies):

            @pl.when(step == shift)
            def _(part=part):
                for copy in part:
                    copy.wait()

        w_qkv, w_out = group_weights(buffers, step)
        do = dot(full_ref[...], w_out).astype(BF)
        qkv = qkv_ref[0]
        q, k, v = qkv[:, :256], qkv[:, 256:384], qkv[:, 384:]
        q_turned = q.T
        do_turned = do.T
        bias = bias_ref[...]
        lse = lse_ref[0]
        dq, dk, dv = [], [], []
        for kv in range(2):
            k_one = k[:, kv * HD : (kv + 1) * HD]
            v_one = v[:, kv * HD : (kv + 1) * HD]
            dk_one = dv_one = None
            for head in (2 * kv, 2 * kv + 1):
                part = slice(head * HD, (head + 1) * HD)
                scores = dot_nt(q[:, part], k_one) + bias
                soft = jnp.exp(scores - lse[:, head : head + 1])
                grad_soft = dot_nt(do[:, part], v_one)
                grad_scores = soft * (
                    grad_soft - jnp.sum(soft * grad_soft, axis=1, keepdims=True)
                )
                grad_scores = grad_scores.astype(BF)
                dq.append(dot(grad_scores, k_one))
                dk_part = dot(q_turned[part, :], grad_scores)
                dv_part = dot(do_turned[part, :], soft.astype(BF))
                dk_one = dk_part if dk_one is None else dk_one + dk_part
                dv_one = dv_part if dv_one is None else dv_one + dv_part
            dk.append(dk_one)
            dv.append(dv_one)
        grad_k = jnp.concatenate(dk, axis=0).T
        grad_v = jnp.concatenate(dv, axis=0).T
        grad_qk = jnp.concatenate([jnp.concatenate(dq, axis=1) * HD**-0.5, grad_k], axis=1)
        cos = jnp.concatenate([cos_ref[...]] * 3, axis=1)
        sin = jnp.concatenate([sin_ref[...]] * 3, axis=1)
        grad_qk = (grad_qk * cos - swap_halves(grad_qk) * sin).astype(BF)
        now[:, :384] = grad_qk
        now[:, 384:] = grad_v.astype(BF)

        @pl.when(step == 0)
        def _():
            dqkv_ref[...] = now[...]

        total[...] += dot_nt(now[own_rows(me, shard), :], w_qkv)

        @pl.when(step == pl.num_programs(0) - 1)
        def _():
            entering = xown_ref[...].astype(F32)
            part, grad_gain = norm_back(
                entering, rms_scale(entering), gains_ref[0:1, :], total[...]
            )
            grad_entering = dh_ref[...] + part
            dx_ref[...] = grad_entering
            dxlow_ref[...] = grad_entering.astype(BF)
            rows = lax.broadcasted_iota(jnp.int32, small_ref.shape, 0)
            small_out_ref[...] = jnp.where(rows == E + 1, grad_gain, small_ref[...])


def attention_backward(
    scalars, pieces, dh, xown, small, gains, tables, qkv, lse, w_attn, after
):
    shard, width = dh.shape
    group = 4 * shard
    dp = width // 64
    cos, sin, bias = tables
    smalls = [dh, xown, small, gains, cos, sin, bias]
    per_step = lambda i, s: (i * s[1], 0, 0)
    outs = [
        ((shard, width), F32),
        ((shard, width), BF),
        (small.shape, F32),
        ((group, width), BF),
        ((group, 512), BF),
    ]
    return pl.pallas_call(
        lambda *refs: attention_backward_kernel(len(after), *refs),
        grid_spec=pltpu.PrefetchScalarGridSpec(
            num_scalar_prefetch=1,
            grid=(4,),
            in_specs=[whole(x.shape) for x in pieces]
            + anywhere(9 + len(after))
            + [whole(x.shape) for x in smalls]
            + [
                pl.BlockSpec((1, group, 512), per_step),
                pl.BlockSpec((1, group, LANES), per_step),
            ],
            out_specs=[whole(shape) for shape, _ in outs],
            scratch_shapes=[
                pltpu.VMEM((shard, width), F32),
                pltpu.VMEM((group, 512), BF),
                pltpu.VMEM((4, dp, 400, LANES), BF),
                pltpu.SemaphoreType.DMA((9,)),
            ],
        ),
        out_shape=[jax.ShapeDtypeStruct(shape, kind) for shape, kind in outs],
        compiler_params=params(),
        cost_estimate=pl.CostEstimate(
            flops=group * width * 1024 * 2 + 16 * 10 * group * group * HD,
            bytes_accessed=width * 768 * 8 + 6 * group * width * 2,
            transcendentals=16 * group * group,
        ),
        name="attention_backward",
    )(scalars, *pieces, *w_attn, *after, *smalls, qkv, lse)


def expert_weights_kernel(n_after, sref, *refs):
    refs = refs[n_after:]
    b, refs = refs[:4], refs[4:]
    g, refs = refs[:4], refs[4:]
    dgu, refs = refs[:4], refs[4:]
    ga, refs = refs[:4], refs[4:]
    out_ref, bt_ref, gt_ref = refs
    group = b[0].shape[0]
    dp, _, _, dr, ff = out_ref.shape
    first = sref[1] > 0

    def chosen(four, micro, *index):
        index = index or (Ellipsis,)
        return jnp.where(first, four[micro][index], four[2 + micro][index])

    @pl.when(pl.program_id(0) == 0)
    def _():
        for micro in range(2):
            place = slice(micro * group, (micro + 1) * group)
            bt_ref[:, place] = chosen(b, micro).T
            gt_ref[:, place] = chosen(g, micro).T

    bt = bt_ref[...]
    for j in range(PER):
        rows = jnp.concatenate([chosen(dgu, 0, j), chosen(dgu, 1, j)], axis=0)
        grads = dot(bt, rows).astype(BF)
        out_ref[:, 0, j] = grads[:, :ff].reshape(dp, dr, ff)
        out_ref[:, 1, j] = grads[:, ff:].reshape(dp, dr, ff)
    rows = jnp.concatenate([chosen(ga, 0), chosen(ga, 1)], axis=0)
    grads = dot(gt_ref[...], rows).astype(BF)
    for j in range(PER):
        out_ref[:, 2, j] = grads[:, j * ff : (j + 1) * ff].reshape(dp, dr, ff)


def expert_weights(scalars, rows_b, grads, dgus, gas, dp, after):
    group, width = rows_b[0].shape
    experts, _, ff2 = dgus[0].shape
    ff = ff2 // 2
    dr = width // dp
    square = whole((group, width))
    wide, flat = [], []
    for held in (lambda s: s[1], lambda s: 1 - s[1]):
        wide += [
            pl.BlockSpec((PER, group, ff2), lambda i, s, held=held: (i * held(s), 0, 0))
        ] * 2
        flat += [pl.BlockSpec((group, PER * ff), lambda i, s, held=held: (0, i * held(s)))] * 2
    return pl.pallas_call(
        lambda *refs: expert_weights_kernel(len(after), *refs),
        grid_spec=pltpu.PrefetchScalarGridSpec(
            num_scalar_prefetch=1,
            grid=(experts // PER,),
            in_specs=anywhere(len(after)) + [square] * 8 + wide + flat,
            out_specs=pl.BlockSpec((dp, 3, PER, dr, ff), lambda i, s: (0, 0, i, 0, 0)),
            scratch_shapes=[
                pltpu.VMEM((width, 2 * group), BF),
                pltpu.VMEM((width, 2 * group), BF),
            ],
        ),
        out_shape=jax.ShapeDtypeStruct((dp, 3, experts, dr, ff), BF),
        compiler_params=params(),
        cost_estimate=pl.CostEstimate(
            flops=4 * group * width * ff * 3 * experts,
            bytes_accessed=dp * 3 * experts * dr * ff * 2 + 6 * experts * group * ff * 2,
            transcendentals=0,
        ),
        name="expert_weight_grads",
    )(scalars, *after, *rows_b, *grads, *dgus, *gas)


def attention_weights_kernel(sref, *refs):
    a, o, f, d, small = (refs[4 * j : 4 * j + 4] for j in range(5))
    out_ref = refs[20]
    dp = out_ref.shape[0]
    first = sref[1] > 0

    def chosen(four, micro):
        return jnp.where(first, four[micro][...], four[2 + micro][...])

    sums = dot_tn(chosen(a, 0), chosen(d, 0)) + dot_tn(chosen(a, 1), chosen(d, 1))
    for j in range(4):
        out_ref[:, 64 * j : 64 * (j + 1), :] = (
            sums[:, LANES * j : LANES * (j + 1)].astype(BF).reshape(dp, 64, LANES)
        )
    sums = dot_tn(chosen(f, 0), chosen(o, 0)) + dot_tn(chosen(f, 1), chosen(o, 1))
    for j in range(2):
        out_ref[:, 64 * (4 + j) : 64 * (5 + j), :] = (
            sums[:, LANES * j : LANES * (j + 1)].astype(BF).reshape(dp, 64, LANES)
        )
    rows = chosen(small, 0) + chosen(small, 1)
    rows = jnp.concatenate(
        [rows, jnp.zeros((LANES - rows.shape[0], rows.shape[1]), F32)], axis=0
    )
    out_ref[:, 384:, :] = rows.T.astype(BF).reshape(dp, 64, LANES)


def attention_weights(scalars, a, o, f, d, small, dp):
    group, width = a[0].shape
    operands = [*a, *o, *f, *d, *small]
    return pl.pallas_call(
        attention_weights_kernel,
        grid_spec=pltpu.PrefetchScalarGridSpec(
            num_scalar_prefetch=1,
            grid=(1,),
            in_specs=[whole(x.shape) for x in operands],
            out_specs=whole((dp, 448, LANES)),
        ),
        out_shape=jax.ShapeDtypeStruct((dp, 448, LANES), BF),
        compiler_params=params(),
        cost_estimate=pl.CostEstimate(
            flops=4 * group * width * 768,
            bytes_accessed=group * width * 14 + width * 768 * 2,
            transcendentals=0,
        ),
        name="attention_weight_grads",
    )(scalars, *operands)


def moved(array, shift):
    return lax.ppermute(array, "tensor", [(i, (i + shift) % 4) for i in range(4)])


def swapped(array, dp):
    return lax.ppermute(array, "dp", [(i, i ^ 1) for i in range(dp)])


def to_owner(pieces):
    return [pieces[0]] + [moved(pieces[s], s) for s in range(1, 4)]


def to_all(rows):
    return [rows] + [moved(rows, s) for s in range(1, 4)]


def across(rows, up):
    start, end = (0, 4) if up else (4, 0)
    return [
        lax.ppermute(
            rows, ("pipe", "tensor"), [(start + i, end + (i + s) % 4) for i in range(4)]
        )
        for s in range(4)
    ]


def tables_of(lengths, group):
    ends = jnp.cumsum(lengths)
    starts = ends - lengths
    index = jnp.arange(group, dtype=jnp.int32)
    inside = index[:, None] >= starts[None, :]
    start = jnp.max(jnp.where(inside, starts[None, :], 0), axis=1)
    position = (index - start).astype(F32)
    half = HD // 2
    freq = jnp.exp(jnp.arange(half, dtype=F32) * (-2.0 * math.log(10000.0) / HD))
    angle = position[:, None] * freq[None, :]
    cos, sin = jnp.cos(angle), jnp.sin(angle)
    visible = (index[None, :] <= index[:, None]) & (index[None, :] >= start[:, None])
    bias = jnp.where(visible, 0.0, MASKED).astype(F32)
    return (
        jnp.concatenate([cos, cos, cos, cos], axis=1),
        jnp.concatenate([-sin, sin, -sin, sin], axis=1),
        bias,
    )


def per_device(
    inputs, cotangent, doc_lengths, routes, norm_attn, w_query, w_key, w_value, w_out,
    w_router, norm_ffn, w_gate, w_up, w_down,
):
    section = lax.axis_index("pipe")
    first_section = section == 0
    me = lax.axis_index("tensor")
    dp = lax.axis_size("dp")
    core = lax.axis_index("dp") % 2
    micro = inputs.shape[0]
    shard, width = inputs.shape[1:]
    group = shard * 4
    rows_dp = width // dp
    scalars = [
        jnp.stack([me, (section == s).astype(jnp.int32), core]).astype(jnp.int32)
        for s in range(2)
    ]

    out_turned = w_out[0].T
    small = jnp.concatenate([w_router[0], norm_attn[0][:, None], norm_ffn[0][:, None]], axis=1)
    small = jnp.pad(small, ((0, 0), (0, LANES - E - 2)))
    piece = jnp.concatenate(
        [
            w_query[0][:, :LANES], w_query[0][:, LANES:], w_key[0], w_value[0],
            out_turned[:, :LANES], out_turned[:, LANES:], small,
        ],
        axis=0,
    )
    w_own = jnp.broadcast_to(piece[None], (dp,) + piece.shape)
    w_own = lax.all_to_all(w_own, "dp", 0, 0, tiled=True)
    pieces_w = jnp.stack([w_gate[0], w_up[0], w_down[0].transpose(0, 2, 1)])
    w_experts = lax.all_gather(pieces_w, "dp", axis=0)
    rows_in, rows_cot = to_all(inputs), to_all(cotangent)
    rows_in, rows_cot, w_own = lax.optimization_barrier((rows_in, rows_cot, w_own))
    half, quarter = dp // 2, dp // 4
    mine = lax.dynamic_slice_in_dim(w_own, core * half, half, 0)
    w_next, w_last = moved(mine, 1), moved(mine, 3)
    w_over = [moved(w_next[:quarter], 1), moved(w_last[quarter:], 3)]
    other = [swapped(x, dp) for x in (w_next, w_last, *w_over)]
    w_attn = [w_own, w_next, other[0], *w_over, other[2], other[3], w_last, other[1]]
    router, gains = smalls_of(scalars[0], w_attn)

    rows_in = [[part[m] for part in rows_in] for m in range(micro)]
    rows_cot = [[part[m] for part in rows_cot] for m in range(micro)]
    tables = [tables_of(doc_lengths[m, 0], group) for m in range(micro)]
    ids = jnp.arange(E, dtype=jnp.int32)
    picked = jnp.any(routes[0][..., None] == ids, axis=2).astype(F32)

    after = []
    saves = [[None] * micro, [None] * micro]
    firsts = [[None] * micro, [None] * micro]
    middles = [[None] * micro, [None] * micro]
    lasts = [[None] * micro, [None] * micro]

    def attend(s, m, pieces):
        nonlocal after
        out = attention_forward(
            scalars[s], pieces, gains, tables[m], picked[m], w_attn, router, after
        )
        saves[s][m] = list(out)
        after = [out[6]]

    def expert(s, m):
        nonlocal after
        b, gates = saves[s][m][6:8]
        *parts, gu = experts_forward(scalars[s], b, gates, w_experts, after)
        saves[s][m].append(gu)
        after = [gu]
        return parts

    def expert_back(s, m, pieces):
        nonlocal after
        gates, gu = saves[s][m][7:9]
        *parts, grad, dgu, ga = experts_backward(
            scalars[s], pieces, gates, gu, w_experts, after
        )
        after = [grad]
        firsts[s][m] = (to_owner(parts), grad, dgu, ga)

    def norm_between(s, m, own):
        nonlocal after
        kept = saves[s][m]
        dh, do, small = middle(
            scalars[s], firsts[s][m][0], own, kept[5], kept[7], kept[6], gains, router, after
        )
        middles[s][m] = (dh, to_all(do), small)
        after = [do]

    def attend_back(s, m):
        nonlocal after
        kept = saves[s][m]
        dh, rows, small = middles[s][m]
        dx, dx_low, small, full, dqkv = attention_backward(
            scalars[s], rows, dh, kept[1], small, gains, tables[m], kept[2], kept[4],
            w_attn, after,
        )
        lasts[s][m] = (small, full, dqkv, dx)
        after = [dx]
        return dx_low

    def layer_sum(parts, hown):
        return finish(to_owner(parts), hown)

    attend(0, 0, rows_in[0])
    first_out = layer_sum(expert(0, 0), saves[0][0][5])
    first_in = across(first_out, True)
    after = [first_out]
    attend(0, 1, rows_in[1])
    attend(1, 0, first_in)
    second_out = layer_sum(expert(0, 1), saves[0][1][5])
    second_in = across(second_out, True)
    late = [expert(1, 0)]
    expert_back(1, 0, rows_cot[0])
    attend(1, 1, second_in)
    late.append(expert(1, 1))
    norm_between(1, 0, cotangent[0])
    expert_back(1, 1, rows_cot[1])
    first_back = across(attend_back(1, 0), False)
    norm_between(1, 1, cotangent[1])
    second_back = across(attend_back(1, 1), False)
    expert_back(0, 0, first_back)
    norm_between(0, 0, first_back[0])
    expert_back(0, 1, second_back)
    joined = firsts[0] + firsts[1]
    grad_experts = expert_weights(
        scalars[0],
        [saves[s][m][6] for s in range(2) for m in range(micro)],
        [x[1] for x in joined],
        [x[2] for x in joined],
        [x[3] for x in joined],
        dp,
        after,
    )
    expert_sums = lax.psum_scatter(grad_experts, "dp", scatter_dimension=0, tiled=True)[0]
    after = [grad_experts]
    norm_between(0, 1, second_back[0])
    attend_back(0, 0)
    attend_back(0, 1)
    late, _ = lax.optimization_barrier((late, lasts[1][1][3]))
    outputs = [
        [first_out, second_out],
        [layer_sum(late[m], saves[1][m][5]) for m in range(micro)],
    ]
    grads_in = [[lasts[s][m][3] for m in range(micro)] for s in range(2)]

    joined = lasts[0] + lasts[1]
    grad_attn = attention_weights(
        scalars[0],
        [saves[s][m][0] for s in range(2) for m in range(micro)],
        [saves[s][m][3] for s in range(2) for m in range(micro)],
        [x[1] for x in joined],
        [x[2] for x in joined],
        [x[0] for x in joined],
        dp,
    )
    grad_attn = lax.all_to_all(grad_attn, "dp", 0, 0, tiled=True)
    attn_sums = jnp.sum(grad_attn.astype(F32), axis=0)
    small = attn_sums[384:].reshape(4, 16, LANES)
    small_own = None
    for shift in range(4):
        part = lax.dynamic_index_in_dim(small, (me + shift) % 4, 0, keepdims=False)
        part = moved(part, shift) if shift else part
        small_own = part if small_own is None else small_own + part
    expert_sums = expert_sums.astype(F32)
    blocks = [attn_sums[64 * j : 64 * (j + 1)] for j in range(6)]
    section_rows = jnp.stack(
        [jnp.where(first_section, outputs[0][m], outputs[1][m]) for m in range(micro)]
    )
    grad_in = jnp.stack(
        [jnp.where(first_section, grads_in[0][m], grads_in[1][m]) for m in range(micro)]
    )
    return (
        section_rows[None],
        grad_in[None],
        small_own[:, E + 1][None],
        jnp.concatenate(blocks[:2], axis=1)[None],
        blocks[2][None],
        blocks[3][None],
        jnp.concatenate(blocks[4:], axis=1).T[None],
        small_own[:, :E][None],
        small_own[:, E][None],
        expert_sums[0][None],
        expert_sums[1][None],
        expert_sums[2].transpose(0, 2, 1)[None],
    )


def finish(parts, hown):
    result = hown
    for part in parts:
        result = result + part.astype(F32)
    return result.astype(BF)


def solution(mesh):
    in_specs = (
        P(None, ("dp", "tensor"), None),
        P(None, ("dp", "tensor"), None),
        P(None, "dp", None),
        P("pipe", None, "dp", None),
        P("pipe", ("dp", "tensor")),
        P("pipe", "dp", "tensor"),
        P("pipe", "dp", "tensor"),
        P("pipe", "dp", "tensor"),
        P("pipe", "tensor", "dp"),
        P("pipe", ("dp", "tensor"), None),
        P("pipe", ("dp", "tensor")),
        P("pipe", None, "dp", "tensor"),
        P("pipe", None, "dp", "tensor"),
        P("pipe", None, "tensor", "dp"),
    )
    out_specs = (
        P("pipe", None, ("dp", "tensor"), None),
        P("pipe", None, ("dp", "tensor"), None),
        P("pipe", ("dp", "tensor")),
        P("pipe", "dp", "tensor"),
        P("pipe", "dp", "tensor"),
        P("pipe", "dp", "tensor"),
        P("pipe", "tensor", "dp"),
        P("pipe", ("dp", "tensor"), None),
        P("pipe", ("dp", "tensor")),
        P("pipe", None, "dp", "tensor"),
        P("pipe", None, "dp", "tensor"),
        P("pipe", None, "tensor", "dp"),
    )
    return jax.shard_map(
        per_device, mesh=mesh, in_specs=in_specs, out_specs=out_specs, check_vma=False
    )
```

```python
import math

import jax
import jax.numpy as jnp
from jax import lax
from jax.experimental import pallas as pl
from jax.experimental.pallas import tpu as pltpu
from jax.sharding import PartitionSpec as P

HD = 64
E = 16
TOP = 8
EPSILON = 1e-06
MASKED = -1000000000.0
BF = jnp.bfloat16
F32 = jnp.float32
VMEM_LIMIT = 56 * 1024 * 1024
PER = 8
PER_GRAD = 4
LANES = 128


def params():
    return pltpu.CompilerParams(
        vmem_limit_bytes=VMEM_LIMIT, dimension_semantics=("arbitrary",)
    )


def dot(left, right):
    return jnp.dot(left, right, preferred_element_type=F32)


def dot_nt(left, right):
    return lax.dot_general(
        left, right, (((1,), (1,)), ((), ())), preferred_element_type=F32
    )


def dot_tn(left, right):
    return lax.dot_general(
        left, right, (((0,), (0,)), ((), ())), preferred_element_type=F32
    )


def column(rows, index):
    lanes = lax.broadcasted_iota(jnp.int32, rows.shape, 1)
    return jnp.sum(jnp.where(lanes == index, rows, 0.0), axis=1, keepdims=True)


def whole(shape):
    return pl.BlockSpec(shape, lambda i, s: (0,) * len(shape))


def rms_scale(values):
    return lax.rsqrt(jnp.mean(values * values, axis=-1, keepdims=True) + EPSILON)


def norm_back(values, scale_rows, gain, grad_normed):
    weighted = grad_normed * gain
    grad_values = scale_rows * weighted - values * scale_rows**3 * jnp.mean(
        weighted * values, axis=-1, keepdims=True
    )
    grad_gain = jnp.sum(grad_normed * values * scale_rows, axis=0, keepdims=True)
    return grad_values, grad_gain


def swap_halves(values):
    width = values.shape[1]
    lanes = lax.broadcasted_iota(jnp.int32, values.shape, 1)
    ahead = pltpu.roll(values, width - HD // 2, 1)
    behind = pltpu.roll(values, HD // 2, 1)
    return jnp.where(lanes % HD < HD // 2, ahead, behind)


def assemble(me, pieces, target):
    rows = pieces[0].shape[0]
    for shift in range(4):
        owner = lax.rem(me + 4 - shift, 4)
        target[own_rows(owner, rows), :] = pieces[shift][...]


def own_rows(me, rows):
    return pl.ds(pl.multiple_of(me * rows, rows), rows)


def anywhere(count):
    return [pl.BlockSpec(memory_space=pl.ANY)] * count


def fetches(core, sources, buffers, sems):
    dp = buffers.shape[1]
    half, quarter = dp // 2, dp // 4
    here, there = core * half, (1 - core) * half
    copies = [[pltpu.make_async_copy(sources[0], buffers.at[0], sems.at[0])]]
    number = 1
    for shift, starts in (
        (1, (here, there)),
        (2, (here, here + quarter, there, there + quarter)),
        (3, (here, there)),
    ):
        group = []
        for start in starts:
            source = sources[number]
            place = buffers.at[shift, pl.ds(start, source.shape[0])]
            group.append(pltpu.make_async_copy(source, place, sems.at[number]))
            number += 1
        copies.append(group)
    return copies


def group_weights(buffers, step):
    dp = buffers.shape[1]
    blocks = [
        buffers[step, :, 64 * j : 64 * (j + 1), :].reshape(dp * 64, LANES) for j in range(6)
    ]
    return jnp.concatenate(blocks[:4], axis=1), jnp.concatenate(blocks[4:], axis=1)


def smalls_kernel(sref, *refs):
    sources, (router_ref, gains_ref, stage, sems) = refs[:9], refs[9:]
    dp = stage.shape[0]
    half, quarter = dp // 2, dp // 4
    me = sref[0]
    here, there = sref[2] * half, (1 - sref[2]) * half
    places = (
        (0, 0), (1, here), (1, there),
        (2, here), (2, here + quarter), (2, there), (2, there + quarter), (3, here), (3, there),
    )
    copies = []
    for number, (shift, start) in enumerate(places):
        source = sources[number]
        owner = lax.rem(me + 4 - shift, 4)
        copies.append(
            pltpu.make_async_copy(
                source.at[:, pl.ds(384, 16)],
                stage.at[pl.ds(start, source.shape[0]), owner],
                sems.at[number],
            )
        )
    for copy in copies:
        copy.start()
    for copy in copies:
        copy.wait()
    rows = stage[...].reshape(dp * 64, LANES)
    router_ref[...] = rows
    turned = rows.astype(F32).T
    gains_ref[...] = turned[E : E + 8, :]


def smalls_of(scalars, w_attn):
    dp = w_attn[0].shape[0]
    width = dp * 64
    return pl.pallas_call(
        smalls_kernel,
        grid_spec=pltpu.PrefetchScalarGridSpec(
            num_scalar_prefetch=1,
            grid=(1,),
            in_specs=anywhere(9),
            out_specs=[whole((width, LANES)), whole((8, width))],
            scratch_shapes=[pltpu.VMEM((dp, 4, 16, LANES), BF), pltpu.SemaphoreType.DMA((9,))],
        ),
        out_shape=[
            jax.ShapeDtypeStruct((width, LANES), BF),
            jax.ShapeDtypeStruct((8, width), F32),
        ],
        compiler_params=params(),
        name="router_and_gains",
    )(scalars, *w_attn)


def attention_forward_kernel(n_after, sref, *refs):
    pieces, refs = refs[:4], refs[4:]
    sources, refs = refs[:9], refs[9 + n_after :]
    (
        gains_ref, cos_ref, sin_ref, bias_ref, picked_ref, router_ref,
        a_ref, xown_ref, qkv_ref, o_ref, lse_ref, hown_ref, b_ref, gates_ref,
        hidden, buffers, sems,
    ) = refs
    me = sref[0]
    group, width = b_ref.shape
    shard = xown_ref.shape[0]

    @pl.when(sref[1] > 0)
    def _():
        copies = fetches(sref[2], sources, buffers, sems)
        for copy in copies[0]:
            copy.start()
        assemble(me, pieces, b_ref)
        entering = b_ref[...].astype(F32)
        a_ref[...] = (entering * rms_scale(entering) * gains_ref[0:1, :]).astype(BF)
        xown_ref[...] = pieces[0][...]
        hidden[...] = entering
        cos = jnp.concatenate([cos_ref[...]] * 3, axis=1)
        sin = jnp.concatenate([sin_ref[...]] * 3, axis=1)
        bias = bias_ref[...]
        lanes = lax.broadcasted_iota(jnp.int32, (group, LANES), 1)
        lse_all = jnp.zeros((group, LANES), F32)
        for step in range(4):
            for copy in copies[step]:
                copy.wait()
            for copy in copies[step + 1] if step < 3 else []:
                copy.start()
            w_qkv, w_out = group_weights(buffers, step)
            qkv = dot(a_ref[...], w_qkv)
            qk = qkv[:, :384]
            turned = qk * cos + swap_halves(qk) * sin
            q = (turned[:, :256] * HD**-0.5).astype(BF)
            k = turned[:, 256:].astype(BF)
            v = qkv[:, 384:].astype(BF)
            qkv_ref[step, :, :256] = q
            qkv_ref[step, :, 256:384] = k
            qkv_ref[step, :, 384:] = v
            outs = []
            for head in range(4):
                kv = head // 2
                scores = dot_nt(
                    q[:, head * HD : (head + 1) * HD], k[:, kv * HD : (kv + 1) * HD]
                )
                scores = scores + bias
                peak = jnp.max(scores, axis=1, keepdims=True)
                soft = jnp.exp(scores - peak)
                total = jnp.sum(soft, axis=1, keepdims=True)
                lse_all = jnp.where(lanes == 4 * step + head, peak + jnp.log(total), lse_all)
                soft = (soft * (1.0 / total)).astype(BF)
                outs.append(dot(soft, v[:, kv * HD : (kv + 1) * HD]))
            mixed = jnp.concatenate(outs, axis=1).astype(BF)
            if step == 0:
                o_ref[...] = mixed
            hidden[...] += dot_nt(mixed, w_out)
        lse_ref[...] = lse_all
        rows = hidden[...]
        normed = (rows * rms_scale(rows) * gains_ref[1:2, :]).astype(BF)
        b_ref[...] = normed
        hown_ref[...] = hidden[own_rows(me, shard), :]
        logits = dot(normed, router_ref[...])[:, :E]
        picked = picked_ref[...]
        peak = jnp.max(jnp.where(picked > 0, logits, -1e30), axis=1, keepdims=True)
        powers = jnp.where(picked > 0, jnp.exp(jnp.minimum(logits - peak, 0.0)), 0.0)
        gates_ref[...] = powers / jnp.sum(powers, axis=1, keepdims=True)


def attention_forward(scalars, pieces, gains, tables, picked, w_attn, router, after):
    shard, width = pieces[0].shape
    group = 4 * shard
    dp = width // 64
    cos, sin, bias = tables
    smalls = [gains, cos, sin, bias, picked, router]
    per_step = lambda i, s: (i * s[1], 0, 0)
    outs = [
        ((group, width), BF, None),
        ((shard, width), BF, None),
        ((4, group, 512), BF, None),
        ((group, 256), BF, None),
        ((group, LANES), F32, None),
        ((shard, width), F32, None),
        ((group, width), BF, None),
        ((group, E), F32, None),
    ]
    return pl.pallas_call(
        lambda *refs: attention_forward_kernel(len(after), *refs),
        grid_spec=pltpu.PrefetchScalarGridSpec(
            num_scalar_prefetch=1,
            grid=(1,),
            in_specs=[whole(x.shape) for x in pieces]
            + anywhere(9 + len(after))
            + [whole(x.shape) for x in smalls],
            out_specs=[
                whole(shape) if block is None else pl.BlockSpec(block, per_step)
                for shape, _, block in outs
            ],
            scratch_shapes=[
                pltpu.VMEM((group, width), F32),
                pltpu.VMEM((4, dp, 400, LANES), BF),
                pltpu.SemaphoreType.DMA((9,)),
            ],
        ),
        out_shape=[jax.ShapeDtypeStruct(shape, kind) for shape, kind, _ in outs],
        compiler_params=params(),
        cost_estimate=pl.CostEstimate(
            flops=2 * group * width * 768 * 4 + 16 * 4 * group * group * HD,
            bytes_accessed=width * 768 * 8 + 6 * group * width * 2,
            transcendentals=16 * group * group,
        ),
        name="attention_forward",
    )(scalars, *pieces, *w_attn, *after, *smalls)


def experts_forward_kernel(n_after, sref, *refs):
    (b_ref, gate_ref, w_ref, *refs) = refs[n_after:]
    pieces, (gu_ref, total) = refs[:4], refs[4:]
    step = pl.program_id(0)
    width = b_ref.shape[1]
    ff = w_ref.shape[-1]

    @pl.when(sref[1] > 0)
    def _():
        b = b_ref[...]
        gates = gate_ref[...]
        acts, downs = [], []
        for j in range(PER):
            gate_up = jnp.concatenate(
                [w_ref[:, 0, j].reshape(width, ff), w_ref[:, 1, j].reshape(width, ff)], axis=1
            )
            both = dot(b, gate_up)
            gu_ref[j] = both.astype(BF)
            gate_pre, up_pre = both[:, :ff], both[:, ff:]
            act = gate_pre * jax.nn.sigmoid(gate_pre) * up_pre
            acts.append((act * column(gates, step * PER + j)).astype(BF))
            downs.append(w_ref[:, 2, j].reshape(width, ff))
        out = dot_nt(jnp.concatenate(acts, axis=1), jnp.concatenate(downs, axis=1))

        @pl.when(step == 0)
        def _():
            total[...] = out

        @pl.when(step > 0)
        def _():
            total[...] += out

        @pl.when(step == pl.num_programs(0) - 1)
        def _():
            rows = b_ref.shape[0] // 4
            for shift in range(4):
                place = own_rows(lax.rem(sref[0] + shift, 4), rows)
                pieces[shift][...] = total[place, :].astype(BF)


def experts_forward(scalars, b, gates, w, after):
    group, width = b.shape
    dp, _, experts, dr, ff = w.shape
    piece = (group // 4, width)
    return pl.pallas_call(
        lambda *refs: experts_forward_kernel(len(after), *refs),
        grid_spec=pltpu.PrefetchScalarGridSpec(
            num_scalar_prefetch=1,
            grid=(experts // PER,),
            in_specs=anywhere(len(after))
            + [
                whole((group, width)),
                whole((group, experts)),
                pl.BlockSpec((dp, 3, PER, dr, ff), lambda i, s: (0, 0, i * s[1], 0, 0)),
            ],
            out_specs=[whole(piece)] * 4
            + [pl.BlockSpec((PER, group, 2 * ff), lambda i, s: (i * s[1], 0, 0))],
            scratch_shapes=[pltpu.VMEM((group, width), F32)],
        ),
        out_shape=[jax.ShapeDtypeStruct(piece, BF)] * 4
        + [jax.ShapeDtypeStruct((experts, group, 2 * ff), BF)],
        compiler_params=params(),
        cost_estimate=pl.CostEstimate(
            flops=2 * group * width * ff * 3 * experts,
            bytes_accessed=w.size * 2 + experts * group * 2 * ff * 2,
            transcendentals=experts * group * ff,
        ),
        name="experts_forward",
    )(scalars, *after, b, gates, w)


def experts_backward_kernel(n_after, sref, *refs):
    (*refs,) = refs[n_after:]
    given, refs = refs[:4], refs[4:]
    gate_ref, gu_ref, w_ref, *refs = refs
    pieces, refs = refs[:4], refs[4:]
    grad_ref, dgu_ref, ga_ref, total, total_gate = refs
    step = pl.program_id(0)
    group, width = grad_ref.shape
    ff = w_ref.shape[-1]

    @pl.when(sref[1] > 0)
    def _():
        @pl.when(step == 0)
        def _():
            assemble(sref[0], given, grad_ref)

        grad = grad_ref[...]
        gates = gate_ref[...]
        down = jnp.concatenate(
            [w_ref[:, 2, j].reshape(width, ff) for j in range(PER)], axis=1
        )
        turned = dot(grad, down)
        lanes = lax.broadcasted_iota(jnp.int32, (group, LANES), 1)
        grad_gate = jnp.zeros((group, LANES), F32)
        out = None
        for j in range(PER):
            expert = step * PER + j
            back = turned[:, j * ff : (j + 1) * ff]
            both = gu_ref[j].astype(F32)
            gate_pre, up_pre = both[:, :ff], both[:, ff:]
            sigma = jax.nn.sigmoid(gate_pre)
            silu = gate_pre * sigma
            act = silu * up_pre
            gate = column(gates, expert)
            grad_gate = jnp.where(
                lanes == expert, jnp.sum(act * back, axis=1, keepdims=True), grad_gate
            )
            grad_act = gate * back
            grad_pre = grad_act * up_pre * sigma * (1.0 + gate_pre * (1.0 - sigma))
            grad_up = grad_act * silu
            grad_both = jnp.concatenate([grad_pre.astype(BF), grad_up.astype(BF)], axis=1)
            dgu_ref[j] = grad_both
            ga_ref[:, j * ff : (j + 1) * ff] = (gate * act).astype(BF)
            gate_up = jnp.concatenate(
                [w_ref[:, 0, j].reshape(width, ff), w_ref[:, 1, j].reshape(width, ff)], axis=1
            )
            part = dot_nt(grad_both, gate_up)
            out = part if out is None else out + part

        @pl.when(step == 0)
        def _():
            total[...] = out
            total_gate[...] = grad_gate

        @pl.when(step > 0)
        def _():
            total[...] += out
            total_gate[...] += grad_gate

        @pl.when(step == pl.num_programs(0) - 1)
        def _():
            rows = group // 4
            for shift in range(4):
                place = own_rows(lax.rem(sref[0] + shift, 4), rows)
                pieces[shift][:, :width] = total[place, :].astype(BF)
                pieces[shift][:, width:] = total_gate[place, :].astype(BF)


def experts_backward(scalars, given, gates, gu, w, after):
    dp, _, experts, dr, ff = w.shape
    group = gates.shape[0]
    width = dp * dr
    piece = (group // 4, width + LANES)
    return pl.pallas_call(
        lambda *refs: experts_backward_kernel(len(after), *refs),
        grid_spec=pltpu.PrefetchScalarGridSpec(
            num_scalar_prefetch=1,
            grid=(experts // PER,),
            in_specs=anywhere(len(after))
            + [whole(x.shape) for x in given]
            + [
                whole((group, experts)),
                pl.BlockSpec((PER, group, 2 * ff), lambda i, s: (i * s[1], 0, 0)),
                pl.BlockSpec((dp, 3, PER, dr, ff), lambda i, s: (0, 0, i * s[1], 0, 0)),
            ],
            out_specs=[whole(piece)] * 4
            + [
                whole((group, width)),
                pl.BlockSpec((PER, group, 2 * ff), lambda i, s: (i * s[1], 0, 0)),
                pl.BlockSpec((group, PER * ff), lambda i, s: (0, i * s[1])),
            ],
            scratch_shapes=[pltpu.VMEM((group, width), F32), pltpu.VMEM((group, LANES), F32)],
        ),
        out_shape=[jax.ShapeDtypeStruct(piece, BF)] * 4
        + [
            jax.ShapeDtypeStruct((group, width), BF),
            jax.ShapeDtypeStruct((experts, group, 2 * ff), BF),
            jax.ShapeDtypeStruct((group, experts * ff), BF),
        ],
        compiler_params=params(),
        cost_estimate=pl.CostEstimate(
            flops=2 * group * width * ff * 3 * experts,
            bytes_accessed=w.size * 2 + 5 * experts * group * ff * 2,
            transcendentals=experts * group * ff,
        ),
        name="experts_backward",
    )(scalars, *after, *given, gates, gu, w)


def middle_kernel(n_after, sref, *refs):
    refs = refs[n_after:]
    pieces, refs = refs[:4], refs[4:]
    grad_ref, hown_ref, gates_ref, b_ref, gains_ref, router_ref, dh_ref, do_ref, small_ref = refs
    rows, width = grad_ref.shape

    @pl.when(sref[1] > 0)
    def _():
        place = own_rows(sref[0], rows)
        joined = pieces[0][...].astype(F32)
        for shift in range(1, 4):
            joined = joined + pieces[shift][...].astype(F32)
        grad_normed = joined[:, :width]
        grad_gate = joined[:, width : width + E]
        gates = gates_ref[place, :]
        grad_logits = (
            gates * (grad_gate - jnp.sum(gates * grad_gate, axis=1, keepdims=True))
        ).astype(BF)
        normed = b_ref[place, :]
        grad_normed = grad_normed + dot_nt(grad_logits, router_ref[:, :E])
        hidden = hown_ref[...]
        part, grad_gain = norm_back(hidden, rms_scale(hidden), gains_ref[1:2, :], grad_normed)
        grad_hidden = grad_ref[...].astype(F32) + part
        dh_ref[...] = grad_hidden
        do_ref[...] = grad_hidden.astype(BF)
        small_ref[0:E, :] = dot_tn(grad_logits, normed)
        small_ref[E : E + 1, :] = grad_gain
        small_ref[E + 1 :, :] = jnp.zeros((small_ref.shape[0] - E - 1, width), F32)


def middle(scalars, pieces, grad_own, hown, gates, b, gains, router, after):
    rows, width = grad_own.shape
    operands = [*pieces, grad_own, hown, gates, b, gains, router]
    return pl.pallas_call(
        lambda *refs: middle_kernel(len(after), *refs),
        grid_spec=pltpu.PrefetchScalarGridSpec(
            num_scalar_prefetch=1,
            grid=(1,),
            in_specs=anywhere(len(after)) + [whole(x.shape) for x in operands],
            out_specs=[whole((rows, width)), whole((rows, width)), whole((24, width))],
        ),
        out_shape=[
            jax.ShapeDtypeStruct((rows, width), F32),
            jax.ShapeDtypeStruct((rows, width), BF),
            jax.ShapeDtypeStruct((24, width), F32),
        ],
        compiler_params=params(),
        cost_estimate=pl.CostEstimate(
            flops=rows * width * 64, bytes_accessed=rows * width * 24, transcendentals=rows
        ),
        name="norm_backward",
    )(scalars, *after, *operands)


def attention_backward_kernel(n_after, sref, *refs):
    pieces, refs = refs[:4], refs[4:]
    sources, refs = refs[:9], refs[9 + n_after :]
    (
        dh_ref, xown_ref, small_ref, gains_ref, cos_ref, sin_ref, bias_ref, qkv_ref, lse_ref,
        dx_ref, dxlow_ref, small_out_ref, full_ref, dqkv_ref,
        now, buffers, sems,
    ) = refs
    me = sref[0]
    shard = dh_ref.shape[0]

    @pl.when(sref[1] > 0)
    def _():
        copies = fetches(sref[2], sources, buffers, sems)
        for copy in copies[0]:
            copy.start()
        assemble(me, pieces, full_ref)
        bias = bias_ref[...]
        lse = lse_ref[...]
        cos = jnp.concatenate([cos_ref[...]] * 3, axis=1)
        sin = jnp.concatenate([sin_ref[...]] * 3, axis=1)
        total = jnp.zeros((shard, full_ref.shape[1]), F32)
        for step in range(4):
            for copy in copies[step]:
                copy.wait()
            for copy in copies[step + 1] if step < 3 else []:
                copy.start()
            w_qkv, w_out = group_weights(buffers, step)
            do = dot(full_ref[...], w_out).astype(BF)
            qkv = qkv_ref[step]
            q, k, v = qkv[:, :256], qkv[:, 256:384], qkv[:, 384:]
            q_turned = q.T
            do_turned = do.T
            dq, dk, dv = [], [], []
            for kv in range(2):
                k_one = k[:, kv * HD : (kv + 1) * HD]
                v_one = v[:, kv * HD : (kv + 1) * HD]
                dk_one = dv_one = None
                for head in (2 * kv, 2 * kv + 1):
                    part = slice(head * HD, (head + 1) * HD)
                    scores = dot_nt(q[:, part], k_one) + bias
                    soft = jnp.exp(scores - lse[:, 4 * step + head : 4 * step + head + 1])
                    grad_soft = dot_nt(do[:, part], v_one)
                    grad_scores = soft * (
                        grad_soft - jnp.sum(soft * grad_soft, axis=1, keepdims=True)
                    )
                    grad_scores = grad_scores.astype(BF)
                    dq.append(dot(grad_scores, k_one))
                    dk_part = dot(q_turned[part, :], grad_scores)
                    dv_part = dot(do_turned[part, :], soft.astype(BF))
                    dk_one = dk_part if dk_one is None else dk_one + dk_part
                    dv_one = dv_part if dv_one is None else dv_one + dv_part
                dk.append(dk_one)
                dv.append(dv_one)
            grad_k = jnp.concatenate(dk, axis=0).T
            grad_v = jnp.concatenate(dv, axis=0).T
            grad_qk = jnp.concatenate([jnp.concatenate(dq, axis=1) * HD**-0.5, grad_k], axis=1)
            grad_qk = (grad_qk * cos - swap_halves(grad_qk) * sin).astype(BF)
            now[step, :, :384] = grad_qk
            now[step, :, 384:] = grad_v.astype(BF)
            if step == 0:
                dqkv_ref[...] = now[0]
            total += dot_nt(now[step, own_rows(me, shard), :], w_qkv)

        entering = xown_ref[...].astype(F32)
        part, grad_gain = norm_back(entering, rms_scale(entering), gains_ref[0:1, :], total)
        grad_entering = dh_ref[...] + part
        dx_ref[...] = grad_entering
        dxlow_ref[...] = grad_entering.astype(BF)
        rows = lax.broadcasted_iota(jnp.int32, small_ref.shape, 0)
        small_out_ref[...] = jnp.where(rows == E + 1, grad_gain, small_ref[...])


def attention_backward(
    scalars, pieces, dh, xown, small, gains, tables, qkv, lse, w_attn, after
):
    shard, width = dh.shape
    group = 4 * shard
    dp = width // 64
    cos, sin, bias = tables
    smalls = [dh, xown, small, gains, cos, sin, bias]
    per_step = lambda i, s: (i * s[1], 0, 0)
    outs = [
        ((shard, width), F32),
        ((shard, width), BF),
        (small.shape, F32),
        ((group, width), BF),
        ((group, 512), BF),
    ]
    return pl.pallas_call(
        lambda *refs: attention_backward_kernel(len(after), *refs),
        grid_spec=pltpu.PrefetchScalarGridSpec(
            num_scalar_prefetch=1,
            grid=(1,),
            in_specs=[whole(x.shape) for x in pieces]
            + anywhere(9 + len(after))
            + [whole(x.shape) for x in smalls]
            + [whole(qkv.shape), whole(lse.shape)],
            out_specs=[whole(shape) for shape, _ in outs],
            scratch_shapes=[
                pltpu.VMEM((4, group, 512), BF),
                pltpu.VMEM((4, dp, 400, LANES), BF),
                pltpu.SemaphoreType.DMA((9,)),
            ],
        ),
        out_shape=[jax.ShapeDtypeStruct(shape, kind) for shape, kind in outs],
        compiler_params=params(),
        cost_estimate=pl.CostEstimate(
            flops=group * width * 1024 * 2 + 16 * 10 * group * group * HD,
            bytes_accessed=width * 768 * 8 + 6 * group * width * 2,
            transcendentals=16 * group * group,
        ),
        name="attention_backward",
    )(scalars, *pieces, *w_attn, *after, *smalls, qkv, lse)


def expert_weights_kernel(n_after, sref, *refs):
    refs = refs[n_after:]
    b, refs = refs[:4], refs[4:]
    g, refs = refs[:4], refs[4:]
    dgu, refs = refs[:4], refs[4:]
    ga, refs = refs[:4], refs[4:]
    out_ref, bt_ref, gt_ref = refs
    group = b[0].shape[0]
    dp, _, _, dr, ff = out_ref.shape
    first = sref[1] > 0

    def chosen(four, micro, *index):
        index = index or (Ellipsis,)
        return jnp.where(first, four[micro][index], four[2 + micro][index])

    @pl.when(pl.program_id(0) == 0)
    def _():
        for micro in range(2):
            place = slice(micro * group, (micro + 1) * group)
            bt_ref[:, place] = chosen(b, micro).T
            gt_ref[:, place] = chosen(g, micro).T

    bt = bt_ref[...]
    for j in range(PER_GRAD):
        rows = jnp.concatenate([chosen(dgu, 0, j), chosen(dgu, 1, j)], axis=0)
        grads = dot(bt, rows).astype(BF)
        out_ref[:, 0, j] = grads[:, :ff].reshape(dp, dr, ff)
        out_ref[:, 1, j] = grads[:, ff:].reshape(dp, dr, ff)
    rows = jnp.concatenate([chosen(ga, 0), chosen(ga, 1)], axis=0)
    grads = dot(gt_ref[...], rows).astype(BF)
    for j in range(PER_GRAD):
        out_ref[:, 2, j] = grads[:, j * ff : (j + 1) * ff].reshape(dp, dr, ff)


def expert_weights(scalars, rows_b, grads, dgus, gas, dp, after):
    group, width = rows_b[0].shape
    experts, _, ff2 = dgus[0].shape
    ff = ff2 // 2
    dr = width // dp
    square = whole((group, width))
    wide, flat = [], []
    for held in (lambda s: s[1], lambda s: 1 - s[1]):
        wide += [
            pl.BlockSpec((PER_GRAD, group, ff2), lambda i, s, held=held: (i * held(s), 0, 0))
        ] * 2
        flat += [pl.BlockSpec((group, PER_GRAD * ff), lambda i, s, held=held: (0, i * held(s)))] * 2
    return pl.pallas_call(
        lambda *refs: expert_weights_kernel(len(after), *refs),
        grid_spec=pltpu.PrefetchScalarGridSpec(
            num_scalar_prefetch=1,
            grid=(experts // PER_GRAD,),
            in_specs=anywhere(len(after)) + [square] * 8 + wide + flat,
            out_specs=pl.BlockSpec((dp, 3, PER_GRAD, dr, ff), lambda i, s: (0, 0, i, 0, 0)),
            scratch_shapes=[
                pltpu.VMEM((width, 2 * group), BF),
                pltpu.VMEM((width, 2 * group), BF),
            ],
        ),
        out_shape=jax.ShapeDtypeStruct((dp, 3, experts, dr, ff), BF),
        compiler_params=params(),
        cost_estimate=pl.CostEstimate(
            flops=4 * group * width * ff * 3 * experts,
            bytes_accessed=dp * 3 * experts * dr * ff * 2 + 6 * experts * group * ff * 2,
            transcendentals=0,
        ),
        name="expert_weight_grads",
    )(scalars, *after, *rows_b, *grads, *dgus, *gas)


def attention_weights_kernel(sref, *refs):
    a, o, f, d, small = (refs[4 * j : 4 * j + 4] for j in range(5))
    out_ref = refs[20]
    dp = out_ref.shape[0]
    first = sref[1] > 0

    def chosen(four, micro):
        return jnp.where(first, four[micro][...], four[2 + micro][...])

    sums = dot_tn(chosen(a, 0), chosen(d, 0)) + dot_tn(chosen(a, 1), chosen(d, 1))
    for j in range(4):
        out_ref[:, 64 * j : 64 * (j + 1), :] = (
            sums[:, LANES * j : LANES * (j + 1)].astype(BF).reshape(dp, 64, LANES)
        )
    sums = dot_tn(chosen(f, 0), chosen(o, 0)) + dot_tn(chosen(f, 1), chosen(o, 1))
    for j in range(2):
        out_ref[:, 64 * (4 + j) : 64 * (5 + j), :] = (
            sums[:, LANES * j : LANES * (j + 1)].astype(BF).reshape(dp, 64, LANES)
        )
    rows = chosen(small, 0) + chosen(small, 1)
    rows = jnp.concatenate(
        [rows, jnp.zeros((LANES - rows.shape[0], rows.shape[1]), F32)], axis=0
    )
    out_ref[:, 384:, :] = rows.T.astype(BF).reshape(dp, 64, LANES)


def attention_weights(scalars, a, o, f, d, small, dp):
    group, width = a[0].shape
    operands = [*a, *o, *f, *d, *small]
    return pl.pallas_call(
        attention_weights_kernel,
        grid_spec=pltpu.PrefetchScalarGridSpec(
            num_scalar_prefetch=1,
            grid=(1,),
            in_specs=[whole(x.shape) for x in operands],
            out_specs=whole((dp, 448, LANES)),
        ),
        out_shape=jax.ShapeDtypeStruct((dp, 448, LANES), BF),
        compiler_params=params(),
        cost_estimate=pl.CostEstimate(
            flops=4 * group * width * 768,
            bytes_accessed=group * width * 14 + width * 768 * 2,
            transcendentals=0,
        ),
        name="attention_weight_grads",
    )(scalars, *operands)


def moved(array, shift):
    return lax.ppermute(array, "tensor", [(i, (i + shift) % 4) for i in range(4)])


def swapped(array, dp):
    return lax.ppermute(array, "dp", [(i, i ^ 1) for i in range(dp)])


def to_owner(pieces):
    return [pieces[0]] + [moved(pieces[s], s) for s in range(1, 4)]


def to_all(rows):
    return [rows] + [moved(rows, s) for s in range(1, 4)]


def across(rows, up):
    start, end = (0, 4) if up else (4, 0)
    return [
        lax.ppermute(
            rows, ("pipe", "tensor"), [(start + i, end + (i + s) % 4) for i in range(4)]
        )
        for s in range(4)
    ]


def tables_of(lengths, group):
    ends = jnp.cumsum(lengths)
    starts = ends - lengths
    index = jnp.arange(group, dtype=jnp.int32)
    inside = index[:, None] >= starts[None, :]
    start = jnp.max(jnp.where(inside, starts[None, :], 0), axis=1)
    position = (index - start).astype(F32)
    half = HD // 2
    freq = jnp.exp(jnp.arange(half, dtype=F32) * (-2.0 * math.log(10000.0) / HD))
    angle = position[:, None] * freq[None, :]
    cos, sin = jnp.cos(angle), jnp.sin(angle)
    visible = (index[None, :] <= index[:, None]) & (index[None, :] >= start[:, None])
    bias = jnp.where(visible, 0.0, MASKED).astype(F32)
    return (
        jnp.concatenate([cos, cos, cos, cos], axis=1),
        jnp.concatenate([-sin, sin, -sin, sin], axis=1),
        bias,
    )


def per_device(
    inputs, cotangent, doc_lengths, routes, norm_attn, w_query, w_key, w_value, w_out,
    w_router, norm_ffn, w_gate, w_up, w_down,
):
    section = lax.axis_index("pipe")
    first_section = section == 0
    me = lax.axis_index("tensor")
    dp = lax.axis_size("dp")
    core = lax.axis_index("dp") % 2
    micro = inputs.shape[0]
    shard, width = inputs.shape[1:]
    group = shard * 4
    rows_dp = width // dp
    scalars = [
        jnp.stack([me, (section == s).astype(jnp.int32), core]).astype(jnp.int32)
        for s in range(2)
    ]

    out_turned = w_out[0].T
    small = jnp.concatenate([w_router[0], norm_attn[0][:, None], norm_ffn[0][:, None]], axis=1)
    small = jnp.pad(small, ((0, 0), (0, LANES - E - 2)))
    piece = jnp.concatenate(
        [
            w_query[0][:, :LANES], w_query[0][:, LANES:], w_key[0], w_value[0],
            out_turned[:, :LANES], out_turned[:, LANES:], small,
        ],
        axis=0,
    )
    w_own = jnp.broadcast_to(piece[None], (dp,) + piece.shape)
    w_own, inputs, cotangent = lax.optimization_barrier((w_own, inputs, cotangent))
    w_own = lax.all_to_all(w_own, "dp", 0, 0, tiled=True)
    pieces_w = jnp.stack([w_gate[0], w_up[0], w_down[0].transpose(0, 2, 1)])
    w_experts = lax.all_gather(pieces_w, "dp", axis=0)
    rows_in, rows_cot = to_all(inputs), to_all(cotangent)
    rows_in, rows_cot, w_own = lax.optimization_barrier((rows_in, rows_cot, w_own))
    half, quarter = dp // 2, dp // 4
    mine = lax.dynamic_slice_in_dim(w_own, core * half, half, 0)
    w_next, w_last = moved(mine, 1), moved(mine, 3)
    w_over = [moved(w_next[:quarter], 1), moved(w_last[quarter:], 3)]
    other = [swapped(x, dp) for x in (w_next, w_last, *w_over)]
    w_attn = [w_own, w_next, other[0], *w_over, other[2], other[3], w_last, other[1]]
    router, gains = smalls_of(scalars[0], w_attn)

    rows_in = [[part[m] for part in rows_in] for m in range(micro)]
    rows_cot = [[part[m] for part in rows_cot] for m in range(micro)]
    tables = [tables_of(doc_lengths[m, 0], group) for m in range(micro)]
    ids = jnp.arange(E, dtype=jnp.int32)
    picked = jnp.any(routes[0][..., None] == ids, axis=2).astype(F32)

    after = []
    saves = [[None] * micro, [None] * micro]
    firsts = [[None] * micro, [None] * micro]
    middles = [[None] * micro, [None] * micro]
    lasts = [[None] * micro, [None] * micro]

    def attend(s, m, pieces):
        nonlocal after
        out = attention_forward(
            scalars[s], pieces, gains, tables[m], picked[m], w_attn, router, after
        )
        saves[s][m] = list(out)
        after = [out[6]]

    def expert(s, m):
        nonlocal after
        b, gates = saves[s][m][6:8]
        *parts, gu = experts_forward(scalars[s], b, gates, w_experts, after)
        saves[s][m].append(gu)
        after = [gu]
        return parts

    def expert_back(s, m, pieces):
        nonlocal after
        gates, gu = saves[s][m][7:9]
        *parts, grad, dgu, ga = experts_backward(
            scalars[s], pieces, gates, gu, w_experts, after
        )
        after = [grad]
        firsts[s][m] = (to_owner(parts), grad, dgu, ga)

    def norm_between(s, m, own):
        nonlocal after
        kept = saves[s][m]
        dh, do, small = middle(
            scalars[s], firsts[s][m][0], own, kept[5], kept[7], kept[6], gains, router, after
        )
        middles[s][m] = (dh, to_all(do), small)
        after = [do]

    def attend_back(s, m):
        nonlocal after
        kept = saves[s][m]
        dh, rows, small = middles[s][m]
        dx, dx_low, small, full, dqkv = attention_backward(
            scalars[s], rows, dh, kept[1], small, gains, tables[m], kept[2], kept[4],
            w_attn, after,
        )
        lasts[s][m] = (small, full, dqkv, dx)
        after = [dx]
        return dx_low

    def layer_sum(parts, hown):
        return finish(to_owner(parts), hown)

    attend(0, 0, rows_in[0])
    first_out = layer_sum(expert(0, 0), saves[0][0][5])
    first_in = across(first_out, True)
    after = [first_out]
    attend(0, 1, rows_in[1])
    attend(1, 0, first_in)
    second_out = layer_sum(expert(0, 1), saves[0][1][5])
    second_in = across(second_out, True)
    late = [expert(1, 0)]
    expert_back(1, 0, rows_cot[0])
    attend(1, 1, second_in)
    late.append(expert(1, 1))
    norm_between(1, 0, cotangent[0])
    expert_back(1, 1, rows_cot[1])
    first_back = across(attend_back(1, 0), False)
    norm_between(1, 1, cotangent[1])
    second_back = across(attend_back(1, 1), False)
    expert_back(0, 0, first_back)
    norm_between(0, 0, first_back[0])
    expert_back(0, 1, second_back)
    joined = firsts[0] + firsts[1]
    grad_experts = expert_weights(
        scalars[0],
        [saves[s][m][6] for s in range(2) for m in range(micro)],
        [x[1] for x in joined],
        [x[2] for x in joined],
        [x[3] for x in joined],
        dp,
        after,
    )
    expert_sums = lax.psum_scatter(grad_experts, "dp", scatter_dimension=0, tiled=True)[0]
    after = [grad_experts]
    norm_between(0, 1, second_back[0])
    attend_back(0, 0)
    attend_back(0, 1)
    late, _ = lax.optimization_barrier((late, lasts[1][1][3]))
    outputs = [
        [first_out, second_out],
        [layer_sum(late[m], saves[1][m][5]) for m in range(micro)],
    ]
    grads_in = [[lasts[s][m][3] for m in range(micro)] for s in range(2)]

    joined = lasts[0] + lasts[1]
    grad_attn = attention_weights(
        scalars[0],
        [saves[s][m][0] for s in range(2) for m in range(micro)],
        [saves[s][m][3] for s in range(2) for m in range(micro)],
        [x[1] for x in joined],
        [x[2] for x in joined],
        [x[0] for x in joined],
        dp,
    )
    grad_attn = lax.all_to_all(grad_attn, "dp", 0, 0, tiled=True)
    attn_sums = jnp.sum(grad_attn.astype(F32), axis=0)
    small = attn_sums[384:].reshape(4, 16, LANES)
    small_own = None
    for shift in range(4):
        part = lax.dynamic_index_in_dim(small, (me + shift) % 4, 0, keepdims=False)
        part = moved(part, shift) if shift else part
        small_own = part if small_own is None else small_own + part
    expert_sums = expert_sums.astype(F32)
    blocks = [attn_sums[64 * j : 64 * (j + 1)] for j in range(6)]
    section_rows = jnp.stack(
        [jnp.where(first_section, outputs[0][m], outputs[1][m]) for m in range(micro)]
    )
    grad_in = jnp.stack(
        [jnp.where(first_section, grads_in[0][m], grads_in[1][m]) for m in range(micro)]
    )
    return (
        section_rows[None],
        grad_in[None],
        small_own[:, E + 1][None],
        jnp.concatenate(blocks[:2], axis=1)[None],
        blocks[2][None],
        blocks[3][None],
        jnp.concatenate(blocks[4:], axis=1).T[None],
        small_own[:, :E][None],
        small_own[:, E][None],
        expert_sums[0][None],
        expert_sums[1][None],
        expert_sums[2].transpose(0, 2, 1)[None],
    )


def finish(parts, hown):
    result = hown
    for part in parts:
        result = result + part.astype(F32)
    return result.astype(BF)


def solution(mesh):
    in_specs = (
        P(None, ("dp", "tensor"), None),
        P(None, ("dp", "tensor"), None),
        P(None, "dp", None),
        P("pipe", None, "dp", None),
        P("pipe", ("dp", "tensor")),
        P("pipe", "dp", "tensor"),
        P("pipe", "dp", "tensor"),
        P("pipe", "dp", "tensor"),
        P("pipe", "tensor", "dp"),
        P("pipe", ("dp", "tensor"), None),
        P("pipe", ("dp", "tensor")),
        P("pipe", None, "dp", "tensor"),
        P("pipe", None, "dp", "tensor"),
        P("pipe", None, "tensor", "dp"),
    )
    out_specs = (
        P("pipe", None, ("dp", "tensor"), None),
        P("pipe", None, ("dp", "tensor"), None),
        P("pipe", ("dp", "tensor")),
        P("pipe", "dp", "tensor"),
        P("pipe", "dp", "tensor"),
        P("pipe", "dp", "tensor"),
        P("pipe", "tensor", "dp"),
        P("pipe", ("dp", "tensor"), None),
        P("pipe", ("dp", "tensor")),
        P("pipe", None, "dp", "tensor"),
        P("pipe", None, "dp", "tensor"),
        P("pipe", None, "tensor", "dp"),
    )
    return jax.shard_map(
        per_device, mesh=mesh, in_specs=in_specs, out_specs=out_specs, check_vma=False
    )
```

```python
import math

import jax
import jax.numpy as jnp
from jax import lax
from jax.experimental import pallas as pl
from jax.experimental.pallas import tpu as pltpu
from jax.sharding import PartitionSpec as P

HD = 64
E = 16
TOP = 8
EPSILON = 1e-06
MASKED = -1000000000.0
BF = jnp.bfloat16
F32 = jnp.float32
VMEM_LIMIT = 56 * 1024 * 1024
PER = 4
PER_BACK = 8
PER_GRAD = 4
LANES = 128


def params():
    return pltpu.CompilerParams(
        vmem_limit_bytes=VMEM_LIMIT, dimension_semantics=("arbitrary",)
    )


def dot(left, right):
    return jnp.dot(left, right, preferred_element_type=F32)


def dot_nt(left, right):
    return lax.dot_general(
        left, right, (((1,), (1,)), ((), ())), preferred_element_type=F32
    )


def dot_tn(left, right):
    return lax.dot_general(
        left, right, (((0,), (0,)), ((), ())), preferred_element_type=F32
    )


def column(rows, index):
    lanes = lax.broadcasted_iota(jnp.int32, rows.shape, 1)
    return jnp.sum(jnp.where(lanes == index, rows, 0.0), axis=1, keepdims=True)


def whole(shape):
    return pl.BlockSpec(shape, lambda i, s: (0,) * len(shape))


def rms_scale(values):
    return lax.rsqrt(jnp.mean(values * values, axis=-1, keepdims=True) + EPSILON)


def norm_back(values, scale_rows, gain, grad_normed):
    weighted = grad_normed * gain
    grad_values = scale_rows * weighted - values * scale_rows**3 * jnp.mean(
        weighted * values, axis=-1, keepdims=True
    )
    grad_gain = jnp.sum(grad_normed * values * scale_rows, axis=0, keepdims=True)
    return grad_values, grad_gain


def swap_halves(values):
    width = values.shape[1]
    lanes = lax.broadcasted_iota(jnp.int32, values.shape, 1)
    ahead = pltpu.roll(values, width - HD // 2, 1)
    behind = pltpu.roll(values, HD // 2, 1)
    return jnp.where(lanes % HD < HD // 2, ahead, behind)


def assemble(me, pieces, target):
    rows = pieces[0].shape[0]
    for shift in range(4):
        owner = lax.rem(me + 4 - shift, 4)
        target[own_rows(owner, rows), :] = pieces[shift][...]


def own_rows(me, rows):
    return pl.ds(pl.multiple_of(me * rows, rows), rows)


def anywhere(count):
    return [pl.BlockSpec(memory_space=pl.ANY)] * count


def fetches(core, sources, buffers, sems):
    dp = buffers.shape[1]
    half, quarter = dp // 2, dp // 4
    here, there = core * half, (1 - core) * half
    copies = [[pltpu.make_async_copy(sources[0], buffers.at[0], sems.at[0])]]
    number = 1
    for shift, starts in (
        (1, (here, there)),
        (2, (here, here + quarter, there, there + quarter)),
        (3, (here, there)),
    ):
        group = []
        for start in starts:
            source = sources[number]
            place = buffers.at[shift, pl.ds(start, source.shape[0])]
            group.append(pltpu.make_async_copy(source, place, sems.at[number]))
            number += 1
        copies.append(group)
    return copies


def group_weights(buffers, step):
    dp = buffers.shape[1]
    blocks = [
        buffers[step, :, 64 * j : 64 * (j + 1), :].reshape(dp * 64, LANES) for j in range(6)
    ]
    return jnp.concatenate(blocks[:4], axis=1), jnp.concatenate(blocks[4:], axis=1)


def smalls_kernel(sref, *refs):
    sources, (router_ref, gains_ref, stage, sems) = refs[:9], refs[9:]
    dp = stage.shape[0]
    half, quarter = dp // 2, dp // 4
    me = sref[0]
    here, there = sref[2] * half, (1 - sref[2]) * half
    places = (
        (0, 0), (1, here), (1, there),
        (2, here), (2, here + quarter), (2, there), (2, there + quarter), (3, here), (3, there),
    )
    copies = []
    for number, (shift, start) in enumerate(places):
        source = sources[number]
        owner = lax.rem(me + 4 - shift, 4)
        copies.append(
            pltpu.make_async_copy(
                source.at[:, pl.ds(384, 16)],
                stage.at[pl.ds(start, source.shape[0]), owner],
                sems.at[number],
            )
        )
    for copy in copies:
        copy.start()
    for copy in copies:
        copy.wait()
    rows = stage[...].reshape(dp * 64, LANES)
    router_ref[...] = rows
    turned = rows.astype(F32).T
    gains_ref[...] = turned[E : E + 8, :]


def smalls_of(scalars, w_attn):
    dp = w_attn[0].shape[0]
    width = dp * 64
    return pl.pallas_call(
        smalls_kernel,
        grid_spec=pltpu.PrefetchScalarGridSpec(
            num_scalar_prefetch=1,
            grid=(1,),
            in_specs=anywhere(9),
            out_specs=[whole((width, LANES)), whole((8, width))],
            scratch_shapes=[pltpu.VMEM((dp, 4, 16, LANES), BF), pltpu.SemaphoreType.DMA((9,))],
        ),
        out_shape=[
            jax.ShapeDtypeStruct((width, LANES), BF),
            jax.ShapeDtypeStruct((8, width), F32),
        ],
        compiler_params=params(),
        name="router_and_gains",
    )(scalars, *w_attn)


def attention_forward_kernel(n_after, sref, *refs):
    pieces, refs = refs[:4], refs[4:]
    sources, refs = refs[:9], refs[9 + n_after :]

    @pl.when(sref[1] > 0)
    def _():
        attention_part(sref, pieces, sources, *refs)


def attention_part(
    sref, pieces, sources,
    gains_ref, cos_ref, sin_ref, bias_ref, picked_ref, router_ref,
    a_ref, xown_ref, qkv_ref, o_ref, lse_ref, hown_ref, b_ref, gates_ref,
    hidden, buffers, sems,
):
    me = sref[0]
    group, width = b_ref.shape
    shard = xown_ref.shape[0]

    copies = fetches(sref[2], sources, buffers, sems)
    for copy in copies[0]:
        copy.start()
    assemble(me, pieces, b_ref)
    entering = b_ref[...].astype(F32)
    a_ref[...] = (entering * rms_scale(entering) * gains_ref[0:1, :]).astype(BF)
    xown_ref[...] = pieces[0][...]
    hidden[...] = entering
    cos = jnp.concatenate([cos_ref[...]] * 3, axis=1)
    sin = jnp.concatenate([sin_ref[...]] * 3, axis=1)
    bias = bias_ref[...]
    lanes = lax.broadcasted_iota(jnp.int32, (group, LANES), 1)
    lse_all = jnp.zeros((group, LANES), F32)
    for step in range(4):
        for copy in copies[step]:
            copy.wait()
        for copy in copies[step + 1] if step < 3 else []:
            copy.start()
        w_qkv, w_out = group_weights(buffers, step)
        qkv = dot(a_ref[...], w_qkv)
        qk = qkv[:, :384]
        turned = qk * cos + swap_halves(qk) * sin
        q = (turned[:, :256] * HD**-0.5).astype(BF)
        k = turned[:, 256:].astype(BF)
        v = qkv[:, 384:].astype(BF)
        qkv_ref[step, :, :256] = q
        qkv_ref[step, :, 256:384] = k
        qkv_ref[step, :, 384:] = v
        outs = []
        for head in range(4):
            kv = head // 2
            scores = dot_nt(
                q[:, head * HD : (head + 1) * HD], k[:, kv * HD : (kv + 1) * HD]
            )
            scores = scores + bias
            peak = jnp.max(scores, axis=1, keepdims=True)
            soft = jnp.exp(scores - peak)
            total = jnp.sum(soft, axis=1, keepdims=True)
            lse_all = jnp.where(lanes == 4 * step + head, peak + jnp.log(total), lse_all)
            soft = (soft * (1.0 / total)).astype(BF)
            outs.append(dot(soft, v[:, kv * HD : (kv + 1) * HD]))
        mixed = jnp.concatenate(outs, axis=1).astype(BF)
        if step == 0:
            o_ref[...] = mixed
        hidden[...] += dot_nt(mixed, w_out)
    lse_ref[...] = lse_all
    rows = hidden[...]
    normed = (rows * rms_scale(rows) * gains_ref[1:2, :]).astype(BF)
    b_ref[...] = normed
    hown_ref[...] = hidden[own_rows(me, shard), :]
    logits = dot(normed, router_ref[...])[:, :E]
    picked = picked_ref[...]
    peak = jnp.max(jnp.where(picked > 0, logits, -1e30), axis=1, keepdims=True)
    powers = jnp.where(picked > 0, jnp.exp(jnp.minimum(logits - peak, 0.0)), 0.0)
    gates_ref[...] = powers / jnp.sum(powers, axis=1, keepdims=True)


def attention_forward(scalars, pieces, gains, tables, picked, w_attn, router, after):
    shard, width = pieces[0].shape
    group = 4 * shard
    dp = width // 64
    cos, sin, bias = tables
    smalls = [gains, cos, sin, bias, picked, router]
    per_step = lambda i, s: (i * s[1], 0, 0)
    outs = [
        ((group, width), BF, None),
        ((shard, width), BF, None),
        ((4, group, 512), BF, None),
        ((group, 256), BF, None),
        ((group, LANES), F32, None),
        ((shard, width), F32, None),
        ((group, width), BF, None),
        ((group, E), F32, None),
    ]
    return pl.pallas_call(
        lambda *refs: attention_forward_kernel(len(after), *refs),
        grid_spec=pltpu.PrefetchScalarGridSpec(
            num_scalar_prefetch=1,
            grid=(1,),
            in_specs=[whole(x.shape) for x in pieces]
            + anywhere(9 + len(after))
            + [whole(x.shape) for x in smalls],
            out_specs=[
                whole(shape) if block is None else pl.BlockSpec(block, per_step)
                for shape, _, block in outs
            ],
            scratch_shapes=[
                pltpu.VMEM((group, width), F32),
                pltpu.VMEM((4, dp, 400, LANES), BF),
                pltpu.SemaphoreType.DMA((9,)),
            ],
        ),
        out_shape=[jax.ShapeDtypeStruct(shape, kind) for shape, kind, _ in outs],
        compiler_params=params(),
        cost_estimate=pl.CostEstimate(
            flops=2 * group * width * 768 * 4 + 16 * 4 * group * group * HD,
            bytes_accessed=width * 768 * 8 + 6 * group * width * 2,
            transcendentals=16 * group * group,
        ),
        name="attention_forward",
    )(scalars, *pieces, *w_attn, *after, *smalls)


def chunk(number):
    return pl.ds(PER * number, PER)


def experts_forward_kernel(n_after, sref, *refs):
    w_ref, b_ref, gate_ref, *refs = refs[n_after:]
    pieces, (gu_ref, total, held, gu_held, sems) = refs[:4], refs[4:]

    @pl.when(sref[1] > 0)
    def _():
        come, leave = experts_copies(w_ref, gu_ref, held, gu_held, sems)
        come[0].start()
        come[1].start()
        experts_part(sref, come, leave, b_ref, gate_ref, pieces, total, held, gu_held)


def experts_copies(w_ref, gu_ref, held, gu_held, sems):
    chunks = w_ref.shape[2] // PER
    come = [
        pltpu.make_async_copy(
            w_ref.at[:, :, chunk(c)], held.at[:, :, chunk(c)], sems.at[c]
        )
        for c in range(chunks)
    ]
    leave = [
        pltpu.make_async_copy(gu_held.at[chunk(c)], gu_ref.at[chunk(c)], sems.at[chunks + c])
        for c in range(chunks)
    ]
    return come, leave


def experts_part(sref, come, leave, b_ref, gate_ref, pieces, total, held, gu_held):
    group, width = b_ref.shape
    ff = held.shape[-1]
    chunks = len(come)
    gates = gate_ref[...]
    for c in range(chunks):
        come[c].wait()
        if c + 2 < chunks:
            come[c + 2].start()
        acts, downs = [], []
        for e in range(PER * c, PER * (c + 1)):
            gate_up = jnp.concatenate(
                [held[:, 0, e].reshape(width, ff), held[:, 1, e].reshape(width, ff)], axis=1
            )
            both = dot(b_ref[...], gate_up)
            gu_held[e] = both.astype(BF)
            gate_pre, up_pre = both[:, :ff], both[:, ff:]
            act = gate_pre * jax.nn.sigmoid(gate_pre) * up_pre
            acts.append((act * gates[:, e : e + 1]).astype(BF))
            downs.append(held[:, 2, e].reshape(width, ff))
        leave[c].start()
        out = dot_nt(jnp.concatenate(acts, axis=1), jnp.concatenate(downs, axis=1))
        if c == 0:
            total[...] = out
        else:
            total[...] += out
    rows = group // 4
    for shift in range(4):
        place = own_rows(lax.rem(sref[0] + shift, 4), rows)
        pieces[shift][...] = total[place, :].astype(BF)
    for c in range(chunks):
        leave[c].wait()


def experts_forward(scalars, b, gates, w, after):
    group, width = b.shape
    dp, _, experts, dr, ff = w.shape
    piece = (group // 4, width)
    return pl.pallas_call(
        lambda *refs: experts_forward_kernel(len(after), *refs),
        grid_spec=pltpu.PrefetchScalarGridSpec(
            num_scalar_prefetch=1,
            grid=(1,),
            in_specs=anywhere(len(after) + 1) + [whole((group, width)), whole((group, experts))],
            out_specs=[whole(piece)] * 4 + anywhere(1),
            scratch_shapes=[
                pltpu.VMEM((group, width), F32),
                pltpu.VMEM(w.shape, BF),
                pltpu.VMEM((experts, group, 2 * ff), BF),
                pltpu.SemaphoreType.DMA((2 * experts // PER,)),
            ],
        ),
        out_shape=[jax.ShapeDtypeStruct(piece, BF)] * 4
        + [jax.ShapeDtypeStruct((experts, group, 2 * ff), BF)],
        compiler_params=params(),
        cost_estimate=pl.CostEstimate(
            flops=2 * group * width * ff * 3 * experts,
            bytes_accessed=w.size * 2 + experts * group * 2 * ff * 2,
            transcendentals=experts * group * ff,
        ),
        name="experts_forward",
    )(scalars, *after, w, b, gates)


def layer_forward_kernel(n_after, sref, *refs):
    pieces, refs = refs[:4], refs[4:]
    sources, refs = refs[:9], refs[9:]
    w_ref, refs = refs[0], refs[1 + n_after :]
    smalls, refs = refs[:6], refs[6:]
    kept, refs = refs[:8], refs[8:]
    parts, refs = refs[:4], refs[4:]
    gu_ref, total, buffers, held, gu_held, sems, expert_sems = refs

    @pl.when(sref[1] > 0)
    def _():
        come, leave = experts_copies(w_ref, gu_ref, held, gu_held, expert_sems)
        come[0].start()
        come[1].start()
        attention_part(sref, pieces, sources, *smalls, *kept, total, buffers, sems)
        experts_part(sref, come, leave, kept[6], kept[7], parts, total, held, gu_held)


def layer_forward(scalars, pieces, gains, tables, picked, w_attn, router, w, after):
    shard, width = pieces[0].shape
    group = 4 * shard
    dp, _, experts, dr, ff = w.shape
    smalls = [gains, *tables, picked, router]
    outs = [
        ((group, width), BF),
        ((shard, width), BF),
        ((4, group, 512), BF),
        ((group, 256), BF),
        ((group, LANES), F32),
        ((shard, width), F32),
        ((group, width), BF),
        ((group, E), F32),
    ] + [((shard, width), BF)] * 4
    gu_shape = (experts, group, 2 * ff)
    out = pl.pallas_call(
        lambda *refs: layer_forward_kernel(len(after), *refs),
        grid_spec=pltpu.PrefetchScalarGridSpec(
            num_scalar_prefetch=1,
            grid=(1,),
            in_specs=[whole(x.shape) for x in pieces]
            + anywhere(10 + len(after))
            + [whole(x.shape) for x in smalls],
            out_specs=[whole(shape) for shape, _ in outs] + anywhere(1),
            scratch_shapes=[
                pltpu.VMEM((group, width), F32),
                pltpu.VMEM((4, dp, 400, LANES), BF),
                pltpu.VMEM(w.shape, BF),
                pltpu.VMEM(gu_shape, BF),
                pltpu.SemaphoreType.DMA((9,)),
                pltpu.SemaphoreType.DMA((2 * experts // PER,)),
            ],
        ),
        out_shape=[jax.ShapeDtypeStruct(shape, kind) for shape, kind in outs]
        + [jax.ShapeDtypeStruct(gu_shape, BF)],
        compiler_params=params(),
        cost_estimate=pl.CostEstimate(
            flops=2 * group * width * (768 * 4 + ff * 3 * experts) + 64 * group * group * HD,
            bytes_accessed=width * 768 * 8 + w.size * 2 + 8 * group * width * 2,
            transcendentals=16 * group * group + experts * group * ff,
        ),
        name="layer_forward",
    )(scalars, *pieces, *w_attn, w, *after, *smalls)
    return list(out[:8]), list(out[8:12]), out[12]


def experts_backward_kernel(n_after, sref, *refs):
    (*refs,) = refs[n_after:]
    given, refs = refs[:4], refs[4:]
    gate_ref, gu_ref, w_ref, *refs = refs
    pieces, refs = refs[:4], refs[4:]
    grad_ref, dgu_ref, ga_ref, total, total_gate = refs
    step = pl.program_id(0)
    group, width = grad_ref.shape
    ff = w_ref.shape[-1]

    @pl.when(sref[1] > 0)
    def _():
        @pl.when(step == 0)
        def _():
            assemble(sref[0], given, grad_ref)

        grad = grad_ref[...]
        gates = gate_ref[...]
        down = jnp.concatenate(
            [w_ref[:, 2, j].reshape(width, ff) for j in range(PER_BACK)], axis=1
        )
        turned = dot(grad, down)
        lanes = lax.broadcasted_iota(jnp.int32, (group, LANES), 1)
        grad_gate = jnp.zeros((group, LANES), F32)
        out = None
        for j in range(PER_BACK):
            expert = step * PER_BACK + j
            back = turned[:, j * ff : (j + 1) * ff]
            both = gu_ref[j].astype(F32)
            gate_pre, up_pre = both[:, :ff], both[:, ff:]
            sigma = jax.nn.sigmoid(gate_pre)
            silu = gate_pre * sigma
            act = silu * up_pre
            gate = column(gates, expert)
            grad_gate = jnp.where(
                lanes == expert, jnp.sum(act * back, axis=1, keepdims=True), grad_gate
            )
            grad_act = gate * back
            grad_pre = grad_act * up_pre * sigma * (1.0 + gate_pre * (1.0 - sigma))
            grad_up = grad_act * silu
            grad_both = jnp.concatenate([grad_pre.astype(BF), grad_up.astype(BF)], axis=1)
            dgu_ref[j] = grad_both
            ga_ref[:, j * ff : (j + 1) * ff] = (gate * act).astype(BF)
            gate_up = jnp.concatenate(
                [w_ref[:, 0, j].reshape(width, ff), w_ref[:, 1, j].reshape(width, ff)], axis=1
            )
            part = dot_nt(grad_both, gate_up)
            out = part if out is None else out + part

        @pl.when(step == 0)
        def _():
            total[...] = out
            total_gate[...] = grad_gate

        @pl.when(step > 0)
        def _():
            total[...] += out
            total_gate[...] += grad_gate

        @pl.when(step == pl.num_programs(0) - 1)
        def _():
            rows = group // 4
            for shift in range(4):
                place = own_rows(lax.rem(sref[0] + shift, 4), rows)
                pieces[shift][:, :width] = total[place, :].astype(BF)
                pieces[shift][:, width:] = total_gate[place, :].astype(BF)


def experts_backward(scalars, given, gates, gu, w, after):
    dp, _, experts, dr, ff = w.shape
    group = gates.shape[0]
    width = dp * dr
    piece = (group // 4, width + LANES)
    return pl.pallas_call(
        lambda *refs: experts_backward_kernel(len(after), *refs),
        grid_spec=pltpu.PrefetchScalarGridSpec(
            num_scalar_prefetch=1,
            grid=(experts // PER_BACK,),
            in_specs=anywhere(len(after))
            + [whole(x.shape) for x in given]
            + [
                whole((group, experts)),
                pl.BlockSpec((PER_BACK, group, 2 * ff), lambda i, s: (i * s[1], 0, 0)),
                pl.BlockSpec((dp, 3, PER_BACK, dr, ff), lambda i, s: (0, 0, i * s[1], 0, 0)),
            ],
            out_specs=[whole(piece)] * 4
            + [
                whole((group, width)),
                pl.BlockSpec((PER_BACK, group, 2 * ff), lambda i, s: (i * s[1], 0, 0)),
                pl.BlockSpec((group, PER_BACK * ff), lambda i, s: (0, i * s[1])),
            ],
            scratch_shapes=[pltpu.VMEM((group, width), F32), pltpu.VMEM((group, LANES), F32)],
        ),
        out_shape=[jax.ShapeDtypeStruct(piece, BF)] * 4
        + [
            jax.ShapeDtypeStruct((group, width), BF),
            jax.ShapeDtypeStruct((experts, group, 2 * ff), BF),
            jax.ShapeDtypeStruct((group, experts * ff), BF),
        ],
        compiler_params=params(),
        cost_estimate=pl.CostEstimate(
            flops=2 * group * width * ff * 3 * experts,
            bytes_accessed=w.size * 2 + 5 * experts * group * ff * 2,
            transcendentals=experts * group * ff,
        ),
        name="experts_backward",
    )(scalars, *after, *given, gates, gu, w)


def middle_kernel(n_after, sref, *refs):
    refs = refs[n_after:]
    pieces, refs = refs[:4], refs[4:]
    grad_ref, hown_ref, gates_ref, b_ref, gains_ref, router_ref, dh_ref, do_ref, small_ref = refs
    rows, width = grad_ref.shape

    @pl.when(sref[1] > 0)
    def _():
        place = own_rows(sref[0], rows)
        joined = pieces[0][...].astype(F32)
        for shift in range(1, 4):
            joined = joined + pieces[shift][...].astype(F32)
        grad_normed = joined[:, :width]
        grad_gate = joined[:, width : width + E]
        gates = gates_ref[place, :]
        grad_logits = (
            gates * (grad_gate - jnp.sum(gates * grad_gate, axis=1, keepdims=True))
        ).astype(BF)
        normed = b_ref[place, :]
        grad_normed = grad_normed + dot_nt(grad_logits, router_ref[:, :E])
        hidden = hown_ref[...]
        part, grad_gain = norm_back(hidden, rms_scale(hidden), gains_ref[1:2, :], grad_normed)
        grad_hidden = grad_ref[...].astype(F32) + part
        dh_ref[...] = grad_hidden
        do_ref[...] = grad_hidden.astype(BF)
        small_ref[0:E, :] = dot_tn(grad_logits, normed)
        small_ref[E : E + 1, :] = grad_gain
        small_ref[E + 1 :, :] = jnp.zeros((small_ref.shape[0] - E - 1, width), F32)


def middle(scalars, pieces, grad_own, hown, gates, b, gains, router, after):
    rows, width = grad_own.shape
    operands = [*pieces, grad_own, hown, gates, b, gains, router]
    return pl.pallas_call(
        lambda *refs: middle_kernel(len(after), *refs),
        grid_spec=pltpu.PrefetchScalarGridSpec(
            num_scalar_prefetch=1,
            grid=(1,),
            in_specs=anywhere(len(after)) + [whole(x.shape) for x in operands],
            out_specs=[whole((rows, width)), whole((rows, width)), whole((24, width))],
        ),
        out_shape=[
            jax.ShapeDtypeStruct((rows, width), F32),
            jax.ShapeDtypeStruct((rows, width), BF),
            jax.ShapeDtypeStruct((24, width), F32),
        ],
        compiler_params=params(),
        cost_estimate=pl.CostEstimate(
            flops=rows * width * 64, bytes_accessed=rows * width * 24, transcendentals=rows
        ),
        name="norm_backward",
    )(scalars, *after, *operands)


def attention_backward_kernel(n_after, sref, *refs):
    pieces, refs = refs[:4], refs[4:]
    sources, refs = refs[:9], refs[9 + n_after :]
    (
        dh_ref, xown_ref, small_ref, gains_ref, cos_ref, sin_ref, bias_ref, qkv_ref, lse_ref,
        dx_ref, dxlow_ref, small_out_ref, full_ref, dqkv_ref,
        now, buffers, sems,
    ) = refs
    me = sref[0]
    shard = dh_ref.shape[0]

    @pl.when(sref[1] > 0)
    def _():
        copies = fetches(sref[2], sources, buffers, sems)
        for copy in copies[0]:
            copy.start()
        assemble(me, pieces, full_ref)
        bias = bias_ref[...]
        lse = lse_ref[...]
        cos = jnp.concatenate([cos_ref[...]] * 3, axis=1)
        sin = jnp.concatenate([sin_ref[...]] * 3, axis=1)
        total = jnp.zeros((shard, full_ref.shape[1]), F32)
        for step in range(4):
            for copy in copies[step]:
                copy.wait()
            for copy in copies[step + 1] if step < 3 else []:
                copy.start()
            w_qkv, w_out = group_weights(buffers, step)
            do = dot(full_ref[...], w_out).astype(BF)
            qkv = qkv_ref[step]
            q, k, v = qkv[:, :256], qkv[:, 256:384], qkv[:, 384:]
            q_turned = q.T
            do_turned = do.T
            dq, dk, dv = [], [], []
            for kv in range(2):
                k_one = k[:, kv * HD : (kv + 1) * HD]
                v_one = v[:, kv * HD : (kv + 1) * HD]
                dk_one = dv_one = None
                for head in (2 * kv, 2 * kv + 1):
                    part = slice(head * HD, (head + 1) * HD)
                    scores = dot_nt(q[:, part], k_one) + bias
                    soft = jnp.exp(scores - lse[:, 4 * step + head : 4 * step + head + 1])
                    grad_soft = dot_nt(do[:, part], v_one)
                    grad_scores = soft * (
                        grad_soft - jnp.sum(soft * grad_soft, axis=1, keepdims=True)
                    )
                    grad_scores = grad_scores.astype(BF)
                    dq.append(dot(grad_scores, k_one))
                    dk_part = dot(q_turned[part, :], grad_scores)
                    dv_part = dot(do_turned[part, :], soft.astype(BF))
                    dk_one = dk_part if dk_one is None else dk_one + dk_part
                    dv_one = dv_part if dv_one is None else dv_one + dv_part
                dk.append(dk_one)
                dv.append(dv_one)
            grad_k = jnp.concatenate(dk, axis=0).T
            grad_v = jnp.concatenate(dv, axis=0).T
            grad_qk = jnp.concatenate([jnp.concatenate(dq, axis=1) * HD**-0.5, grad_k], axis=1)
            grad_qk = (grad_qk * cos - swap_halves(grad_qk) * sin).astype(BF)
            now[step, :, :384] = grad_qk
            now[step, :, 384:] = grad_v.astype(BF)
            if step == 0:
                dqkv_ref[...] = now[0]
            total += dot_nt(now[step, own_rows(me, shard), :], w_qkv)

        entering = xown_ref[...].astype(F32)
        part, grad_gain = norm_back(entering, rms_scale(entering), gains_ref[0:1, :], total)
        grad_entering = dh_ref[...] + part
        dx_ref[...] = grad_entering
        dxlow_ref[...] = grad_entering.astype(BF)
        rows = lax.broadcasted_iota(jnp.int32, small_ref.shape, 0)
        small_out_ref[...] = jnp.where(rows == E + 1, grad_gain, small_ref[...])


def attention_backward(
    scalars, pieces, dh, xown, small, gains, tables, qkv, lse, w_attn, after
):
    shard, width = dh.shape
    group = 4 * shard
    dp = width // 64
    cos, sin, bias = tables
    smalls = [dh, xown, small, gains, cos, sin, bias]
    per_step = lambda i, s: (i * s[1], 0, 0)
    outs = [
        ((shard, width), F32),
        ((shard, width), BF),
        (small.shape, F32),
        ((group, width), BF),
        ((group, 512), BF),
    ]
    return pl.pallas_call(
        lambda *refs: attention_backward_kernel(len(after), *refs),
        grid_spec=pltpu.PrefetchScalarGridSpec(
            num_scalar_prefetch=1,
            grid=(1,),
            in_specs=[whole(x.shape) for x in pieces]
            + anywhere(9 + len(after))
            + [whole(x.shape) for x in smalls]
            + [whole(qkv.shape), whole(lse.shape)],
            out_specs=[whole(shape) for shape, _ in outs],
            scratch_shapes=[
                pltpu.VMEM((4, group, 512), BF),
                pltpu.VMEM((4, dp, 400, LANES), BF),
                pltpu.SemaphoreType.DMA((9,)),
            ],
        ),
        out_shape=[jax.ShapeDtypeStruct(shape, kind) for shape, kind in outs],
        compiler_params=params(),
        cost_estimate=pl.CostEstimate(
            flops=group * width * 1024 * 2 + 16 * 10 * group * group * HD,
            bytes_accessed=width * 768 * 8 + 6 * group * width * 2,
            transcendentals=16 * group * group,
        ),
        name="attention_backward",
    )(scalars, *pieces, *w_attn, *after, *smalls, qkv, lse)


def expert_weights_kernel(n_after, sref, *refs):
    refs = refs[n_after:]
    b, refs = refs[:4], refs[4:]
    g, refs = refs[:4], refs[4:]
    dgu, refs = refs[:4], refs[4:]
    ga, refs = refs[:4], refs[4:]
    out_ref, bt_ref, gt_ref = refs
    group = b[0].shape[0]
    dp, _, _, dr, ff = out_ref.shape
    first = sref[1] > 0

    def chosen(four, micro, *index):
        index = index or (Ellipsis,)
        return jnp.where(first, four[micro][index], four[2 + micro][index])

    @pl.when(pl.program_id(0) == 0)
    def _():
        for micro in range(2):
            place = slice(micro * group, (micro + 1) * group)
            bt_ref[:, place] = chosen(b, micro).T
            gt_ref[:, place] = chosen(g, micro).T

    bt = bt_ref[...]
    for j in range(PER_GRAD):
        rows = jnp.concatenate([chosen(dgu, 0, j), chosen(dgu, 1, j)], axis=0)
        grads = dot(bt, rows).astype(BF)
        out_ref[:, 0, j] = grads[:, :ff].reshape(dp, dr, ff)
        out_ref[:, 1, j] = grads[:, ff:].reshape(dp, dr, ff)
    rows = jnp.concatenate([chosen(ga, 0), chosen(ga, 1)], axis=0)
    grads = dot(gt_ref[...], rows).astype(BF)
    for j in range(PER_GRAD):
        out_ref[:, 2, j] = grads[:, j * ff : (j + 1) * ff].reshape(dp, dr, ff)


def expert_weights(scalars, rows_b, grads, dgus, gas, dp, after):
    group, width = rows_b[0].shape
    experts, _, ff2 = dgus[0].shape
    ff = ff2 // 2
    dr = width // dp
    square = whole((group, width))
    wide, flat = [], []
    for held in (lambda s: s[1], lambda s: 1 - s[1]):
        wide += [
            pl.BlockSpec((PER_GRAD, group, ff2), lambda i, s, held=held: (i * held(s), 0, 0))
        ] * 2
        flat += [pl.BlockSpec((group, PER_GRAD * ff), lambda i, s, held=held: (0, i * held(s)))] * 2
    return pl.pallas_call(
        lambda *refs: expert_weights_kernel(len(after), *refs),
        grid_spec=pltpu.PrefetchScalarGridSpec(
            num_scalar_prefetch=1,
            grid=(experts // PER_GRAD,),
            in_specs=anywhere(len(after)) + [square] * 8 + wide + flat,
            out_specs=pl.BlockSpec((dp, 3, PER_GRAD, dr, ff), lambda i, s: (0, 0, i, 0, 0)),
            scratch_shapes=[
                pltpu.VMEM((width, 2 * group), BF),
                pltpu.VMEM((width, 2 * group), BF),
            ],
        ),
        out_shape=jax.ShapeDtypeStruct((dp, 3, experts, dr, ff), BF),
        compiler_params=params(),
        cost_estimate=pl.CostEstimate(
            flops=4 * group * width * ff * 3 * experts,
            bytes_accessed=dp * 3 * experts * dr * ff * 2 + 6 * experts * group * ff * 2,
            transcendentals=0,
        ),
        name="expert_weight_grads",
    )(scalars, *after, *rows_b, *grads, *dgus, *gas)


def attention_weights_kernel(sref, *refs):
    a, o, f, d, small = (refs[4 * j : 4 * j + 4] for j in range(5))
    out_ref = refs[20]
    dp = out_ref.shape[0]
    first = sref[1] > 0

    def chosen(four, micro):
        return jnp.where(first, four[micro][...], four[2 + micro][...])

    sums = dot_tn(chosen(a, 0), chosen(d, 0)) + dot_tn(chosen(a, 1), chosen(d, 1))
    for j in range(4):
        out_ref[:, 64 * j : 64 * (j + 1), :] = (
            sums[:, LANES * j : LANES * (j + 1)].astype(BF).reshape(dp, 64, LANES)
        )
    sums = dot_tn(chosen(f, 0), chosen(o, 0)) + dot_tn(chosen(f, 1), chosen(o, 1))
    for j in range(2):
        out_ref[:, 64 * (4 + j) : 64 * (5 + j), :] = (
            sums[:, LANES * j : LANES * (j + 1)].astype(BF).reshape(dp, 64, LANES)
        )
    rows = chosen(small, 0) + chosen(small, 1)
    rows = jnp.concatenate(
        [rows, jnp.zeros((LANES - rows.shape[0], rows.shape[1]), F32)], axis=0
    )
    out_ref[:, 384:, :] = rows.T.astype(BF).reshape(dp, 64, LANES)


def attention_weights(scalars, a, o, f, d, small, dp):
    group, width = a[0].shape
    operands = [*a, *o, *f, *d, *small]
    return pl.pallas_call(
        attention_weights_kernel,
        grid_spec=pltpu.PrefetchScalarGridSpec(
            num_scalar_prefetch=1,
            grid=(1,),
            in_specs=[whole(x.shape) for x in operands],
            out_specs=whole((dp, 448, LANES)),
        ),
        out_shape=jax.ShapeDtypeStruct((dp, 448, LANES), BF),
        compiler_params=params(),
        cost_estimate=pl.CostEstimate(
            flops=4 * group * width * 768,
            bytes_accessed=group * width * 14 + width * 768 * 2,
            transcendentals=0,
        ),
        name="attention_weight_grads",
    )(scalars, *operands)


def moved(array, shift):
    return lax.ppermute(array, "tensor", [(i, (i + shift) % 4) for i in range(4)])


def swapped(array, dp):
    return lax.ppermute(array, "dp", [(i, i ^ 1) for i in range(dp)])


def to_owner(pieces):
    return [pieces[0]] + [moved(pieces[s], s) for s in range(1, 4)]


def to_all(rows):
    return [rows] + [moved(rows, s) for s in range(1, 4)]


def across(rows, up):
    start, end = (0, 4) if up else (4, 0)
    return [
        lax.ppermute(
            rows, ("pipe", "tensor"), [(start + i, end + (i + s) % 4) for i in range(4)]
        )
        for s in range(4)
    ]


def tables_of(lengths, group):
    ends = jnp.cumsum(lengths)
    starts = ends - lengths
    index = jnp.arange(group, dtype=jnp.int32)
    inside = index[:, None] >= starts[None, :]
    start = jnp.max(jnp.where(inside, starts[None, :], 0), axis=1)
    position = (index - start).astype(F32)
    half = HD // 2
    freq = jnp.exp(jnp.arange(half, dtype=F32) * (-2.0 * math.log(10000.0) / HD))
    angle = position[:, None] * freq[None, :]
    cos, sin = jnp.cos(angle), jnp.sin(angle)
    visible = (index[None, :] <= index[:, None]) & (index[None, :] >= start[:, None])
    bias = jnp.where(visible, 0.0, MASKED).astype(F32)
    return (
        jnp.concatenate([cos, cos, cos, cos], axis=1),
        jnp.concatenate([-sin, sin, -sin, sin], axis=1),
        bias,
    )


def per_device(
    inputs, cotangent, doc_lengths, routes, norm_attn, w_query, w_key, w_value, w_out,
    w_router, norm_ffn, w_gate, w_up, w_down,
):
    section = lax.axis_index("pipe")
    first_section = section == 0
    me = lax.axis_index("tensor")
    dp = lax.axis_size("dp")
    core = lax.axis_index("dp") % 2
    micro = inputs.shape[0]
    shard, width = inputs.shape[1:]
    group = shard * 4
    rows_dp = width // dp
    scalars = [
        jnp.stack([me, (section == s).astype(jnp.int32), core]).astype(jnp.int32)
        for s in range(2)
    ]

    out_turned = w_out[0].T
    small = jnp.concatenate([w_router[0], norm_attn[0][:, None], norm_ffn[0][:, None]], axis=1)
    small = jnp.pad(small, ((0, 0), (0, LANES - E - 2)))
    piece = jnp.concatenate(
        [
            w_query[0][:, :LANES], w_query[0][:, LANES:], w_key[0], w_value[0],
            out_turned[:, :LANES], out_turned[:, LANES:], small,
        ],
        axis=0,
    )
    w_own = jnp.broadcast_to(piece[None], (dp,) + piece.shape)
    w_own = lax.all_to_all(w_own, "dp", 0, 0, tiled=True)
    pieces_w = jnp.stack([w_gate[0], w_up[0], w_down[0].transpose(0, 2, 1)])
    w_experts = lax.all_gather(pieces_w, "dp", axis=0)
    tables = [tables_of(doc_lengths[m, 0], group) for m in range(micro)]
    tables, inputs, cotangent = lax.optimization_barrier((tables, inputs, cotangent))
    rows_in, rows_cot = to_all(inputs), to_all(cotangent)
    rows_in, rows_cot, w_own = lax.optimization_barrier((rows_in, rows_cot, w_own))
    rows_in = [[part[m] for part in rows_in] for m in range(micro)]
    rows_cot = [[part[m] for part in rows_cot] for m in range(micro)]
    half, quarter = dp // 2, dp // 4
    mine = lax.dynamic_slice_in_dim(w_own, core * half, half, 0)
    w_next, w_last = moved(mine, 1), moved(mine, 3)
    w_over = [moved(w_next[:quarter], 1), moved(w_last[quarter:], 3)]
    other = [swapped(x, dp) for x in (w_next, w_last, *w_over)]
    w_attn = [w_own, w_next, other[0], *w_over, other[2], other[3], w_last, other[1]]
    w_attn, rows_in, rows_cot = lax.optimization_barrier((w_attn, rows_in, rows_cot))
    router, gains = smalls_of(scalars[0], w_attn)

    ids = jnp.arange(E, dtype=jnp.int32)
    picked = jnp.any(routes[0][..., None] == ids, axis=2).astype(F32)

    after = []
    saves = [[None] * micro, [None] * micro]
    firsts = [[None] * micro, [None] * micro]
    middles = [[None] * micro, [None] * micro]
    lasts = [[None] * micro, [None] * micro]

    def attend(s, m, pieces):
        nonlocal after
        out = attention_forward(
            scalars[s], pieces, gains, tables[m], picked[m], w_attn, router, after
        )
        saves[s][m] = list(out)
        after = [out[6]]

    def expert(s, m):
        nonlocal after
        b, gates = saves[s][m][6:8]
        *parts, gu = experts_forward(scalars[s], b, gates, w_experts, after)
        saves[s][m].append(gu)
        after = [gu]
        return parts

    def layer(s, m, pieces):
        nonlocal after
        kept, parts, gu = layer_forward(
            scalars[s], pieces, gains, tables[m], picked[m], w_attn, router, w_experts, after
        )
        saves[s][m] = [*kept, gu]
        after = [gu]
        return parts

    def expert_back(s, m, pieces):
        nonlocal after
        gates, gu = saves[s][m][7:9]
        *parts, grad, dgu, ga = experts_backward(
            scalars[s], pieces, gates, gu, w_experts, after
        )
        after = [grad]
        firsts[s][m] = (to_owner(parts), grad, dgu, ga)

    def norm_between(s, m, own):
        nonlocal after
        kept = saves[s][m]
        dh, do, small = middle(
            scalars[s], firsts[s][m][0], own, kept[5], kept[7], kept[6], gains, router, after
        )
        middles[s][m] = (dh, to_all(do), small)
        after = [do]

    def attend_back(s, m):
        nonlocal after
        kept = saves[s][m]
        dh, rows, small = middles[s][m]
        dx, dx_low, small, full, dqkv = attention_backward(
            scalars[s], rows, dh, kept[1], small, gains, tables[m], kept[2], kept[4],
            w_attn, after,
        )
        lasts[s][m] = (small, full, dqkv, dx)
        after = [dx]
        return dx_low

    def layer_sum(parts, hown):
        return finish(to_owner(parts), hown)

    attend(0, 0, rows_in[0])
    first_out = layer_sum(expert(0, 0), saves[0][0][5])
    first_in = across(first_out, True)
    after = [first_out]
    attend(0, 1, rows_in[1])
    late = [layer(1, 0, first_in)]
    second_out = layer_sum(expert(0, 1), saves[0][1][5])
    second_in = across(second_out, True)
    expert_back(1, 0, rows_cot[0])
    late.append(layer(1, 1, second_in))
    norm_between(1, 0, cotangent[0])
    expert_back(1, 1, rows_cot[1])
    first_back = across(attend_back(1, 0), False)
    norm_between(1, 1, cotangent[1])
    expert_back(0, 0, first_back)
    second_back = across(attend_back(1, 1), False)
    norm_between(0, 0, first_back[0])
    expert_back(0, 1, second_back)
    joined = firsts[0] + firsts[1]
    grad_experts = expert_weights(
        scalars[0],
        [saves[s][m][6] for s in range(2) for m in range(micro)],
        [x[1] for x in joined],
        [x[2] for x in joined],
        [x[3] for x in joined],
        dp,
        after,
    )
    expert_sums = lax.psum_scatter(grad_experts, "dp", scatter_dimension=0, tiled=True)[0]
    after = [grad_experts]
    norm_between(0, 1, second_back[0])
    attend_back(0, 0)
    attend_back(0, 1)
    late, _ = lax.optimization_barrier((late, lasts[1][1][3]))
    outputs = [
        [first_out, second_out],
        [layer_sum(late[m], saves[1][m][5]) for m in range(micro)],
    ]
    grads_in = [[lasts[s][m][3] for m in range(micro)] for s in range(2)]

    joined = lasts[0] + lasts[1]
    grad_attn = attention_weights(
        scalars[0],
        [saves[s][m][0] for s in range(2) for m in range(micro)],
        [saves[s][m][3] for s in range(2) for m in range(micro)],
        [x[1] for x in joined],
        [x[2] for x in joined],
        [x[0] for x in joined],
        dp,
    )
    grad_attn = lax.all_to_all(grad_attn, "dp", 0, 0, tiled=True)
    attn_sums = jnp.sum(grad_attn.astype(F32), axis=0)
    small = attn_sums[384:].reshape(4, 16, LANES)
    small_own = None
    for shift in range(4):
        part = lax.dynamic_index_in_dim(small, (me + shift) % 4, 0, keepdims=False)
        part = moved(part, shift) if shift else part
        small_own = part if small_own is None else small_own + part
    expert_sums = expert_sums.astype(F32)
    blocks = [attn_sums[64 * j : 64 * (j + 1)] for j in range(6)]
    section_rows = jnp.stack(
        [jnp.where(first_section, outputs[0][m], outputs[1][m]) for m in range(micro)]
    )
    grad_in = jnp.stack(
        [jnp.where(first_section, grads_in[0][m], grads_in[1][m]) for m in range(micro)]
    )
    return (
        section_rows[None],
        grad_in[None],
        small_own[:, E + 1][None],
        jnp.concatenate(blocks[:2], axis=1)[None],
        blocks[2][None],
        blocks[3][None],
        jnp.concatenate(blocks[4:], axis=1).T[None],
        small_own[:, :E][None],
        small_own[:, E][None],
        expert_sums[0][None],
        expert_sums[1][None],
        expert_sums[2].transpose(0, 2, 1)[None],
    )


def finish(parts, hown):
    result = hown
    for part in parts:
        result = result + part.astype(F32)
    return result.astype(BF)


def solution(mesh):
    in_specs = (
        P(None, ("dp", "tensor"), None),
        P(None, ("dp", "tensor"), None),
        P(None, "dp", None),
        P("pipe", None, "dp", None),
        P("pipe", ("dp", "tensor")),
        P("pipe", "dp", "tensor"),
        P("pipe", "dp", "tensor"),
        P("pipe", "dp", "tensor"),
        P("pipe", "tensor", "dp"),
        P("pipe", ("dp", "tensor"), None),
        P("pipe", ("dp", "tensor")),
        P("pipe", None, "dp", "tensor"),
        P("pipe", None, "dp", "tensor"),
        P("pipe", None, "tensor", "dp"),
    )
    out_specs = (
        P("pipe", None, ("dp", "tensor"), None),
        P("pipe", None, ("dp", "tensor"), None),
        P("pipe", ("dp", "tensor")),
        P("pipe", "dp", "tensor"),
        P("pipe", "dp", "tensor"),
        P("pipe", "dp", "tensor"),
        P("pipe", "tensor", "dp"),
        P("pipe", ("dp", "tensor"), None),
        P("pipe", ("dp", "tensor")),
        P("pipe", None, "dp", "tensor"),
        P("pipe", None, "dp", "tensor"),
        P("pipe", None, "tensor", "dp"),
    )
    return jax.shard_map(
        per_device, mesh=mesh, in_specs=in_specs, out_specs=out_specs, check_vma=False
    )
```

```python
import math

import jax
import jax.numpy as jnp
from jax import lax
from jax.experimental import pallas as pl
from jax.experimental.pallas import tpu as pltpu
from jax.sharding import PartitionSpec as P

HD = 64
E = 16
TOP = 8
EPSILON = 1e-06
MASKED = -1000000000.0
BF = jnp.bfloat16
F32 = jnp.float32
VMEM_LIMIT = 56 * 1024 * 1024
PER = 4
PER_STEP = 8
PER_GRAD = 4
LANES = 128


def params():
    return pltpu.CompilerParams(
        vmem_limit_bytes=VMEM_LIMIT, dimension_semantics=("arbitrary",)
    )


def dot(left, right):
    return jnp.dot(left, right, preferred_element_type=F32)


def dot_nt(left, right):
    return lax.dot_general(
        left, right, (((1,), (1,)), ((), ())), preferred_element_type=F32
    )


def dot_tn(left, right):
    return lax.dot_general(
        left, right, (((0,), (0,)), ((), ())), preferred_element_type=F32
    )


def column(rows, index):
    lanes = lax.broadcasted_iota(jnp.int32, rows.shape, 1)
    return jnp.sum(jnp.where(lanes == index, rows, 0.0), axis=1, keepdims=True)


def whole(shape):
    return pl.BlockSpec(shape, lambda i, s: (0,) * len(shape))


def rms_scale(values):
    return lax.rsqrt(jnp.mean(values * values, axis=-1, keepdims=True) + EPSILON)


def norm_back(values, scale_rows, gain, grad_normed):
    weighted = grad_normed * gain
    grad_values = scale_rows * weighted - values * scale_rows**3 * jnp.mean(
        weighted * values, axis=-1, keepdims=True
    )
    grad_gain = jnp.sum(grad_normed * values * scale_rows, axis=0, keepdims=True)
    return grad_values, grad_gain


def swap_halves(values):
    width = values.shape[1]
    lanes = lax.broadcasted_iota(jnp.int32, values.shape, 1)
    ahead = pltpu.roll(values, width - HD // 2, 1)
    behind = pltpu.roll(values, HD // 2, 1)
    return jnp.where(lanes % HD < HD // 2, ahead, behind)


def assemble(me, pieces, target):
    rows = pieces[0].shape[0]
    for shift in range(4):
        owner = lax.rem(me + 4 - shift, 4)
        target[own_rows(owner, rows), :] = pieces[shift][...]


def own_rows(me, rows):
    return pl.ds(pl.multiple_of(me * rows, rows), rows)


def anywhere(count):
    return [pl.BlockSpec(memory_space=pl.ANY)] * count


def fetches(core, sources, buffers, sems):
    dp = buffers.shape[1]
    half, quarter = dp // 2, dp // 4
    here, there = core * half, (1 - core) * half
    copies = [[pltpu.make_async_copy(sources[0], buffers.at[0], sems.at[0])]]
    number = 1
    for shift, starts in (
        (1, (here, there)),
        (2, (here, here + quarter, there, there + quarter)),
        (3, (here, there)),
    ):
        group = []
        for start in starts:
            source = sources[number]
            place = buffers.at[shift, pl.ds(start, source.shape[0])]
            group.append(pltpu.make_async_copy(source, place, sems.at[number]))
            number += 1
        copies.append(group)
    return copies


def group_weights(buffers, step):
    dp = buffers.shape[1]
    blocks = [
        buffers[step, :, 64 * j : 64 * (j + 1), :].reshape(dp * 64, LANES) for j in range(6)
    ]
    return jnp.concatenate(blocks[:4], axis=1), jnp.concatenate(blocks[4:], axis=1)


def smalls_kernel(sref, *refs):
    sources, (router_ref, gains_ref, stage, sems) = refs[:9], refs[9:]
    dp = stage.shape[0]
    half, quarter = dp // 2, dp // 4
    me = sref[0]
    here, there = sref[2] * half, (1 - sref[2]) * half
    places = (
        (0, 0), (1, here), (1, there),
        (2, here), (2, here + quarter), (2, there), (2, there + quarter), (3, here), (3, there),
    )
    copies = []
    for number, (shift, start) in enumerate(places):
        source = sources[number]
        owner = lax.rem(me + 4 - shift, 4)
        copies.append(
            pltpu.make_async_copy(
                source.at[:, pl.ds(384, 16)],
                stage.at[pl.ds(start, source.shape[0]), owner],
                sems.at[number],
            )
        )
    for copy in copies:
        copy.start()
    for copy in copies:
        copy.wait()
    rows = stage[...].reshape(dp * 64, LANES)
    router_ref[...] = rows
    turned = rows.astype(F32).T
    gains_ref[...] = turned[E : E + 8, :]


def smalls_of(scalars, w_attn):
    dp = w_attn[0].shape[0]
    width = dp * 64
    return pl.pallas_call(
        smalls_kernel,
        grid_spec=pltpu.PrefetchScalarGridSpec(
            num_scalar_prefetch=1,
            grid=(1,),
            in_specs=anywhere(9),
            out_specs=[whole((width, LANES)), whole((8, width))],
            scratch_shapes=[pltpu.VMEM((dp, 4, 16, LANES), BF), pltpu.SemaphoreType.DMA((9,))],
        ),
        out_shape=[
            jax.ShapeDtypeStruct((width, LANES), BF),
            jax.ShapeDtypeStruct((8, width), F32),
        ],
        compiler_params=params(),
        name="router_and_gains",
    )(scalars, *w_attn)


def attention_forward_kernel(n_after, sref, *refs):
    pieces, refs = refs[:4], refs[4:]
    sources, refs = refs[:9], refs[9 + n_after :]
    (
        gains_ref, cos_ref, sin_ref, bias_ref, picked_ref, router_ref,
        a_ref, xown_ref, qkv_ref, o_ref, lse_ref, hown_ref, b_ref, gates_ref,
        hidden, buffers, sems,
    ) = refs
    step = pl.program_id(0)
    me = sref[0]
    group, width = b_ref.shape
    shard = xown_ref.shape[0]

    @pl.when(sref[1] > 0)
    def _():
        copies = fetches(sref[2], sources, buffers, sems)

        @pl.when(step == 0)
        def _():
            for part in copies:
                for copy in part:
                    copy.start()
            assemble(me, pieces, b_ref)
            entering = b_ref[...].astype(F32)
            a_ref[...] = (entering * rms_scale(entering) * gains_ref[0:1, :]).astype(BF)
            xown_ref[...] = pieces[0][...]
            hidden[...] = entering

        for shift, part in enumerate(copies):

            @pl.when(step == shift)
            def _(part=part):
                for copy in part:
                    copy.wait()

        w_qkv, w_out = group_weights(buffers, step)
        qkv = dot(a_ref[...], w_qkv)
        qk = qkv[:, :384]
        cos = jnp.concatenate([cos_ref[...]] * 3, axis=1)
        sin = jnp.concatenate([sin_ref[...]] * 3, axis=1)
        turned = qk * cos + swap_halves(qk) * sin
        q = (turned[:, :256] * HD**-0.5).astype(BF)
        k = turned[:, 256:].astype(BF)
        v = qkv[:, 384:].astype(BF)
        qkv_ref[0, :, :256] = q
        qkv_ref[0, :, 256:384] = k
        qkv_ref[0, :, 384:] = v
        bias = bias_ref[...]
        lanes = lax.broadcasted_iota(jnp.int32, (group, LANES), 1)
        lse_all = jnp.where(step == 0, 0.0, lse_ref[...])
        outs = []
        for head in range(4):
            kv = head // 2
            scores = dot_nt(q[:, head * HD : (head + 1) * HD], k[:, kv * HD : (kv + 1) * HD])
            scores = scores + bias
            peak = jnp.max(scores, axis=1, keepdims=True)
            soft = jnp.exp(scores - peak)
            total = jnp.sum(soft, axis=1, keepdims=True)
            lse_all = jnp.where(lanes == 4 * step + head, peak + jnp.log(total), lse_all)
            soft = (soft * (1.0 / total)).astype(BF)
            outs.append(dot(soft, v[:, kv * HD : (kv + 1) * HD]))
        mixed = jnp.concatenate(outs, axis=1).astype(BF)

        @pl.when(step == 0)
        def _():
            o_ref[...] = mixed

        lse_ref[...] = lse_all
        hidden[...] += dot_nt(mixed, w_out)

        @pl.when(step == pl.num_programs(0) - 1)
        def _():
            rows = hidden[...]
            normed = (rows * rms_scale(rows) * gains_ref[1:2, :]).astype(BF)
            b_ref[...] = normed
            hown_ref[...] = hidden[own_rows(me, shard), :]
            logits = dot(normed, router_ref[...])[:, :E]
            picked = picked_ref[...]
            peak = jnp.max(jnp.where(picked > 0, logits, -1e30), axis=1, keepdims=True)
            powers = jnp.where(picked > 0, jnp.exp(jnp.minimum(logits - peak, 0.0)), 0.0)
            gates_ref[...] = powers / jnp.sum(powers, axis=1, keepdims=True)


def attention_forward(scalars, pieces, gains, tables, picked, w_attn, router, after):
    shard, width = pieces[0].shape
    group = 4 * shard
    dp = width // 64
    cos, sin, bias = tables
    smalls = [gains, cos, sin, bias, picked, router]
    per_step = lambda i, s: (i * s[1], 0, 0)
    outs = [
        ((group, width), BF, None),
        ((shard, width), BF, None),
        ((4, group, 512), BF, (1, group, 512)),
        ((group, 256), BF, None),
        ((group, LANES), F32, None),
        ((shard, width), F32, None),
        ((group, width), BF, None),
        ((group, E), F32, None),
    ]
    return pl.pallas_call(
        lambda *refs: attention_forward_kernel(len(after), *refs),
        grid_spec=pltpu.PrefetchScalarGridSpec(
            num_scalar_prefetch=1,
            grid=(4,),
            in_specs=[whole(x.shape) for x in pieces]
            + anywhere(9 + len(after))
            + [whole(x.shape) for x in smalls],
            out_specs=[
                whole(shape) if block is None else pl.BlockSpec(block, per_step)
                for shape, _, block in outs
            ],
            scratch_shapes=[
                pltpu.VMEM((group, width), F32),
                pltpu.VMEM((4, dp, 400, LANES), BF),
                pltpu.SemaphoreType.DMA((9,)),
            ],
        ),
        out_shape=[jax.ShapeDtypeStruct(shape, kind) for shape, kind, _ in outs],
        compiler_params=params(),
        cost_estimate=pl.CostEstimate(
            flops=2 * group * width * 768 * 4 + 16 * 4 * group * group * HD,
            bytes_accessed=width * 768 * 8 + 6 * group * width * 2,
            transcendentals=16 * group * group,
        ),
        name="attention_forward",
    )(scalars, *pieces, *w_attn, *after, *smalls)

def attention_part(
    sref, pieces, sources,
    gains_ref, cos_ref, sin_ref, bias_ref, picked_ref, router_ref,
    a_ref, xown_ref, qkv_ref, o_ref, lse_ref, hown_ref, b_ref, gates_ref,
    hidden, buffers, sems,
):
    me = sref[0]
    group, width = b_ref.shape
    shard = xown_ref.shape[0]

    copies = fetches(sref[2], sources, buffers, sems)
    for copy in copies[0]:
        copy.start()
    assemble(me, pieces, b_ref)
    entering = b_ref[...].astype(F32)
    a_ref[...] = (entering * rms_scale(entering) * gains_ref[0:1, :]).astype(BF)
    xown_ref[...] = pieces[0][...]
    hidden[...] = entering
    cos = jnp.concatenate([cos_ref[...]] * 3, axis=1)
    sin = jnp.concatenate([sin_ref[...]] * 3, axis=1)
    bias = bias_ref[...]
    lanes = lax.broadcasted_iota(jnp.int32, (group, LANES), 1)
    lse_all = jnp.zeros((group, LANES), F32)
    for step in range(4):
        for copy in copies[step]:
            copy.wait()
        for copy in copies[step + 1] if step < 3 else []:
            copy.start()
        w_qkv, w_out = group_weights(buffers, step)
        qkv = dot(a_ref[...], w_qkv)
        qk = qkv[:, :384]
        turned = qk * cos + swap_halves(qk) * sin
        q = (turned[:, :256] * HD**-0.5).astype(BF)
        k = turned[:, 256:].astype(BF)
        v = qkv[:, 384:].astype(BF)
        qkv_ref[step, :, :256] = q
        qkv_ref[step, :, 256:384] = k
        qkv_ref[step, :, 384:] = v
        outs = []
        for head in range(4):
            kv = head // 2
            scores = dot_nt(
                q[:, head * HD : (head + 1) * HD], k[:, kv * HD : (kv + 1) * HD]
            )
            scores = scores + bias
            peak = jnp.max(scores, axis=1, keepdims=True)
            soft = jnp.exp(scores - peak)
            total = jnp.sum(soft, axis=1, keepdims=True)
            lse_all = jnp.where(lanes == 4 * step + head, peak + jnp.log(total), lse_all)
            soft = (soft * (1.0 / total)).astype(BF)
            outs.append(dot(soft, v[:, kv * HD : (kv + 1) * HD]))
        mixed = jnp.concatenate(outs, axis=1).astype(BF)
        if step == 0:
            o_ref[...] = mixed
        hidden[...] += dot_nt(mixed, w_out)
    lse_ref[...] = lse_all
    rows = hidden[...]
    normed = (rows * rms_scale(rows) * gains_ref[1:2, :]).astype(BF)
    b_ref[...] = normed
    hown_ref[...] = hidden[own_rows(me, shard), :]
    logits = dot(normed, router_ref[...])[:, :E]
    picked = picked_ref[...]
    peak = jnp.max(jnp.where(picked > 0, logits, -1e30), axis=1, keepdims=True)
    powers = jnp.where(picked > 0, jnp.exp(jnp.minimum(logits - peak, 0.0)), 0.0)
    gates_ref[...] = powers / jnp.sum(powers, axis=1, keepdims=True)


def chunk(number):
    return pl.ds(PER * number, PER)


def experts_forward_kernel(n_after, sref, *refs):
    (b_ref, gate_ref, w_ref, *refs) = refs[n_after:]
    pieces, (gu_ref, total) = refs[:4], refs[4:]
    step = pl.program_id(0)
    width = b_ref.shape[1]
    ff = w_ref.shape[-1]

    @pl.when(sref[1] > 0)
    def _():
        b = b_ref[...]
        gates = gate_ref[...]
        acts, downs = [], []
        for j in range(PER_STEP):
            gate_up = jnp.concatenate(
                [w_ref[:, 0, j].reshape(width, ff), w_ref[:, 1, j].reshape(width, ff)], axis=1
            )
            both = dot(b, gate_up)
            gu_ref[j] = both.astype(BF)
            gate_pre, up_pre = both[:, :ff], both[:, ff:]
            act = gate_pre * jax.nn.sigmoid(gate_pre) * up_pre
            acts.append((act * column(gates, step * PER_STEP + j)).astype(BF))
            downs.append(w_ref[:, 2, j].reshape(width, ff))
        out = dot_nt(jnp.concatenate(acts, axis=1), jnp.concatenate(downs, axis=1))

        @pl.when(step == 0)
        def _():
            total[...] = out

        @pl.when(step > 0)
        def _():
            total[...] += out

        @pl.when(step == pl.num_programs(0) - 1)
        def _():
            rows = b_ref.shape[0] // 4
            for shift in range(4):
                place = own_rows(lax.rem(sref[0] + shift, 4), rows)
                pieces[shift][...] = total[place, :].astype(BF)


def experts_forward(scalars, b, gates, w, after):
    group, width = b.shape
    dp, _, experts, dr, ff = w.shape
    piece = (group // 4, width)
    return pl.pallas_call(
        lambda *refs: experts_forward_kernel(len(after), *refs),
        grid_spec=pltpu.PrefetchScalarGridSpec(
            num_scalar_prefetch=1,
            grid=(experts // PER_STEP,),
            in_specs=anywhere(len(after))
            + [
                whole((group, width)),
                whole((group, experts)),
                pl.BlockSpec((dp, 3, PER_STEP, dr, ff), lambda i, s: (0, 0, i * s[1], 0, 0)),
            ],
            out_specs=[whole(piece)] * 4
            + [pl.BlockSpec((PER_STEP, group, 2 * ff), lambda i, s: (i * s[1], 0, 0))],
            scratch_shapes=[pltpu.VMEM((group, width), F32)],
        ),
        out_shape=[jax.ShapeDtypeStruct(piece, BF)] * 4
        + [jax.ShapeDtypeStruct((experts, group, 2 * ff), BF)],
        compiler_params=params(),
        cost_estimate=pl.CostEstimate(
            flops=2 * group * width * ff * 3 * experts,
            bytes_accessed=w.size * 2 + experts * group * 2 * ff * 2,
            transcendentals=experts * group * ff,
        ),
        name="experts_forward",
    )(scalars, *after, b, gates, w)


def experts_copies(w_ref, gu_ref, held, gu_held, sems):
    chunks = w_ref.shape[2] // PER
    come = [
        pltpu.make_async_copy(
            w_ref.at[:, :, chunk(c)], held.at[:, :, chunk(c)], sems.at[c]
        )
        for c in range(chunks)
    ]
    leave = [
        pltpu.make_async_copy(gu_held.at[chunk(c)], gu_ref.at[chunk(c)], sems.at[chunks + c])
        for c in range(chunks)
    ]
    return come, leave


def experts_part(sref, come, leave, b_ref, gate_ref, pieces, total, held, gu_held):
    group, width = b_ref.shape
    ff = held.shape[-1]
    chunks = len(come)
    gates = gate_ref[...]
    for c in range(chunks):
        come[c].wait()
        if c + 2 < chunks:
            come[c + 2].start()
        acts, downs = [], []
        for e in range(PER * c, PER * (c + 1)):
            gate_up = jnp.concatenate(
                [held[:, 0, e].reshape(width, ff), held[:, 1, e].reshape(width, ff)], axis=1
            )
            both = dot(b_ref[...], gate_up)
            gu_held[e] = both.astype(BF)
            gate_pre, up_pre = both[:, :ff], both[:, ff:]
            act = gate_pre * jax.nn.sigmoid(gate_pre) * up_pre
            acts.append((act * gates[:, e : e + 1]).astype(BF))
            downs.append(held[:, 2, e].reshape(width, ff))
        leave[c].start()
        out = dot_nt(jnp.concatenate(acts, axis=1), jnp.concatenate(downs, axis=1))
        if c == 0:
            total[...] = out
        else:
            total[...] += out
    rows = group // 4
    for shift in range(4):
        place = own_rows(lax.rem(sref[0] + shift, 4), rows)
        pieces[shift][...] = total[place, :].astype(BF)
    for c in range(chunks):
        leave[c].wait()


def layer_forward_kernel(n_after, sref, *refs):
    pieces, refs = refs[:4], refs[4:]
    sources, refs = refs[:9], refs[9:]
    w_ref, refs = refs[0], refs[1 + n_after :]
    smalls, refs = refs[:6], refs[6:]
    kept, refs = refs[:8], refs[8:]
    parts, refs = refs[:4], refs[4:]
    gu_ref, total, buffers, held, gu_held, sems, expert_sems = refs

    @pl.when(sref[1] > 0)
    def _():
        come, leave = experts_copies(w_ref, gu_ref, held, gu_held, expert_sems)
        come[0].start()
        come[1].start()
        attention_part(sref, pieces, sources, *smalls, *kept, total, buffers, sems)
        experts_part(sref, come, leave, kept[6], kept[7], parts, total, held, gu_held)


def layer_forward(scalars, pieces, gains, tables, picked, w_attn, router, w, after):
    shard, width = pieces[0].shape
    group = 4 * shard
    dp, _, experts, dr, ff = w.shape
    smalls = [gains, *tables, picked, router]
    outs = [
        ((group, width), BF),
        ((shard, width), BF),
        ((4, group, 512), BF),
        ((group, 256), BF),
        ((group, LANES), F32),
        ((shard, width), F32),
        ((group, width), BF),
        ((group, E), F32),
    ] + [((shard, width), BF)] * 4
    gu_shape = (experts, group, 2 * ff)
    out = pl.pallas_call(
        lambda *refs: layer_forward_kernel(len(after), *refs),
        grid_spec=pltpu.PrefetchScalarGridSpec(
            num_scalar_prefetch=1,
            grid=(1,),
            in_specs=[whole(x.shape) for x in pieces]
            + anywhere(10 + len(after))
            + [whole(x.shape) for x in smalls],
            out_specs=[whole(shape) for shape, _ in outs] + anywhere(1),
            scratch_shapes=[
                pltpu.VMEM((group, width), F32),
                pltpu.VMEM((4, dp, 400, LANES), BF),
                pltpu.VMEM(w.shape, BF),
                pltpu.VMEM(gu_shape, BF),
                pltpu.SemaphoreType.DMA((9,)),
                pltpu.SemaphoreType.DMA((2 * experts // PER,)),
            ],
        ),
        out_shape=[jax.ShapeDtypeStruct(shape, kind) for shape, kind in outs]
        + [jax.ShapeDtypeStruct(gu_shape, BF)],
        compiler_params=params(),
        cost_estimate=pl.CostEstimate(
            flops=2 * group * width * (768 * 4 + ff * 3 * experts) + 64 * group * group * HD,
            bytes_accessed=width * 768 * 8 + w.size * 2 + 8 * group * width * 2,
            transcendentals=16 * group * group + experts * group * ff,
        ),
        name="layer_forward",
    )(scalars, *pieces, *w_attn, w, *after, *smalls)
    return list(out[:8]), list(out[8:12]), out[12]


def experts_backward_kernel(n_after, sref, *refs):
    (*refs,) = refs[n_after:]
    given, refs = refs[:4], refs[4:]
    gate_ref, gu_ref, w_ref, *refs = refs
    pieces, refs = refs[:4], refs[4:]
    grad_ref, dgu_ref, ga_ref, total, total_gate = refs
    step = pl.program_id(0)
    group, width = grad_ref.shape
    ff = w_ref.shape[-1]

    @pl.when(sref[1] > 0)
    def _():
        @pl.when(step == 0)
        def _():
            assemble(sref[0], given, grad_ref)

        grad = grad_ref[...]
        gates = gate_ref[...]
        down = jnp.concatenate(
            [w_ref[:, 2, j].reshape(width, ff) for j in range(PER_STEP)], axis=1
        )
        turned = dot(grad, down)
        lanes = lax.broadcasted_iota(jnp.int32, (group, LANES), 1)
        grad_gate = jnp.zeros((group, LANES), F32)
        out = None
        for j in range(PER_STEP):
            expert = step * PER_STEP + j
            back = turned[:, j * ff : (j + 1) * ff]
            both = gu_ref[j].astype(F32)
            gate_pre, up_pre = both[:, :ff], both[:, ff:]
            sigma = jax.nn.sigmoid(gate_pre)
            silu = gate_pre * sigma
            act = silu * up_pre
            gate = column(gates, expert)
            grad_gate = jnp.where(
                lanes == expert, jnp.sum(act * back, axis=1, keepdims=True), grad_gate
            )
            grad_act = gate * back
            grad_pre = grad_act * up_pre * sigma * (1.0 + gate_pre * (1.0 - sigma))
            grad_up = grad_act * silu
            grad_both = jnp.concatenate([grad_pre.astype(BF), grad_up.astype(BF)], axis=1)
            dgu_ref[j] = grad_both
            ga_ref[:, j * ff : (j + 1) * ff] = (gate * act).astype(BF)
            gate_up = jnp.concatenate(
                [w_ref[:, 0, j].reshape(width, ff), w_ref[:, 1, j].reshape(width, ff)], axis=1
            )
            part = dot_nt(grad_both, gate_up)
            out = part if out is None else out + part

        @pl.when(step == 0)
        def _():
            total[...] = out
            total_gate[...] = grad_gate

        @pl.when(step > 0)
        def _():
            total[...] += out
            total_gate[...] += grad_gate

        @pl.when(step == pl.num_programs(0) - 1)
        def _():
            rows = group // 4
            for shift in range(4):
                place = own_rows(lax.rem(sref[0] + shift, 4), rows)
                pieces[shift][:, :width] = total[place, :].astype(BF)
                pieces[shift][:, width:] = total_gate[place, :].astype(BF)


def experts_backward(scalars, given, gates, gu, w, after):
    dp, _, experts, dr, ff = w.shape
    group = gates.shape[0]
    width = dp * dr
    piece = (group // 4, width + LANES)
    return pl.pallas_call(
        lambda *refs: experts_backward_kernel(len(after), *refs),
        grid_spec=pltpu.PrefetchScalarGridSpec(
            num_scalar_prefetch=1,
            grid=(experts // PER_STEP,),
            in_specs=anywhere(len(after))
            + [whole(x.shape) for x in given]
            + [
                whole((group, experts)),
                pl.BlockSpec((PER_STEP, group, 2 * ff), lambda i, s: (i * s[1], 0, 0)),
                pl.BlockSpec((dp, 3, PER_STEP, dr, ff), lambda i, s: (0, 0, i * s[1], 0, 0)),
            ],
            out_specs=[whole(piece)] * 4
            + [
                whole((group, width)),
                pl.BlockSpec((PER_STEP, group, 2 * ff), lambda i, s: (i * s[1], 0, 0)),
                pl.BlockSpec((group, PER_STEP * ff), lambda i, s: (0, i * s[1])),
            ],
            scratch_shapes=[pltpu.VMEM((group, width), F32), pltpu.VMEM((group, LANES), F32)],
        ),
        out_shape=[jax.ShapeDtypeStruct(piece, BF)] * 4
        + [
            jax.ShapeDtypeStruct((group, width), BF),
            jax.ShapeDtypeStruct((experts, group, 2 * ff), BF),
            jax.ShapeDtypeStruct((group, experts * ff), BF),
        ],
        compiler_params=params(),
        cost_estimate=pl.CostEstimate(
            flops=2 * group * width * ff * 3 * experts,
            bytes_accessed=w.size * 2 + 5 * experts * group * ff * 2,
            transcendentals=experts * group * ff,
        ),
        name="experts_backward",
    )(scalars, *after, *given, gates, gu, w)


def middle_kernel(n_after, sref, *refs):
    refs = refs[n_after:]
    pieces, refs = refs[:4], refs[4:]
    grad_ref, hown_ref, gates_ref, b_ref, gains_ref, router_ref, dh_ref, do_ref, small_ref = refs
    rows, width = grad_ref.shape

    @pl.when(sref[1] > 0)
    def _():
        place = own_rows(sref[0], rows)
        joined = pieces[0][...].astype(F32)
        for shift in range(1, 4):
            joined = joined + pieces[shift][...].astype(F32)
        grad_normed = joined[:, :width]
        grad_gate = joined[:, width : width + E]
        gates = gates_ref[place, :]
        grad_logits = (
            gates * (grad_gate - jnp.sum(gates * grad_gate, axis=1, keepdims=True))
        ).astype(BF)
        normed = b_ref[place, :]
        grad_normed = grad_normed + dot_nt(grad_logits, router_ref[:, :E])
        hidden = hown_ref[...]
        part, grad_gain = norm_back(hidden, rms_scale(hidden), gains_ref[1:2, :], grad_normed)
        grad_hidden = grad_ref[...].astype(F32) + part
        dh_ref[...] = grad_hidden
        do_ref[...] = grad_hidden.astype(BF)
        small_ref[0:E, :] = dot_tn(grad_logits, normed)
        small_ref[E : E + 1, :] = grad_gain
        small_ref[E + 1 :, :] = jnp.zeros((small_ref.shape[0] - E - 1, width), F32)


def middle(scalars, pieces, grad_own, hown, gates, b, gains, router, after):
    rows, width = grad_own.shape
    operands = [*pieces, grad_own, hown, gates, b, gains, router]
    return pl.pallas_call(
        lambda *refs: middle_kernel(len(after), *refs),
        grid_spec=pltpu.PrefetchScalarGridSpec(
            num_scalar_prefetch=1,
            grid=(1,),
            in_specs=anywhere(len(after)) + [whole(x.shape) for x in operands],
            out_specs=[whole((rows, width)), whole((rows, width)), whole((24, width))],
        ),
        out_shape=[
            jax.ShapeDtypeStruct((rows, width), F32),
            jax.ShapeDtypeStruct((rows, width), BF),
            jax.ShapeDtypeStruct((24, width), F32),
        ],
        compiler_params=params(),
        cost_estimate=pl.CostEstimate(
            flops=rows * width * 64, bytes_accessed=rows * width * 24, transcendentals=rows
        ),
        name="norm_backward",
    )(scalars, *after, *operands)


def attention_backward_kernel(n_after, sref, *refs):
    pieces, refs = refs[:4], refs[4:]
    sources, refs = refs[:9], refs[9 + n_after :]
    (
        dh_ref, xown_ref, small_ref, gains_ref, cos_ref, sin_ref, bias_ref, qkv_ref, lse_ref,
        dx_ref, dxlow_ref, small_out_ref, full_ref, dqkv_ref,
        now, buffers, sems,
    ) = refs
    me = sref[0]
    shard = dh_ref.shape[0]

    @pl.when(sref[1] > 0)
    def _():
        copies = fetches(sref[2], sources, buffers, sems)
        for copy in copies[0]:
            copy.start()
        assemble(me, pieces, full_ref)
        bias = bias_ref[...]
        lse = lse_ref[...]
        cos = jnp.concatenate([cos_ref[...]] * 3, axis=1)
        sin = jnp.concatenate([sin_ref[...]] * 3, axis=1)
        total = jnp.zeros((shard, full_ref.shape[1]), F32)
        for step in range(4):
            for copy in copies[step]:
                copy.wait()
            for copy in copies[step + 1] if step < 3 else []:
                copy.start()
            w_qkv, w_out = group_weights(buffers, step)
            do = dot(full_ref[...], w_out).astype(BF)
            qkv = qkv_ref[step]
            q, k, v = qkv[:, :256], qkv[:, 256:384], qkv[:, 384:]
            q_turned = q.T
            do_turned = do.T
            dq, dk, dv = [], [], []
            for kv in range(2):
                k_one = k[:, kv * HD : (kv + 1) * HD]
                v_one = v[:, kv * HD : (kv + 1) * HD]
                dk_one = dv_one = None
                for head in (2 * kv, 2 * kv + 1):
                    part = slice(head * HD, (head + 1) * HD)
                    scores = dot_nt(q[:, part], k_one) + bias
                    soft = jnp.exp(scores - lse[:, 4 * step + head : 4 * step + head + 1])
                    grad_soft = dot_nt(do[:, part], v_one)
                    grad_scores = soft * (
                        grad_soft - jnp.sum(soft * grad_soft, axis=1, keepdims=True)
                    )
                    grad_scores = grad_scores.astype(BF)
                    dq.append(dot(grad_scores, k_one))
                    dk_part = dot(q_turned[part, :], grad_scores)
                    dv_part = dot(do_turned[part, :], soft.astype(BF))
                    dk_one = dk_part if dk_one is None else dk_one + dk_part
                    dv_one = dv_part if dv_one is None else dv_one + dv_part
                dk.append(dk_one)
                dv.append(dv_one)
            grad_k = jnp.concatenate(dk, axis=0).T
            grad_v = jnp.concatenate(dv, axis=0).T
            grad_qk = jnp.concatenate([jnp.concatenate(dq, axis=1) * HD**-0.5, grad_k], axis=1)
            grad_qk = (grad_qk * cos - swap_halves(grad_qk) * sin).astype(BF)
            now[step, :, :384] = grad_qk
            now[step, :, 384:] = grad_v.astype(BF)
            if step == 0:
                dqkv_ref[...] = now[0]
            total += dot_nt(now[step, own_rows(me, shard), :], w_qkv)

        entering = xown_ref[...].astype(F32)
        part, grad_gain = norm_back(entering, rms_scale(entering), gains_ref[0:1, :], total)
        grad_entering = dh_ref[...] + part
        dx_ref[...] = grad_entering
        dxlow_ref[...] = grad_entering.astype(BF)
        rows = lax.broadcasted_iota(jnp.int32, small_ref.shape, 0)
        small_out_ref[...] = jnp.where(rows == E + 1, grad_gain, small_ref[...])


def attention_backward(
    scalars, pieces, dh, xown, small, gains, tables, qkv, lse, w_attn, after
):
    shard, width = dh.shape
    group = 4 * shard
    dp = width // 64
    cos, sin, bias = tables
    smalls = [dh, xown, small, gains, cos, sin, bias]
    per_step = lambda i, s: (i * s[1], 0, 0)
    outs = [
        ((shard, width), F32),
        ((shard, width), BF),
        (small.shape, F32),
        ((group, width), BF),
        ((group, 512), BF),
    ]
    return pl.pallas_call(
        lambda *refs: attention_backward_kernel(len(after), *refs),
        grid_spec=pltpu.PrefetchScalarGridSpec(
            num_scalar_prefetch=1,
            grid=(1,),
            in_specs=[whole(x.shape) for x in pieces]
            + anywhere(9 + len(after))
            + [whole(x.shape) for x in smalls]
            + [whole(qkv.shape), whole(lse.shape)],
            out_specs=[whole(shape) for shape, _ in outs],
            scratch_shapes=[
                pltpu.VMEM((4, group, 512), BF),
                pltpu.VMEM((4, dp, 400, LANES), BF),
                pltpu.SemaphoreType.DMA((9,)),
            ],
        ),
        out_shape=[jax.ShapeDtypeStruct(shape, kind) for shape, kind in outs],
        compiler_params=params(),
        cost_estimate=pl.CostEstimate(
            flops=group * width * 1024 * 2 + 16 * 10 * group * group * HD,
            bytes_accessed=width * 768 * 8 + 6 * group * width * 2,
            transcendentals=16 * group * group,
        ),
        name="attention_backward",
    )(scalars, *pieces, *w_attn, *after, *smalls, qkv, lse)


def expert_weights_kernel(n_after, sref, *refs):
    refs = refs[n_after:]
    b, refs = refs[:4], refs[4:]
    g, refs = refs[:4], refs[4:]
    dgu, refs = refs[:4], refs[4:]
    ga, refs = refs[:4], refs[4:]
    out_ref, bt_ref, gt_ref = refs
    group = b[0].shape[0]
    dp, _, _, dr, ff = out_ref.shape
    first = sref[1] > 0

    def chosen(four, micro, *index):
        index = index or (Ellipsis,)
        return jnp.where(first, four[micro][index], four[2 + micro][index])

    @pl.when(pl.program_id(0) == 0)
    def _():
        for micro in range(2):
            place = slice(micro * group, (micro + 1) * group)
            bt_ref[:, place] = chosen(b, micro).T
            gt_ref[:, place] = chosen(g, micro).T

    bt = bt_ref[...]
    for j in range(PER_GRAD):
        rows = jnp.concatenate([chosen(dgu, 0, j), chosen(dgu, 1, j)], axis=0)
        grads = dot(bt, rows).astype(BF)
        out_ref[:, 0, j] = grads[:, :ff].reshape(dp, dr, ff)
        out_ref[:, 1, j] = grads[:, ff:].reshape(dp, dr, ff)
    rows = jnp.concatenate([chosen(ga, 0), chosen(ga, 1)], axis=0)
    grads = dot(gt_ref[...], rows).astype(BF)
    for j in range(PER_GRAD):
        out_ref[:, 2, j] = grads[:, j * ff : (j + 1) * ff].reshape(dp, dr, ff)


def expert_weights(scalars, rows_b, grads, dgus, gas, dp, after):
    group, width = rows_b[0].shape
    experts, _, ff2 = dgus[0].shape
    ff = ff2 // 2
    dr = width // dp
    square = whole((group, width))
    wide, flat = [], []
    for held in (lambda s: s[1], lambda s: 1 - s[1]):
        wide += [
            pl.BlockSpec((PER_GRAD, group, ff2), lambda i, s, held=held: (i * held(s), 0, 0))
        ] * 2
        flat += [pl.BlockSpec((group, PER_GRAD * ff), lambda i, s, held=held: (0, i * held(s)))] * 2
    return pl.pallas_call(
        lambda *refs: expert_weights_kernel(len(after), *refs),
        grid_spec=pltpu.PrefetchScalarGridSpec(
            num_scalar_prefetch=1,
            grid=(experts // PER_GRAD,),
            in_specs=anywhere(len(after)) + [square] * 8 + wide + flat,
            out_specs=pl.BlockSpec((dp, 3, PER_GRAD, dr, ff), lambda i, s: (0, 0, i, 0, 0)),
            scratch_shapes=[
                pltpu.VMEM((width, 2 * group), BF),
                pltpu.VMEM((width, 2 * group), BF),
            ],
        ),
        out_shape=jax.ShapeDtypeStruct((dp, 3, experts, dr, ff), BF),
        compiler_params=params(),
        cost_estimate=pl.CostEstimate(
            flops=4 * group * width * ff * 3 * experts,
            bytes_accessed=dp * 3 * experts * dr * ff * 2 + 6 * experts * group * ff * 2,
            transcendentals=0,
        ),
        name="expert_weight_grads",
    )(scalars, *after, *rows_b, *grads, *dgus, *gas)


def attention_weights_kernel(sref, *refs):
    a, o, f, d, small = (refs[4 * j : 4 * j + 4] for j in range(5))
    out_ref = refs[20]
    dp = out_ref.shape[0]
    first = sref[1] > 0

    def chosen(four, micro):
        return jnp.where(first, four[micro][...], four[2 + micro][...])

    sums = dot_tn(chosen(a, 0), chosen(d, 0)) + dot_tn(chosen(a, 1), chosen(d, 1))
    for j in range(4):
        out_ref[:, 64 * j : 64 * (j + 1), :] = (
            sums[:, LANES * j : LANES * (j + 1)].astype(BF).reshape(dp, 64, LANES)
        )
    sums = dot_tn(chosen(f, 0), chosen(o, 0)) + dot_tn(chosen(f, 1), chosen(o, 1))
    for j in range(2):
        out_ref[:, 64 * (4 + j) : 64 * (5 + j), :] = (
            sums[:, LANES * j : LANES * (j + 1)].astype(BF).reshape(dp, 64, LANES)
        )
    rows = chosen(small, 0) + chosen(small, 1)
    rows = jnp.concatenate(
        [rows, jnp.zeros((LANES - rows.shape[0], rows.shape[1]), F32)], axis=0
    )
    out_ref[:, 384:, :] = rows.T.astype(BF).reshape(dp, 64, LANES)


def attention_weights(scalars, a, o, f, d, small, dp):
    group, width = a[0].shape
    operands = [*a, *o, *f, *d, *small]
    return pl.pallas_call(
        attention_weights_kernel,
        grid_spec=pltpu.PrefetchScalarGridSpec(
            num_scalar_prefetch=1,
            grid=(1,),
            in_specs=[whole(x.shape) for x in operands],
            out_specs=whole((dp, 448, LANES)),
        ),
        out_shape=jax.ShapeDtypeStruct((dp, 448, LANES), BF),
        compiler_params=params(),
        cost_estimate=pl.CostEstimate(
            flops=4 * group * width * 768,
            bytes_accessed=group * width * 14 + width * 768 * 2,
            transcendentals=0,
        ),
        name="attention_weight_grads",
    )(scalars, *operands)


def moved(array, shift):
    return lax.ppermute(array, "tensor", [(i, (i + shift) % 4) for i in range(4)])


def swapped(array, dp):
    return lax.ppermute(array, "dp", [(i, i ^ 1) for i in range(dp)])


def to_owner(pieces):
    return [pieces[0]] + [moved(pieces[s], s) for s in range(1, 4)]


def to_all(rows):
    return [rows] + [moved(rows, s) for s in range(1, 4)]


def across(rows, up):
    start, end = (0, 4) if up else (4, 0)
    return [
        lax.ppermute(
            rows, ("pipe", "tensor"), [(start + i, end + (i + s) % 4) for i in range(4)]
        )
        for s in range(4)
    ]


def tables_of(lengths, group):
    ends = jnp.cumsum(lengths)
    starts = ends - lengths
    index = jnp.arange(group, dtype=jnp.int32)
    inside = index[:, None] >= starts[None, :]
    start = jnp.max(jnp.where(inside, starts[None, :], 0), axis=1)
    position = (index - start).astype(F32)
    half = HD // 2
    freq = jnp.exp(jnp.arange(half, dtype=F32) * (-2.0 * math.log(10000.0) / HD))
    angle = position[:, None] * freq[None, :]
    cos, sin = jnp.cos(angle), jnp.sin(angle)
    visible = (index[None, :] <= index[:, None]) & (index[None, :] >= start[:, None])
    bias = jnp.where(visible, 0.0, MASKED).astype(F32)
    return (
        jnp.concatenate([cos, cos, cos, cos], axis=1),
        jnp.concatenate([-sin, sin, -sin, sin], axis=1),
        bias,
    )


def per_device(
    inputs, cotangent, doc_lengths, routes, norm_attn, w_query, w_key, w_value, w_out,
    w_router, norm_ffn, w_gate, w_up, w_down,
):
    section = lax.axis_index("pipe")
    first_section = section == 0
    me = lax.axis_index("tensor")
    dp = lax.axis_size("dp")
    core = lax.axis_index("dp") % 2
    micro = inputs.shape[0]
    shard, width = inputs.shape[1:]
    group = shard * 4
    rows_dp = width // dp
    scalars = [
        jnp.stack([me, (section == s).astype(jnp.int32), core]).astype(jnp.int32)
        for s in range(2)
    ]

    out_turned = w_out[0].T
    small = jnp.concatenate([w_router[0], norm_attn[0][:, None], norm_ffn[0][:, None]], axis=1)
    small = jnp.pad(small, ((0, 0), (0, LANES - E - 2)))
    piece = jnp.concatenate(
        [
            w_query[0][:, :LANES], w_query[0][:, LANES:], w_key[0], w_value[0],
            out_turned[:, :LANES], out_turned[:, LANES:], small,
        ],
        axis=0,
    )
    w_own = jnp.broadcast_to(piece[None], (dp,) + piece.shape)
    w_own = lax.all_to_all(w_own, "dp", 0, 0, tiled=True)
    pieces_w = jnp.stack([w_gate[0], w_up[0], w_down[0].transpose(0, 2, 1)])
    w_experts = lax.all_gather(pieces_w, "dp", axis=0)
    tables = [tables_of(doc_lengths[m, 0], group) for m in range(micro)]
    tables, inputs, cotangent = lax.optimization_barrier((tables, inputs, cotangent))
    rows_in, rows_cot = to_all(inputs), to_all(cotangent)
    rows_in, rows_cot, w_own = lax.optimization_barrier((rows_in, rows_cot, w_own))
    rows_in = [[part[m] for part in rows_in] for m in range(micro)]
    rows_cot = [[part[m] for part in rows_cot] for m in range(micro)]
    half, quarter = dp // 2, dp // 4
    mine = lax.dynamic_slice_in_dim(w_own, core * half, half, 0)
    w_next, w_last = moved(mine, 1), moved(mine, 3)
    w_over = [moved(w_next[:quarter], 1), moved(w_last[quarter:], 3)]
    other = [swapped(x, dp) for x in (w_next, w_last, *w_over)]
    w_attn = [w_own, w_next, other[0], *w_over, other[2], other[3], w_last, other[1]]
    w_attn, rows_in, rows_cot = lax.optimization_barrier((w_attn, rows_in, rows_cot))
    router, gains = smalls_of(scalars[0], w_attn)

    ids = jnp.arange(E, dtype=jnp.int32)
    picked = jnp.any(routes[0][..., None] == ids, axis=2).astype(F32)

    after = []
    saves = [[None] * micro, [None] * micro]
    firsts = [[None] * micro, [None] * micro]
    middles = [[None] * micro, [None] * micro]
    lasts = [[None] * micro, [None] * micro]

    def attend(s, m, pieces):
        nonlocal after
        out = attention_forward(
            scalars[s], pieces, gains, tables[m], picked[m], w_attn, router, after
        )
        saves[s][m] = list(out)
        after = [out[6]]

    def expert(s, m):
        nonlocal after
        b, gates = saves[s][m][6:8]
        *parts, gu = experts_forward(scalars[s], b, gates, w_experts, after)
        saves[s][m].append(gu)
        after = [gu]
        return parts

    def layer(s, m, pieces):
        nonlocal after
        kept, parts, gu = layer_forward(
            scalars[s], pieces, gains, tables[m], picked[m], w_attn, router, w_experts, after
        )
        saves[s][m] = [*kept, gu]
        after = [gu]
        return parts

    def expert_back(s, m, pieces):
        nonlocal after
        gates, gu = saves[s][m][7:9]
        *parts, grad, dgu, ga = experts_backward(
            scalars[s], pieces, gates, gu, w_experts, after
        )
        after = [grad]
        firsts[s][m] = (to_owner(parts), grad, dgu, ga)

    def norm_between(s, m, own):
        nonlocal after
        kept = saves[s][m]
        dh, do, small = middle(
            scalars[s], firsts[s][m][0], own, kept[5], kept[7], kept[6], gains, router, after
        )
        middles[s][m] = (dh, to_all(do), small)
        after = [do]

    def attend_back(s, m):
        nonlocal after
        kept = saves[s][m]
        dh, rows, small = middles[s][m]
        dx, dx_low, small, full, dqkv = attention_backward(
            scalars[s], rows, dh, kept[1], small, gains, tables[m], kept[2], kept[4],
            w_attn, after,
        )
        lasts[s][m] = (small, full, dqkv, dx)
        after = [dx]
        return dx_low

    def layer_sum(parts, hown):
        return finish(to_owner(parts), hown)

    attend(0, 0, rows_in[0])
    first_out = layer_sum(expert(0, 0), saves[0][0][5])
    first_in = across(first_out, True)
    after = [first_out]
    attend(0, 1, rows_in[1])
    late = [layer(1, 0, first_in)]
    second_out = layer_sum(expert(0, 1), saves[0][1][5])
    second_in = across(second_out, True)
    expert_back(1, 0, rows_cot[0])
    late.append(layer(1, 1, second_in))
    norm_between(1, 0, cotangent[0])
    expert_back(1, 1, rows_cot[1])
    first_back = across(attend_back(1, 0), False)
    norm_between(1, 1, cotangent[1])
    expert_back(0, 0, first_back)
    second_back = across(attend_back(1, 1), False)
    norm_between(0, 0, first_back[0])
    expert_back(0, 1, second_back)
    joined = firsts[0] + firsts[1]
    grad_experts = expert_weights(
        scalars[0],
        [saves[s][m][6] for s in range(2) for m in range(micro)],
        [x[1] for x in joined],
        [x[2] for x in joined],
        [x[3] for x in joined],
        dp,
        after,
    )
    expert_sums = lax.psum_scatter(grad_experts, "dp", scatter_dimension=0, tiled=True)[0]
    after = [grad_experts]
    norm_between(0, 1, second_back[0])
    attend_back(0, 0)
    attend_back(0, 1)
    late, _ = lax.optimization_barrier((late, lasts[1][1][3]))
    outputs = [
        [first_out, second_out],
        [layer_sum(late[m], saves[1][m][5]) for m in range(micro)],
    ]
    grads_in = [[lasts[s][m][3] for m in range(micro)] for s in range(2)]

    joined = lasts[0] + lasts[1]
    grad_attn = attention_weights(
        scalars[0],
        [saves[s][m][0] for s in range(2) for m in range(micro)],
        [saves[s][m][3] for s in range(2) for m in range(micro)],
        [x[1] for x in joined],
        [x[2] for x in joined],
        [x[0] for x in joined],
        dp,
    )
    grad_attn = lax.all_to_all(grad_attn, "dp", 0, 0, tiled=True)
    attn_sums = jnp.sum(grad_attn.astype(F32), axis=0)
    small = attn_sums[384:].reshape(4, 16, LANES)
    small_own = None
    for shift in range(4):
        part = lax.dynamic_index_in_dim(small, (me + shift) % 4, 0, keepdims=False)
        part = moved(part, shift) if shift else part
        small_own = part if small_own is None else small_own + part
    expert_sums = expert_sums.astype(F32)
    blocks = [attn_sums[64 * j : 64 * (j + 1)] for j in range(6)]
    section_rows = jnp.stack(
        [jnp.where(first_section, outputs[0][m], outputs[1][m]) for m in range(micro)]
    )
    grad_in = jnp.stack(
        [jnp.where(first_section, grads_in[0][m], grads_in[1][m]) for m in range(micro)]
    )
    return (
        section_rows[None],
        grad_in[None],
        small_own[:, E + 1][None],
        jnp.concatenate(blocks[:2], axis=1)[None],
        blocks[2][None],
        blocks[3][None],
        jnp.concatenate(blocks[4:], axis=1).T[None],
        small_own[:, :E][None],
        small_own[:, E][None],
        expert_sums[0][None],
        expert_sums[1][None],
        expert_sums[2].transpose(0, 2, 1)[None],
    )


def finish(parts, hown):
    result = hown
    for part in parts:
        result = result + part.astype(F32)
    return result.astype(BF)


def solution(mesh):
    in_specs = (
        P(None, ("dp", "tensor"), None),
        P(None, ("dp", "tensor"), None),
        P(None, "dp", None),
        P("pipe", None, "dp", None),
        P("pipe", ("dp", "tensor")),
        P("pipe", "dp", "tensor"),
        P("pipe", "dp", "tensor"),
        P("pipe", "dp", "tensor"),
        P("pipe", "tensor", "dp"),
        P("pipe", ("dp", "tensor"), None),
        P("pipe", ("dp", "tensor")),
        P("pipe", None, "dp", "tensor"),
        P("pipe", None, "dp", "tensor"),
        P("pipe", None, "tensor", "dp"),
    )
    out_specs = (
        P("pipe", None, ("dp", "tensor"), None),
        P("pipe", None, ("dp", "tensor"), None),
        P("pipe", ("dp", "tensor")),
        P("pipe", "dp", "tensor"),
        P("pipe", "dp", "tensor"),
        P("pipe", "dp", "tensor"),
        P("pipe", "tensor", "dp"),
        P("pipe", ("dp", "tensor"), None),
        P("pipe", ("dp", "tensor")),
        P("pipe", None, "dp", "tensor"),
        P("pipe", None, "dp", "tensor"),
        P("pipe", None, "tensor", "dp"),
    )
    return jax.shard_map(
        per_device, mesh=mesh, in_specs=in_specs, out_specs=out_specs, check_vma=False
    )
```

```python
import math

import jax
import jax.numpy as jnp
from jax import lax
from jax.experimental import pallas as pl
from jax.experimental.pallas import tpu as pltpu
from jax.sharding import PartitionSpec as P

HD = 64
E = 16
TOP = 8
EPSILON = 1e-06
MASKED = -1000000000.0
BF = jnp.bfloat16
F32 = jnp.float32
VMEM_LIMIT = 56 * 1024 * 1024
PER = 4
PER_STEP = 8
PER_GRAD = 4
LANES = 128


def params():
    return pltpu.CompilerParams(
        vmem_limit_bytes=VMEM_LIMIT, dimension_semantics=("arbitrary",)
    )


def dot(left, right):
    return jnp.dot(left, right, preferred_element_type=F32)


def dot_nt(left, right):
    return lax.dot_general(
        left, right, (((1,), (1,)), ((), ())), preferred_element_type=F32
    )


def dot_tn(left, right):
    return lax.dot_general(
        left, right, (((0,), (0,)), ((), ())), preferred_element_type=F32
    )


def column(rows, index):
    lanes = lax.broadcasted_iota(jnp.int32, rows.shape, 1)
    return jnp.sum(jnp.where(lanes == index, rows, 0.0), axis=1, keepdims=True)


def whole(shape):
    return pl.BlockSpec(shape, lambda i, s: (0,) * len(shape))


def rms_scale(values):
    return lax.rsqrt(jnp.mean(values * values, axis=-1, keepdims=True) + EPSILON)


def norm_back(values, scale_rows, gain, grad_normed):
    weighted = grad_normed * gain
    grad_values = scale_rows * weighted - values * scale_rows**3 * jnp.mean(
        weighted * values, axis=-1, keepdims=True
    )
    grad_gain = jnp.sum(grad_normed * values * scale_rows, axis=0, keepdims=True)
    return grad_values, grad_gain


def swap_halves(values):
    width = values.shape[1]
    lanes = lax.broadcasted_iota(jnp.int32, values.shape, 1)
    ahead = pltpu.roll(values, width - HD // 2, 1)
    behind = pltpu.roll(values, HD // 2, 1)
    return jnp.where(lanes % HD < HD // 2, ahead, behind)


def assemble(me, pieces, target):
    rows = pieces[0].shape[0]
    for shift in range(4):
        owner = lax.rem(me + 4 - shift, 4)
        target[own_rows(owner, rows), :] = pieces[shift][...]


def own_rows(me, rows):
    return pl.ds(pl.multiple_of(me * rows, rows), rows)


def anywhere(count):
    return [pl.BlockSpec(memory_space=pl.ANY)] * count


def fetches(core, sources, buffers, sems):
    dp = buffers.shape[1]
    half, quarter = dp // 2, dp // 4
    here, there = core * half, (1 - core) * half
    copies = [[pltpu.make_async_copy(sources[0], buffers.at[0], sems.at[0])]]
    number = 1
    for shift, starts in (
        (1, (here, there)),
        (2, (here, here + quarter, there, there + quarter)),
        (3, (here, there)),
    ):
        group = []
        for start in starts:
            source = sources[number]
            place = buffers.at[shift, pl.ds(start, source.shape[0])]
            group.append(pltpu.make_async_copy(source, place, sems.at[number]))
            number += 1
        copies.append(group)
    return copies


def group_weights(buffers, step):
    dp = buffers.shape[1]
    blocks = [
        buffers[step, :, 64 * j : 64 * (j + 1), :].reshape(dp * 64, LANES) for j in range(6)
    ]
    return jnp.concatenate(blocks[:4], axis=1), jnp.concatenate(blocks[4:], axis=1)


def smalls_kernel(sref, *refs):
    sources, (router_ref, gains_ref, stage, sems) = refs[:9], refs[9:]
    dp = stage.shape[0]
    half, quarter = dp // 2, dp // 4
    me = sref[0]
    here, there = sref[2] * half, (1 - sref[2]) * half
    places = (
        (0, 0), (1, here), (1, there),
        (2, here), (2, here + quarter), (2, there), (2, there + quarter), (3, here), (3, there),
    )
    copies = []
    for number, (shift, start) in enumerate(places):
        source = sources[number]
        owner = lax.rem(me + 4 - shift, 4)
        copies.append(
            pltpu.make_async_copy(
                source.at[:, pl.ds(384, 16)],
                stage.at[pl.ds(start, source.shape[0]), owner],
                sems.at[number],
            )
        )
    for copy in copies:
        copy.start()
    for copy in copies:
        copy.wait()
    rows = stage[...].reshape(dp * 64, LANES)
    router_ref[...] = rows
    turned = rows.astype(F32).T
    gains_ref[...] = turned[E : E + 8, :]


def smalls_of(scalars, w_attn):
    dp = w_attn[0].shape[0]
    width = dp * 64
    return pl.pallas_call(
        smalls_kernel,
        grid_spec=pltpu.PrefetchScalarGridSpec(
            num_scalar_prefetch=1,
            grid=(1,),
            in_specs=anywhere(9),
            out_specs=[whole((width, LANES)), whole((8, width))],
            scratch_shapes=[pltpu.VMEM((dp, 4, 16, LANES), BF), pltpu.SemaphoreType.DMA((9,))],
        ),
        out_shape=[
            jax.ShapeDtypeStruct((width, LANES), BF),
            jax.ShapeDtypeStruct((8, width), F32),
        ],
        compiler_params=params(),
        name="router_and_gains",
    )(scalars, *w_attn)


def attention_forward_kernel(n_after, sref, *refs):
    pieces, refs = refs[:4], refs[4:]
    sources, refs = refs[:9], refs[9 + n_after :]
    (
        gains_ref, cos_ref, sin_ref, bias_ref, picked_ref, router_ref,
        a_ref, xown_ref, qkv_ref, o_ref, lse_ref, hown_ref, b_ref, gates_ref,
        hidden, buffers, sems,
    ) = refs
    step = pl.program_id(0)
    me = sref[0]
    group, width = b_ref.shape
    shard = xown_ref.shape[0]

    @pl.when(sref[1] > 0)
    def _():
        copies = fetches(sref[2], sources, buffers, sems)

        @pl.when(step == 0)
        def _():
            for part in copies:
                for copy in part:
                    copy.start()
            assemble(me, pieces, b_ref)
            entering = b_ref[...].astype(F32)
            a_ref[...] = (entering * rms_scale(entering) * gains_ref[0:1, :]).astype(BF)
            xown_ref[...] = pieces[0][...]
            hidden[...] = entering

        for shift, part in enumerate(copies):

            @pl.when(step == shift)
            def _(part=part):
                for copy in part:
                    copy.wait()

        w_qkv, w_out = group_weights(buffers, step)
        qkv = dot(a_ref[...], w_qkv)
        qk = qkv[:, :384]
        cos = jnp.concatenate([cos_ref[...]] * 3, axis=1)
        sin = jnp.concatenate([sin_ref[...]] * 3, axis=1)
        turned = qk * cos + swap_halves(qk) * sin
        q = (turned[:, :256] * HD**-0.5).astype(BF)
        k = turned[:, 256:].astype(BF)
        v = qkv[:, 384:].astype(BF)
        qkv_ref[0, :, :256] = q
        qkv_ref[0, :, 256:384] = k
        qkv_ref[0, :, 384:] = v
        bias = bias_ref[...]
        lanes = lax.broadcasted_iota(jnp.int32, (group, LANES), 1)
        lse_all = jnp.where(step == 0, 0.0, lse_ref[...])
        outs = []
        for head in range(4):
            kv = head // 2
            scores = dot_nt(q[:, head * HD : (head + 1) * HD], k[:, kv * HD : (kv + 1) * HD])
            scores = scores + bias
            peak = jnp.max(scores, axis=1, keepdims=True)
            soft = jnp.exp(scores - peak)
            total = jnp.sum(soft, axis=1, keepdims=True)
            lse_all = jnp.where(lanes == 4 * step + head, peak + jnp.log(total), lse_all)
            soft = (soft * (1.0 / total)).astype(BF)
            outs.append(dot(soft, v[:, kv * HD : (kv + 1) * HD]))
        mixed = jnp.concatenate(outs, axis=1).astype(BF)

        @pl.when(step == 0)
        def _():
            o_ref[...] = mixed

        lse_ref[...] = lse_all
        hidden[...] += dot_nt(mixed, w_out)

        @pl.when(step == pl.num_programs(0) - 1)
        def _():
            rows = hidden[...]
            normed = (rows * rms_scale(rows) * gains_ref[1:2, :]).astype(BF)
            b_ref[...] = normed
            hown_ref[...] = hidden[own_rows(me, shard), :]
            logits = dot(normed, router_ref[...])[:, :E]
            picked = picked_ref[...]
            peak = jnp.max(jnp.where(picked > 0, logits, -1e30), axis=1, keepdims=True)
            powers = jnp.where(picked > 0, jnp.exp(jnp.minimum(logits - peak, 0.0)), 0.0)
            gates_ref[...] = powers / jnp.sum(powers, axis=1, keepdims=True)


def attention_forward(scalars, pieces, gains, tables, picked, w_attn, router, after):
    shard, width = pieces[0].shape
    group = 4 * shard
    dp = width // 64
    cos, sin, bias = tables
    smalls = [gains, cos, sin, bias, picked, router]
    per_step = lambda i, s: (i * s[1], 0, 0)
    outs = [
        ((group, width), BF, None),
        ((shard, width), BF, None),
        ((4, group, 512), BF, (1, group, 512)),
        ((group, 256), BF, None),
        ((group, LANES), F32, None),
        ((shard, width), F32, None),
        ((group, width), BF, None),
        ((group, E), F32, None),
    ]
    return pl.pallas_call(
        lambda *refs: attention_forward_kernel(len(after), *refs),
        grid_spec=pltpu.PrefetchScalarGridSpec(
            num_scalar_prefetch=1,
            grid=(4,),
            in_specs=[whole(x.shape) for x in pieces]
            + anywhere(9 + len(after))
            + [whole(x.shape) for x in smalls],
            out_specs=[
                whole(shape) if block is None else pl.BlockSpec(block, per_step)
                for shape, _, block in outs
            ],
            scratch_shapes=[
                pltpu.VMEM((group, width), F32),
                pltpu.VMEM((4, dp, 400, LANES), BF),
                pltpu.SemaphoreType.DMA((9,)),
            ],
        ),
        out_shape=[jax.ShapeDtypeStruct(shape, kind) for shape, kind, _ in outs],
        compiler_params=params(),
        cost_estimate=pl.CostEstimate(
            flops=2 * group * width * 768 * 4 + 16 * 4 * group * group * HD,
            bytes_accessed=width * 768 * 8 + 6 * group * width * 2,
            transcendentals=16 * group * group,
        ),
        name="attention_forward",
    )(scalars, *pieces, *w_attn, *after, *smalls)

def attention_part(
    sref, pieces, sources,
    gains_ref, cos_ref, sin_ref, bias_ref, picked_ref, router_ref,
    a_ref, xown_ref, qkv_ref, o_ref, lse_ref, hown_ref, b_ref, gates_ref,
    hidden, buffers, sems,
):
    me = sref[0]
    group, width = b_ref.shape
    shard = xown_ref.shape[0]

    copies = fetches(sref[2], sources, buffers, sems)
    for copy in copies[0]:
        copy.start()
    assemble(me, pieces, b_ref)
    entering = b_ref[...].astype(F32)
    a_ref[...] = (entering * rms_scale(entering) * gains_ref[0:1, :]).astype(BF)
    xown_ref[...] = pieces[0][...]
    hidden[...] = entering
    cos = jnp.concatenate([cos_ref[...]] * 3, axis=1)
    sin = jnp.concatenate([sin_ref[...]] * 3, axis=1)
    bias = bias_ref[...]
    lanes = lax.broadcasted_iota(jnp.int32, (group, LANES), 1)
    lse_all = jnp.zeros((group, LANES), F32)
    for step in range(4):
        for copy in copies[step]:
            copy.wait()
        for copy in copies[step + 1] if step < 3 else []:
            copy.start()
        w_qkv, w_out = group_weights(buffers, step)
        qkv = dot(a_ref[...], w_qkv)
        qk = qkv[:, :384]
        turned = qk * cos + swap_halves(qk) * sin
        q = (turned[:, :256] * HD**-0.5).astype(BF)
        k = turned[:, 256:].astype(BF)
        v = qkv[:, 384:].astype(BF)
        qkv_ref[step, :, :256] = q
        qkv_ref[step, :, 256:384] = k
        qkv_ref[step, :, 384:] = v
        outs = []
        for head in range(4):
            kv = head // 2
            scores = dot_nt(
                q[:, head * HD : (head + 1) * HD], k[:, kv * HD : (kv + 1) * HD]
            )
            scores = scores + bias
            peak = jnp.max(scores, axis=1, keepdims=True)
            soft = jnp.exp(scores - peak)
            total = jnp.sum(soft, axis=1, keepdims=True)
            lse_all = jnp.where(lanes == 4 * step + head, peak + jnp.log(total), lse_all)
            soft = (soft * (1.0 / total)).astype(BF)
            outs.append(dot(soft, v[:, kv * HD : (kv + 1) * HD]))
        mixed = jnp.concatenate(outs, axis=1).astype(BF)
        if step == 0:
            o_ref[...] = mixed
        hidden[...] += dot_nt(mixed, w_out)
    lse_ref[...] = lse_all
    rows = hidden[...]
    normed = (rows * rms_scale(rows) * gains_ref[1:2, :]).astype(BF)
    b_ref[...] = normed
    hown_ref[...] = hidden[own_rows(me, shard), :]
    logits = dot(normed, router_ref[...])[:, :E]
    picked = picked_ref[...]
    peak = jnp.max(jnp.where(picked > 0, logits, -1e30), axis=1, keepdims=True)
    powers = jnp.where(picked > 0, jnp.exp(jnp.minimum(logits - peak, 0.0)), 0.0)
    gates_ref[...] = powers / jnp.sum(powers, axis=1, keepdims=True)


def chunk(number):
    return pl.ds(PER * number, PER)


def experts_forward_kernel(n_after, sref, *refs):
    (b_ref, gate_ref, w_ref, *refs) = refs[n_after:]
    pieces, (gu_ref, total) = refs[:4], refs[4:]
    step = pl.program_id(0)
    width = b_ref.shape[1]
    ff = w_ref.shape[-1]

    @pl.when(sref[1] > 0)
    def _():
        b = b_ref[...]
        gates = gate_ref[...]
        acts, downs = [], []
        for j in range(PER_STEP):
            gate_up = jnp.concatenate(
                [w_ref[:, 0, j].reshape(width, ff), w_ref[:, 1, j].reshape(width, ff)], axis=1
            )
            both = dot(b, gate_up)
            gu_ref[j] = both.astype(BF)
            gate_pre, up_pre = both[:, :ff], both[:, ff:]
            act = gate_pre * jax.nn.sigmoid(gate_pre) * up_pre
            acts.append((act * column(gates, step * PER_STEP + j)).astype(BF))
            downs.append(w_ref[:, 2, j].reshape(width, ff))
        out = dot_nt(jnp.concatenate(acts, axis=1), jnp.concatenate(downs, axis=1))

        @pl.when(step == 0)
        def _():
            total[...] = out

        @pl.when(step > 0)
        def _():
            total[...] += out

        @pl.when(step == pl.num_programs(0) - 1)
        def _():
            rows = b_ref.shape[0] // 4
            for shift in range(4):
                place = own_rows(lax.rem(sref[0] + shift, 4), rows)
                pieces[shift][...] = total[place, :].astype(BF)


def experts_forward(scalars, b, gates, w, after):
    group, width = b.shape
    dp, _, experts, dr, ff = w.shape
    piece = (group // 4, width)
    return pl.pallas_call(
        lambda *refs: experts_forward_kernel(len(after), *refs),
        grid_spec=pltpu.PrefetchScalarGridSpec(
            num_scalar_prefetch=1,
            grid=(experts // PER_STEP,),
            in_specs=anywhere(len(after))
            + [
                whole((group, width)),
                whole((group, experts)),
                pl.BlockSpec((dp, 3, PER_STEP, dr, ff), lambda i, s: (0, 0, i * s[1], 0, 0)),
            ],
            out_specs=[whole(piece)] * 4
            + [pl.BlockSpec((PER_STEP, group, 2 * ff), lambda i, s: (i * s[1], 0, 0))],
            scratch_shapes=[pltpu.VMEM((group, width), F32)],
        ),
        out_shape=[jax.ShapeDtypeStruct(piece, BF)] * 4
        + [jax.ShapeDtypeStruct((experts, group, 2 * ff), BF)],
        compiler_params=params(),
        cost_estimate=pl.CostEstimate(
            flops=2 * group * width * ff * 3 * experts,
            bytes_accessed=w.size * 2 + experts * group * 2 * ff * 2,
            transcendentals=experts * group * ff,
        ),
        name="experts_forward",
    )(scalars, *after, b, gates, w)


def experts_copies(w_ref, gu_ref, held, gu_held, sems):
    chunks = w_ref.shape[2] // PER
    come = [
        pltpu.make_async_copy(
            w_ref.at[:, :, chunk(c)], held.at[:, :, chunk(c)], sems.at[c]
        )
        for c in range(chunks)
    ]
    leave = [
        pltpu.make_async_copy(gu_held.at[chunk(c)], gu_ref.at[chunk(c)], sems.at[chunks + c])
        for c in range(chunks)
    ]
    return come, leave


def experts_part(sref, come, leave, b_ref, gate_ref, pieces, total, held, gu_held):
    group, width = b_ref.shape
    ff = held.shape[-1]
    chunks = len(come)
    gates = gate_ref[...]
    for c in range(chunks):
        come[c].wait()
        if c + 2 < chunks:
            come[c + 2].start()
        acts, downs = [], []
        for e in range(PER * c, PER * (c + 1)):
            gate_up = jnp.concatenate(
                [held[:, 0, e].reshape(width, ff), held[:, 1, e].reshape(width, ff)], axis=1
            )
            both = dot(b_ref[...], gate_up)
            gu_held[e] = both.astype(BF)
            gate_pre, up_pre = both[:, :ff], both[:, ff:]
            act = gate_pre * jax.nn.sigmoid(gate_pre) * up_pre
            acts.append((act * gates[:, e : e + 1]).astype(BF))
            downs.append(held[:, 2, e].reshape(width, ff))
        leave[c].start()
        out = dot_nt(jnp.concatenate(acts, axis=1), jnp.concatenate(downs, axis=1))
        if c == 0:
            total[...] = out
        else:
            total[...] += out
    rows = group // 4
    for shift in range(4):
        place = own_rows(lax.rem(sref[0] + shift, 4), rows)
        pieces[shift][...] = total[place, :].astype(BF)
    for c in range(chunks):
        leave[c].wait()


def layer_forward_kernel(n_after, sref, *refs):
    pieces, refs = refs[:4], refs[4:]
    sources, refs = refs[:9], refs[9:]
    w_ref, refs = refs[0], refs[1 + n_after :]
    smalls, refs = refs[:6], refs[6:]
    kept, refs = refs[:8], refs[8:]
    parts, refs = refs[:4], refs[4:]
    gu_ref, total, buffers, held, gu_held, sems, expert_sems = refs

    @pl.when(sref[1] > 0)
    def _():
        come, leave = experts_copies(w_ref, gu_ref, held, gu_held, expert_sems)
        come[0].start()
        come[1].start()
        attention_part(sref, pieces, sources, *smalls, *kept, total, buffers, sems)
        experts_part(sref, come, leave, kept[6], kept[7], parts, total, held, gu_held)


def layer_forward(scalars, pieces, gains, tables, picked, w_attn, router, w, after):
    shard, width = pieces[0].shape
    group = 4 * shard
    dp, _, experts, dr, ff = w.shape
    smalls = [gains, *tables, picked, router]
    outs = [
        ((group, width), BF),
        ((shard, width), BF),
        ((4, group, 512), BF),
        ((group, 256), BF),
        ((group, LANES), F32),
        ((shard, width), F32),
        ((group, width), BF),
        ((group, E), F32),
    ] + [((shard, width), BF)] * 4
    gu_shape = (experts, group, 2 * ff)
    out = pl.pallas_call(
        lambda *refs: layer_forward_kernel(len(after), *refs),
        grid_spec=pltpu.PrefetchScalarGridSpec(
            num_scalar_prefetch=1,
            grid=(1,),
            in_specs=[whole(x.shape) for x in pieces]
            + anywhere(10 + len(after))
            + [whole(x.shape) for x in smalls],
            out_specs=[whole(shape) for shape, _ in outs] + anywhere(1),
            scratch_shapes=[
                pltpu.VMEM((group, width), F32),
                pltpu.VMEM((4, dp, 400, LANES), BF),
                pltpu.VMEM(w.shape, BF),
                pltpu.VMEM(gu_shape, BF),
                pltpu.SemaphoreType.DMA((9,)),
                pltpu.SemaphoreType.DMA((2 * experts // PER,)),
            ],
        ),
        out_shape=[jax.ShapeDtypeStruct(shape, kind) for shape, kind in outs]
        + [jax.ShapeDtypeStruct(gu_shape, BF)],
        compiler_params=params(),
        cost_estimate=pl.CostEstimate(
            flops=2 * group * width * (768 * 4 + ff * 3 * experts) + 64 * group * group * HD,
            bytes_accessed=width * 768 * 8 + w.size * 2 + 8 * group * width * 2,
            transcendentals=16 * group * group + experts * group * ff,
        ),
        name="layer_forward",
    )(scalars, *pieces, *w_attn, w, *after, *smalls)
    return list(out[:8]), list(out[8:12]), out[12]


def experts_backward_kernel(n_after, sref, *refs):
    (*refs,) = refs[n_after:]
    given, refs = refs[:4], refs[4:]
    gate_ref, gu_ref, w_ref, *refs = refs
    pieces, refs = refs[:4], refs[4:]
    grad_ref, dgu_ref, ga_ref, total, total_gate = refs
    step = pl.program_id(0)
    group, width = grad_ref.shape
    ff = w_ref.shape[-1]

    @pl.when(sref[1] > 0)
    def _():
        @pl.when(step == 0)
        def _():
            assemble(sref[0], given, grad_ref)

        grad = grad_ref[...]
        gates = gate_ref[...]
        down = jnp.concatenate(
            [w_ref[:, 2, j].reshape(width, ff) for j in range(PER_STEP)], axis=1
        )
        turned = dot(grad, down)
        lanes = lax.broadcasted_iota(jnp.int32, (group, LANES), 1)
        grad_gate = jnp.zeros((group, LANES), F32)
        out = None
        for j in range(PER_STEP):
            expert = step * PER_STEP + j
            back = turned[:, j * ff : (j + 1) * ff]
            both = gu_ref[j].astype(F32)
            gate_pre, up_pre = both[:, :ff], both[:, ff:]
            sigma = jax.nn.sigmoid(gate_pre)
            silu = gate_pre * sigma
            act = silu * up_pre
            gate = column(gates, expert)
            grad_gate = jnp.where(
                lanes == expert, jnp.sum(act * back, axis=1, keepdims=True), grad_gate
            )
            grad_act = gate * back
            grad_pre = grad_act * up_pre * sigma * (1.0 + gate_pre * (1.0 - sigma))
            grad_up = grad_act * silu
            grad_both = jnp.concatenate([grad_pre.astype(BF), grad_up.astype(BF)], axis=1)
            dgu_ref[j] = grad_both
            ga_ref[:, j * ff : (j + 1) * ff] = (gate * act).astype(BF)
            gate_up = jnp.concatenate(
                [w_ref[:, 0, j].reshape(width, ff), w_ref[:, 1, j].reshape(width, ff)], axis=1
            )
            part = dot_nt(grad_both, gate_up)
            out = part if out is None else out + part

        @pl.when(step == 0)
        def _():
            total[...] = out
            total_gate[...] = grad_gate

        @pl.when(step > 0)
        def _():
            total[...] += out
            total_gate[...] += grad_gate

        @pl.when(step == pl.num_programs(0) - 1)
        def _():
            rows = group // 4
            for shift in range(4):
                place = own_rows(lax.rem(sref[0] + shift, 4), rows)
                pieces[shift][:, :width] = total[place, :].astype(BF)
                pieces[shift][:, width:] = total_gate[place, :].astype(BF)


def experts_backward(scalars, given, gates, gu, w, after):
    dp, _, experts, dr, ff = w.shape
    group = gates.shape[0]
    width = dp * dr
    piece = (group // 4, width + LANES)
    return pl.pallas_call(
        lambda *refs: experts_backward_kernel(len(after), *refs),
        grid_spec=pltpu.PrefetchScalarGridSpec(
            num_scalar_prefetch=1,
            grid=(experts // PER_STEP,),
            in_specs=anywhere(len(after))
            + [whole(x.shape) for x in given]
            + [
                whole((group, experts)),
                pl.BlockSpec((PER_STEP, group, 2 * ff), lambda i, s: (i * s[1], 0, 0)),
                pl.BlockSpec((dp, 3, PER_STEP, dr, ff), lambda i, s: (0, 0, i * s[1], 0, 0)),
            ],
            out_specs=[whole(piece)] * 4
            + [
                whole((group, width)),
                pl.BlockSpec((PER_STEP, group, 2 * ff), lambda i, s: (i * s[1], 0, 0)),
                pl.BlockSpec((group, PER_STEP * ff), lambda i, s: (0, i * s[1])),
            ],
            scratch_shapes=[pltpu.VMEM((group, width), F32), pltpu.VMEM((group, LANES), F32)],
        ),
        out_shape=[jax.ShapeDtypeStruct(piece, BF)] * 4
        + [
            jax.ShapeDtypeStruct((group, width), BF),
            jax.ShapeDtypeStruct((experts, group, 2 * ff), BF),
            jax.ShapeDtypeStruct((group, experts * ff), BF),
        ],
        compiler_params=params(),
        cost_estimate=pl.CostEstimate(
            flops=2 * group * width * ff * 3 * experts,
            bytes_accessed=w.size * 2 + 5 * experts * group * ff * 2,
            transcendentals=experts * group * ff,
        ),
        name="experts_backward",
    )(scalars, *after, *given, gates, gu, w)


def middle_kernel(n_after, sref, *refs):
    refs = refs[n_after:]
    pieces, refs = refs[:4], refs[4:]
    grad_ref, hown_ref, gates_ref, b_ref, gains_ref, router_ref, dh_ref, do_ref, small_ref = refs
    rows, width = grad_ref.shape

    @pl.when(sref[1] > 0)
    def _():
        place = own_rows(sref[0], rows)
        joined = pieces[0][...].astype(F32)
        for shift in range(1, 4):
            joined = joined + pieces[shift][...].astype(F32)
        grad_normed = joined[:, :width]
        grad_gate = joined[:, width : width + E]
        gates = gates_ref[place, :]
        grad_logits = (
            gates * (grad_gate - jnp.sum(gates * grad_gate, axis=1, keepdims=True))
        ).astype(BF)
        normed = b_ref[place, :]
        grad_normed = grad_normed + dot_nt(grad_logits, router_ref[:, :E])
        hidden = hown_ref[...]
        part, grad_gain = norm_back(hidden, rms_scale(hidden), gains_ref[1:2, :], grad_normed)
        grad_hidden = grad_ref[...].astype(F32) + part
        dh_ref[...] = grad_hidden
        do_ref[...] = grad_hidden.astype(BF)
        small_ref[0:E, :] = dot_tn(grad_logits, normed)
        small_ref[E : E + 1, :] = grad_gain
        small_ref[E + 1 :, :] = jnp.zeros((small_ref.shape[0] - E - 1, width), F32)


def middle(scalars, pieces, grad_own, hown, gates, b, gains, router, after):
    rows, width = grad_own.shape
    operands = [*pieces, grad_own, hown, gates, b, gains, router]
    return pl.pallas_call(
        lambda *refs: middle_kernel(len(after), *refs),
        grid_spec=pltpu.PrefetchScalarGridSpec(
            num_scalar_prefetch=1,
            grid=(1,),
            in_specs=anywhere(len(after)) + [whole(x.shape) for x in operands],
            out_specs=[whole((rows, width)), whole((rows, width)), whole((24, width))],
        ),
        out_shape=[
            jax.ShapeDtypeStruct((rows, width), F32),
            jax.ShapeDtypeStruct((rows, width), BF),
            jax.ShapeDtypeStruct((24, width), F32),
        ],
        compiler_params=params(),
        cost_estimate=pl.CostEstimate(
            flops=rows * width * 64, bytes_accessed=rows * width * 24, transcendentals=rows
        ),
        name="norm_backward",
    )(scalars, *after, *operands)


def attention_backward_kernel(n_after, sref, *refs):
    pieces, refs = refs[:4], refs[4:]
    sources, refs = refs[:9], refs[9 + n_after :]
    (
        dh_ref, xown_ref, small_ref, gains_ref, cos_ref, sin_ref, bias_ref, qkv_ref, lse_ref,
        dx_ref, dxlow_ref, small_out_ref, full_ref, dqkv_ref,
        now, buffers, sems,
    ) = refs
    me = sref[0]
    shard = dh_ref.shape[0]

    @pl.when(sref[1] > 0)
    def _():
        copies = fetches(sref[2], sources, buffers, sems)
        for copy in copies[0]:
            copy.start()
        assemble(me, pieces, full_ref)
        bias = bias_ref[...]
        lse = lse_ref[...]
        cos = jnp.concatenate([cos_ref[...]] * 3, axis=1)
        sin = jnp.concatenate([sin_ref[...]] * 3, axis=1)
        total = jnp.zeros((shard, full_ref.shape[1]), F32)
        for step in range(4):
            for copy in copies[step]:
                copy.wait()
            for copy in copies[step + 1] if step < 3 else []:
                copy.start()
            w_qkv, w_out = group_weights(buffers, step)
            do = dot(full_ref[...], w_out).astype(BF)
            qkv = qkv_ref[step]
            q, k, v = qkv[:, :256], qkv[:, 256:384], qkv[:, 384:]
            q_turned = q.T
            do_turned = do.T
            dq, dk, dv = [], [], []
            for kv in range(2):
                k_one = k[:, kv * HD : (kv + 1) * HD]
                v_one = v[:, kv * HD : (kv + 1) * HD]
                dk_one = dv_one = None
                for head in (2 * kv, 2 * kv + 1):
                    part = slice(head * HD, (head + 1) * HD)
                    scores = dot_nt(q[:, part], k_one) + bias
                    soft = jnp.exp(scores - lse[:, 4 * step + head : 4 * step + head + 1])
                    grad_soft = dot_nt(do[:, part], v_one)
                    grad_scores = soft * (
                        grad_soft - jnp.sum(soft * grad_soft, axis=1, keepdims=True)
                    )
                    grad_scores = grad_scores.astype(BF)
                    dq.append(dot(grad_scores, k_one))
                    dk_part = dot(q_turned[part, :], grad_scores)
                    dv_part = dot(do_turned[part, :], soft.astype(BF))
                    dk_one = dk_part if dk_one is None else dk_one + dk_part
                    dv_one = dv_part if dv_one is None else dv_one + dv_part
                dk.append(dk_one)
                dv.append(dv_one)
            grad_k = jnp.concatenate(dk, axis=0).T
            grad_v = jnp.concatenate(dv, axis=0).T
            grad_qk = jnp.concatenate([jnp.concatenate(dq, axis=1) * HD**-0.5, grad_k], axis=1)
            grad_qk = (grad_qk * cos - swap_halves(grad_qk) * sin).astype(BF)
            now[step, :, :384] = grad_qk
            now[step, :, 384:] = grad_v.astype(BF)
            if step == 0:
                dqkv_ref[...] = now[0]
            total += dot_nt(now[step, own_rows(me, shard), :], w_qkv)

        entering = xown_ref[...].astype(F32)
        part, grad_gain = norm_back(entering, rms_scale(entering), gains_ref[0:1, :], total)
        grad_entering = dh_ref[...] + part
        dx_ref[...] = grad_entering
        dxlow_ref[...] = grad_entering.astype(BF)
        rows = lax.broadcasted_iota(jnp.int32, small_ref.shape, 0)
        small_out_ref[...] = jnp.where(rows == E + 1, grad_gain, small_ref[...])


def attention_backward(
    scalars, pieces, dh, xown, small, gains, tables, qkv, lse, w_attn, after
):
    shard, width = dh.shape
    group = 4 * shard
    dp = width // 64
    cos, sin, bias = tables
    smalls = [dh, xown, small, gains, cos, sin, bias]
    per_step = lambda i, s: (i * s[1], 0, 0)
    outs = [
        ((shard, width), F32),
        ((shard, width), BF),
        (small.shape, F32),
        ((group, width), BF),
        ((group, 512), BF),
    ]
    return pl.pallas_call(
        lambda *refs: attention_backward_kernel(len(after), *refs),
        grid_spec=pltpu.PrefetchScalarGridSpec(
            num_scalar_prefetch=1,
            grid=(1,),
            in_specs=[whole(x.shape) for x in pieces]
            + anywhere(9 + len(after))
            + [whole(x.shape) for x in smalls]
            + [whole(qkv.shape), whole(lse.shape)],
            out_specs=[whole(shape) for shape, _ in outs],
            scratch_shapes=[
                pltpu.VMEM((4, group, 512), BF),
                pltpu.VMEM((4, dp, 400, LANES), BF),
                pltpu.SemaphoreType.DMA((9,)),
            ],
        ),
        out_shape=[jax.ShapeDtypeStruct(shape, kind) for shape, kind in outs],
        compiler_params=params(),
        cost_estimate=pl.CostEstimate(
            flops=group * width * 1024 * 2 + 16 * 10 * group * group * HD,
            bytes_accessed=width * 768 * 8 + 6 * group * width * 2,
            transcendentals=16 * group * group,
        ),
        name="attention_backward",
    )(scalars, *pieces, *w_attn, *after, *smalls, qkv, lse)


def expert_weights_kernel(n_after, sref, *refs):
    refs = refs[n_after:]
    b, refs = refs[:4], refs[4:]
    g, refs = refs[:4], refs[4:]
    dgu, refs = refs[:4], refs[4:]
    ga, refs = refs[:4], refs[4:]
    out_ref, bt_ref, gt_ref = refs
    group = b[0].shape[0]
    dp, _, _, dr, ff = out_ref.shape
    first = sref[1] > 0

    def chosen(four, micro, *index):
        index = index or (Ellipsis,)
        return jnp.where(first, four[micro][index], four[2 + micro][index])

    @pl.when(pl.program_id(0) == 0)
    def _():
        for micro in range(2):
            place = slice(micro * group, (micro + 1) * group)
            bt_ref[:, place] = chosen(b, micro).T
            gt_ref[:, place] = chosen(g, micro).T

    bt = bt_ref[...]
    for j in range(PER_GRAD):
        rows = jnp.concatenate([chosen(dgu, 0, j), chosen(dgu, 1, j)], axis=0)
        grads = dot(bt, rows).astype(BF)
        out_ref[:, 0, j] = grads[:, :ff].reshape(dp, dr, ff)
        out_ref[:, 1, j] = grads[:, ff:].reshape(dp, dr, ff)
    rows = jnp.concatenate([chosen(ga, 0), chosen(ga, 1)], axis=0)
    grads = dot(gt_ref[...], rows).astype(BF)
    for j in range(PER_GRAD):
        out_ref[:, 2, j] = grads[:, j * ff : (j + 1) * ff].reshape(dp, dr, ff)


def expert_weights(scalars, rows_b, grads, dgus, gas, dp, after):
    group, width = rows_b[0].shape
    experts, _, ff2 = dgus[0].shape
    ff = ff2 // 2
    dr = width // dp
    square = whole((group, width))
    wide, flat = [], []
    for held in (lambda s: s[1], lambda s: 1 - s[1]):
        wide += [
            pl.BlockSpec((PER_GRAD, group, ff2), lambda i, s, held=held: (i * held(s), 0, 0))
        ] * 2
        flat += [pl.BlockSpec((group, PER_GRAD * ff), lambda i, s, held=held: (0, i * held(s)))] * 2
    return pl.pallas_call(
        lambda *refs: expert_weights_kernel(len(after), *refs),
        grid_spec=pltpu.PrefetchScalarGridSpec(
            num_scalar_prefetch=1,
            grid=(experts // PER_GRAD,),
            in_specs=anywhere(len(after)) + [square] * 8 + wide + flat,
            out_specs=pl.BlockSpec((dp, 3, PER_GRAD, dr, ff), lambda i, s: (0, 0, i, 0, 0)),
            scratch_shapes=[
                pltpu.VMEM((width, 2 * group), BF),
                pltpu.VMEM((width, 2 * group), BF),
            ],
        ),
        out_shape=jax.ShapeDtypeStruct((dp, 3, experts, dr, ff), BF),
        compiler_params=params(),
        cost_estimate=pl.CostEstimate(
            flops=4 * group * width * ff * 3 * experts,
            bytes_accessed=dp * 3 * experts * dr * ff * 2 + 6 * experts * group * ff * 2,
            transcendentals=0,
        ),
        name="expert_weight_grads",
    )(scalars, *after, *rows_b, *grads, *dgus, *gas)


def attention_weights_kernel(sref, *refs):
    a, o, f, d, small = (refs[4 * j : 4 * j + 4] for j in range(5))
    out_ref = refs[20]
    dp = out_ref.shape[0]
    first = sref[1] > 0

    def chosen(four, micro):
        return jnp.where(first, four[micro][...], four[2 + micro][...])

    sums = dot_tn(chosen(a, 0), chosen(d, 0)) + dot_tn(chosen(a, 1), chosen(d, 1))
    for j in range(4):
        out_ref[:, 64 * j : 64 * (j + 1), :] = (
            sums[:, LANES * j : LANES * (j + 1)].astype(BF).reshape(dp, 64, LANES)
        )
    sums = dot_tn(chosen(f, 0), chosen(o, 0)) + dot_tn(chosen(f, 1), chosen(o, 1))
    for j in range(2):
        out_ref[:, 64 * (4 + j) : 64 * (5 + j), :] = (
            sums[:, LANES * j : LANES * (j + 1)].astype(BF).reshape(dp, 64, LANES)
        )
    rows = chosen(small, 0) + chosen(small, 1)
    rows = jnp.concatenate(
        [rows, jnp.zeros((LANES - rows.shape[0], rows.shape[1]), F32)], axis=0
    )
    out_ref[:, 384:, :] = rows.T.astype(BF).reshape(dp, 64, LANES)


def attention_weights(scalars, a, o, f, d, small, dp):
    group, width = a[0].shape
    operands = [*a, *o, *f, *d, *small]
    return pl.pallas_call(
        attention_weights_kernel,
        grid_spec=pltpu.PrefetchScalarGridSpec(
            num_scalar_prefetch=1,
            grid=(1,),
            in_specs=[whole(x.shape) for x in operands],
            out_specs=whole((dp, 448, LANES)),
        ),
        out_shape=jax.ShapeDtypeStruct((dp, 448, LANES), BF),
        compiler_params=params(),
        cost_estimate=pl.CostEstimate(
            flops=4 * group * width * 768,
            bytes_accessed=group * width * 14 + width * 768 * 2,
            transcendentals=0,
        ),
        name="attention_weight_grads",
    )(scalars, *operands)


def moved(array, shift):
    return lax.ppermute(array, "tensor", [(i, (i + shift) % 4) for i in range(4)])


def swapped(array, dp):
    return lax.ppermute(array, "dp", [(i, i ^ 1) for i in range(dp)])


def to_owner(pieces):
    return [pieces[0]] + [moved(pieces[s], s) for s in range(1, 4)]


def to_all(rows):
    return [rows] + [moved(rows, s) for s in range(1, 4)]


def across(rows, up):
    start, end = (0, 4) if up else (4, 0)
    return [
        lax.ppermute(
            rows, ("pipe", "tensor"), [(start + i, end + (i + s) % 4) for i in range(4)]
        )
        for s in range(4)
    ]


def tables_of(lengths, group):
    ends = jnp.cumsum(lengths)
    starts = ends - lengths
    index = jnp.arange(group, dtype=jnp.int32)
    inside = index[:, None] >= starts[None, :]
    start = jnp.max(jnp.where(inside, starts[None, :], 0), axis=1)
    position = (index - start).astype(F32)
    half = HD // 2
    freq = jnp.exp(jnp.arange(half, dtype=F32) * (-2.0 * math.log(10000.0) / HD))
    angle = position[:, None] * freq[None, :]
    cos, sin = jnp.cos(angle), jnp.sin(angle)
    visible = (index[None, :] <= index[:, None]) & (index[None, :] >= start[:, None])
    bias = jnp.where(visible, 0.0, MASKED).astype(F32)
    return (
        jnp.concatenate([cos, cos, cos, cos], axis=1),
        jnp.concatenate([-sin, sin, -sin, sin], axis=1),
        bias,
    )


def per_device(
    inputs, cotangent, doc_lengths, routes, norm_attn, w_query, w_key, w_value, w_out,
    w_router, norm_ffn, w_gate, w_up, w_down,
):
    section = lax.axis_index("pipe")
    first_section = section == 0
    me = lax.axis_index("tensor")
    dp = lax.axis_size("dp")
    core = lax.axis_index("dp") % 2
    micro = inputs.shape[0]
    shard, width = inputs.shape[1:]
    group = shard * 4
    rows_dp = width // dp
    scalars = [
        jnp.stack([me, (section == s).astype(jnp.int32), core]).astype(jnp.int32)
        for s in range(2)
    ]

    out_turned = w_out[0].T
    small = jnp.concatenate([w_router[0], norm_attn[0][:, None], norm_ffn[0][:, None]], axis=1)
    small = jnp.pad(small, ((0, 0), (0, LANES - E - 2)))
    piece = jnp.concatenate(
        [
            w_query[0][:, :LANES], w_query[0][:, LANES:], w_key[0], w_value[0],
            out_turned[:, :LANES], out_turned[:, LANES:], small,
        ],
        axis=0,
    )
    w_own = jnp.broadcast_to(piece[None], (dp,) + piece.shape)
    w_own = lax.all_to_all(w_own, "dp", 0, 0, tiled=True)
    pieces_w = jnp.stack([w_gate[0], w_up[0], w_down[0].transpose(0, 2, 1)])
    w_experts = lax.all_gather(pieces_w, "dp", axis=0)
    tables = [tables_of(doc_lengths[m, 0], group) for m in range(micro)]
    tables, inputs, cotangent = lax.optimization_barrier((tables, inputs, cotangent))
    rows_in, rows_cot = to_all(inputs), to_all(cotangent)
    rows_in, rows_cot, w_own = lax.optimization_barrier((rows_in, rows_cot, w_own))
    rows_in = [[part[m] for part in rows_in] for m in range(micro)]
    rows_cot = [[part[m] for part in rows_cot] for m in range(micro)]
    half, quarter = dp // 2, dp // 4
    mine = lax.dynamic_slice_in_dim(w_own, core * half, half, 0)
    w_next, w_last = moved(mine, 1), moved(mine, 3)
    w_over = [moved(w_next[:quarter], 1), moved(w_last[quarter:], 3)]
    other = [swapped(x, dp) for x in (w_next, w_last, *w_over)]
    w_attn = [w_own, w_next, other[0], *w_over, other[2], other[3], w_last, other[1]]
    w_attn, rows_in, rows_cot = lax.optimization_barrier((w_attn, rows_in, rows_cot))
    router, gains = smalls_of(scalars[0], w_attn)

    ids = jnp.arange(E, dtype=jnp.int32)
    picked = jnp.any(routes[0][..., None] == ids, axis=2).astype(F32)

    after = []
    saves = [[None] * micro, [None] * micro]
    firsts = [[None] * micro, [None] * micro]
    middles = [[None] * micro, [None] * micro]
    lasts = [[None] * micro, [None] * micro]

    def attend(s, m, pieces):
        nonlocal after
        out = attention_forward(
            scalars[s], pieces, gains, tables[m], picked[m], w_attn, router, after
        )
        saves[s][m] = list(out)
        after = [out[6]]

    def expert(s, m):
        nonlocal after
        b, gates = saves[s][m][6:8]
        *parts, gu = experts_forward(scalars[s], b, gates, w_experts, after)
        saves[s][m].append(gu)
        after = [gu]
        return parts

    def layer(s, m, pieces):
        nonlocal after
        kept, parts, gu = layer_forward(
            scalars[s], pieces, gains, tables[m], picked[m], w_attn, router, w_experts, after
        )
        saves[s][m] = [*kept, gu]
        after = [gu]
        return parts

    def expert_back(s, m, pieces):
        nonlocal after
        gates, gu = saves[s][m][7:9]
        *parts, grad, dgu, ga = experts_backward(
            scalars[s], pieces, gates, gu, w_experts, after
        )
        after = [grad]
        firsts[s][m] = (to_owner(parts), grad, dgu, ga)

    def norm_between(s, m, own):
        nonlocal after
        kept = saves[s][m]
        dh, do, small = middle(
            scalars[s], firsts[s][m][0], own, kept[5], kept[7], kept[6], gains, router, after
        )
        middles[s][m] = (dh, to_all(do), small)
        after = [do]

    def attend_back(s, m):
        nonlocal after
        kept = saves[s][m]
        dh, rows, small = middles[s][m]
        dx, dx_low, small, full, dqkv = attention_backward(
            scalars[s], rows, dh, kept[1], small, gains, tables[m], kept[2], kept[4],
            w_attn, after,
        )
        lasts[s][m] = (small, full, dqkv, dx)
        after = [dx]
        return dx_low

    def layer_sum(parts, hown):
        return finish(to_owner(parts), hown)

    attend(0, 0, rows_in[0])
    first_out = layer_sum(expert(0, 0), saves[0][0][5])
    first_in = across(first_out, True)
    after = [first_out]
    attend(0, 1, rows_in[1])
    after = [*after, *first_in]
    parts = to_owner(expert(0, 1))
    late = [layer(1, 0, first_in)]
    second_out = finish(parts, saves[0][1][5])
    second_in = across(second_out, True)
    expert_back(1, 0, rows_cot[0])
    late.append(layer(1, 1, second_in))
    norm_between(1, 0, cotangent[0])
    expert_back(1, 1, rows_cot[1])
    first_back = across(attend_back(1, 0), False)
    norm_between(1, 1, cotangent[1])
    expert_back(0, 0, first_back)
    second_back = across(attend_back(1, 1), False)
    norm_between(0, 0, first_back[0])
    expert_back(0, 1, second_back)
    joined = firsts[0] + firsts[1]
    grad_experts = expert_weights(
        scalars[0],
        [saves[s][m][6] for s in range(2) for m in range(micro)],
        [x[1] for x in joined],
        [x[2] for x in joined],
        [x[3] for x in joined],
        dp,
        after,
    )
    expert_sums = lax.psum_scatter(grad_experts, "dp", scatter_dimension=0, tiled=True)[0]
    after = [grad_experts]
    norm_between(0, 1, second_back[0])
    attend_back(0, 0)
    attend_back(0, 1)
    late, _ = lax.optimization_barrier((late, lasts[1][1][3]))
    outputs = [
        [first_out, second_out],
        [layer_sum(late[m], saves[1][m][5]) for m in range(micro)],
    ]
    grads_in = [[lasts[s][m][3] for m in range(micro)] for s in range(2)]

    joined = lasts[0] + lasts[1]
    grad_attn = attention_weights(
        scalars[0],
        [saves[s][m][0] for s in range(2) for m in range(micro)],
        [saves[s][m][3] for s in range(2) for m in range(micro)],
        [x[1] for x in joined],
        [x[2] for x in joined],
        [x[0] for x in joined],
        dp,
    )
    grad_attn = lax.all_to_all(grad_attn, "dp", 0, 0, tiled=True)
    attn_sums = jnp.sum(grad_attn.astype(F32), axis=0)
    small = attn_sums[384:].reshape(4, 16, LANES)
    small_own = None
    for shift in range(4):
        part = lax.dynamic_index_in_dim(small, (me + shift) % 4, 0, keepdims=False)
        part = moved(part, shift) if shift else part
        small_own = part if small_own is None else small_own + part
    expert_sums = expert_sums.astype(F32)
    blocks = [attn_sums[64 * j : 64 * (j + 1)] for j in range(6)]
    section_rows = jnp.stack(
        [jnp.where(first_section, outputs[0][m], outputs[1][m]) for m in range(micro)]
    )
    grad_in = jnp.stack(
        [jnp.where(first_section, grads_in[0][m], grads_in[1][m]) for m in range(micro)]
    )
    return (
        section_rows[None],
        grad_in[None],
        small_own[:, E + 1][None],
        jnp.concatenate(blocks[:2], axis=1)[None],
        blocks[2][None],
        blocks[3][None],
        jnp.concatenate(blocks[4:], axis=1).T[None],
        small_own[:, :E][None],
        small_own[:, E][None],
        expert_sums[0][None],
        expert_sums[1][None],
        expert_sums[2].transpose(0, 2, 1)[None],
    )


def finish(parts, hown):
    result = hown
    for part in parts:
        result = result + part.astype(F32)
    return result.astype(BF)


def solution(mesh):
    in_specs = (
        P(None, ("dp", "tensor"), None),
        P(None, ("dp", "tensor"), None),
        P(None, "dp", None),
        P("pipe", None, "dp", None),
        P("pipe", ("dp", "tensor")),
        P("pipe", "dp", "tensor"),
        P("pipe", "dp", "tensor"),
        P("pipe", "dp", "tensor"),
        P("pipe", "tensor", "dp"),
        P("pipe", ("dp", "tensor"), None),
        P("pipe", ("dp", "tensor")),
        P("pipe", None, "dp", "tensor"),
        P("pipe", None, "dp", "tensor"),
        P("pipe", None, "tensor", "dp"),
    )
    out_specs = (
        P("pipe", None, ("dp", "tensor"), None),
        P("pipe", None, ("dp", "tensor"), None),
        P("pipe", ("dp", "tensor")),
        P("pipe", "dp", "tensor"),
        P("pipe", "dp", "tensor"),
        P("pipe", "dp", "tensor"),
        P("pipe", "tensor", "dp"),
        P("pipe", ("dp", "tensor"), None),
        P("pipe", ("dp", "tensor")),
        P("pipe", None, "dp", "tensor"),
        P("pipe", None, "dp", "tensor"),
        P("pipe", None, "tensor", "dp"),
    )
    return jax.shard_map(
        per_device, mesh=mesh, in_specs=in_specs, out_specs=out_specs, check_vma=False
    )
```
